128 devices in a mesh: row: 8 (over x, z_lo), col: 16 (over y, z_hi, core).
Axes of the slice: x: 4, y: 4, z: 4 (z_hi: 2, z_lo: 2; z = z_hi * 2 + z_lo), core: 2. Of those that a mesh axis runs over, the one named last changes fastest.
Arguments:
- front: float32 [16384, 16384], P('row', 'col'), may hold values from -6 to 6
- child_left: bfloat16 [14336, 256, 64], P(('row', 'col')), may hold values from -6 to 6
- child_right: bfloat16 [14336, 64, 256], P(('row', 'col')), may hold values from -0.75 to 0.75
- child_owner: int32 [14336, 1], P(('row', 'col')), may hold values from 0 to 127; in each aligned block of 112 rows (0 to 111, 112 to 223, ...) at most 2 rows name the same one
- child_slot: int32 [14336], P(('row', 'col')), may hold values from 0 to 31
- pivots: int32 [256], replicated, may hold values from 0 to 255, each once
- upper_inverse: float32 [256, 256], replicated, may hold values from -0.375 to 0.375
- lower_inverse: float32 [256, 256], replicated, may hold values from -0.375 to 0.375
- column_basis: float32 [256, 64], replicated, may hold values from -0.375 to 0.375
- row_basis: float32 [256, 64], replicated, may hold values from -0.375 to 0.375
- column_ranks: int32 [64], P('row'), may hold values from 32 to 64
- row_ranks: int32 [64], P('col'), may hold values from 32 to 64
Outputs:
- updated_front: float32 [16384, 16384], P('row', 'col')
The draws below stay inside these ranges and needn't reach their ends.
Inputs may be any that keep to these rules, and one draw needn't show every extreme that they name: `child_owner`: owner device, numbered row index * 16 + col index; among the 112 child blocks of one device no owner is named more than 2 times, and exactly 2 times for some owner. `child_slot`: local block of the owner, numbered block row * 4 + block column. `pivots`: each of 0 to 255 once.
All inputs are finite; a program needn't handle non-finite values.
Results may differ from the reference program's by a relative error of at most 0.0003.
Values may be sent and summed in bfloat16 or wider, within the bound.
A program may use at most 192 MiB of HBM per device.

```python
import math
import jax
import jax.numpy as jnp
import numpy as np
from jax import lax

B = 256
R = 64
RB_DEV = 8
CB_DEV = 4
CAP = 2
KC = 112
CHILDREN = 14336
NBR = 64
NBC = 64
NF = 16384
NC = 16384
N_COL = 16
DEVICES = 128


def plant(drawn, own_key, smallest, top_value):
    dims = drawn.shape
    place = [jax.random.randint(jax.random.fold_in(own_key, axis), (), 0, dims[axis]) for axis in range(len(dims))]
    drawn = drawn.at[tuple(place)].set(smallest)
    longest = dims.index(max(dims))
    place[longest] = (place[longest] + 1) % dims[longest]
    return drawn.at[tuple(place)].set(top_value)


def block_levels(own_key, extent, pieces, least, top_value):
    level, own = 1.0, jax.random.fold_in(own_key, 6)
    for axis_at, parts in pieces:
        heights = jnp.exp(jax.random.uniform(jax.random.fold_in(own, axis_at), (parts,), jnp.float32, least / len(pieces), top_value / len(pieces)))
        level = level * jnp.repeat(heights, extent[axis_at] // parts).reshape([-1 if axis == axis_at else 1 for axis in range(len(extent))])
    return level


def deal_out(key, own, number, rows, count, top, bound, slope):
    order = jax.random.permutation(key, count)
    heavy_load, common = shares(count, rows * top, bound, slope, True), shares(count, rows * top, bound, slope, False)
    places = jnp.arange(count)

    def named(tallies, turn):
        used = int((tallies > 0).sum())
        fixed = max(1, used // 4)
        moved = fixed + (places - fixed + turn * (used - fixed)) % max(1, count - fixed)
        return jnp.zeros((count,), jnp.int32).at[order[jnp.where(places < fixed, places, moved)]].set(jnp.asarray(tallies, jnp.int32))

    tallies = jnp.where(number % 4 == 0, named(heavy_load, number // 4), named(common, number - number // 4 - 1))
    mixed = jax.random.permutation(jax.random.fold_in(own, 3), count)
    source_of, sink = mixed[0:count // 2 * 2:2], mixed[1:count // 2 * 2:2]
    slack = jnp.minimum(tallies[source_of] - 1, bound - tallies[sink]) // 2
    slack = jnp.where((source_of == order[0]) | (sink == order[0]) | (tallies[sink] == 0), 0, jnp.maximum(slack, 0))
    moved = jax.random.randint(jax.random.fold_in(own, 4), (count // 2,), 0, 1 << 20) % (slack + 1)
    tallies = tallies.at[source_of].add(-moved).at[sink].add(moved)
    labels = jnp.searchsorted(jnp.cumsum(tallies), jnp.arange(rows * top), side="right").astype(jnp.int32)
    listing = labels.reshape(top, rows).T
    listing = listing[jax.random.permutation(jax.random.fold_in(own, 1), rows)]
    turn = jax.random.randint(jax.random.fold_in(own, 2), (rows, 1), 0, top)
    return jnp.take_along_axis(listing, (jnp.arange(top)[None, :] + turn) % top, axis=1)


def shares(count, total, bound, skew, full):
    weights = [(1 << 20) // math.isqrt(rank ** skew) + 1 for rank in range(1, count + 1)]
    largest = bound if full else min(bound, max(-(-total // count), total * weights[0] // sum(weights)))
    least = 1 if total - largest >= count - 1 else 0
    holding, rest = [largest] + [least] * (count - 1), total - largest - least * (count - 1)
    while rest > 0:
        movable = [i for i in range(1, count) if holding[i] < largest] or [i for i in range(1, count) if holding[i] < bound]
        whole, left = sum([weights[i] for i in movable]), rest
        for i in movable:
            addition = min(bound - holding[i], max(1, left * weights[i] // whole), rest)
            holding[i] = holding[i] + addition
            rest = rest - addition
    return np.array(holding)


def gaussian(key, extent, scale, most, pieces=(), dtype=jnp.bfloat16):
    factor_of = block_levels(key, extent, pieces, -0.22, 0.18) if pieces else 1.0
    values = jax.random.normal(key, extent, jnp.float32) * scale * factor_of
    return jnp.minimum(jnp.maximum(values, -most), most).astype(dtype)


def setup_inputs(seed: int = 0) -> dict:
    key_of = jax.random.split(jax.random.key(seed), 13)
    front = gaussian(key_of[0], (NF, NC), 1.0, 6.0, ((0, 8), (1, 16)), jnp.float32)
    child_left = gaussian(key_of[1], (CHILDREN, B, R), 1.0, 6.0, ((0, 128),))
    child_right = gaussian(key_of[2], (CHILDREN, R, B), R ** -0.5, 0.75, ((0, 128),))
    child_owner_keys = jax.random.split(jax.random.fold_in(key_of[3], 1), CHILDREN // KC)
    child_owner_turns = jax.random.permutation(jax.random.fold_in(key_of[3], 3), CHILDREN // KC)
    child_owner = jax.vmap(lambda own, number: deal_out(jax.random.fold_in(key_of[3], 2), own, number, KC, DEVICES, 1, CAP, 2))(child_owner_keys, child_owner_turns).reshape((CHILDREN, 1))
    child_slot = plant(jax.random.randint(key_of[4], (CHILDREN,), 0, RB_DEV * CB_DEV), jax.random.fold_in(key_of[4], 1), 0, (RB_DEV * CB_DEV) - 1).astype(jnp.int32)
    pivots = jax.random.permutation(key_of[5], B).astype(jnp.int32)
    upper_inverse = gaussian(key_of[6], (B, B), B ** -0.5, 0.375, (), jnp.float32)
    lower_inverse = gaussian(key_of[7], (B, B), B ** -0.5, 0.375, (), jnp.float32)
    column_basis = gaussian(key_of[8], (B, R), B ** -0.5, 0.375, (), jnp.float32)
    row_basis = gaussian(key_of[9], (B, R), B ** -0.5, 0.375, (), jnp.float32)
    column_ranks = plant(jax.random.randint(key_of[10], (NBR,), R // 2, R + 1), jax.random.fold_in(key_of[10], 1), R // 2, R).astype(jnp.int32)
    row_ranks = plant(jax.random.randint(key_of[11], (NBC,), R // 2, R + 1), jax.random.fold_in(key_of[11], 1), R // 2, R).astype(jnp.int32)
    return dict(front=front, child_left=child_left, child_right=child_right, child_owner=child_owner, child_slot=child_slot, pivots=pivots, upper_inverse=upper_inverse, lower_inverse=lower_inverse, column_basis=column_basis, row_basis=row_basis, column_ranks=column_ranks, row_ranks=row_ranks)


def reference(front, child_left, child_right, child_owner, child_slot, pivots, upper_inverse, lower_inverse, column_basis, row_basis, column_ranks, row_ranks):
    highest = lax.Precision.HIGHEST
    owners = child_owner[:, 0].astype(jnp.int32)
    block_row = (owners // N_COL) * RB_DEV + child_slot // CB_DEV
    block_col = (owners % N_COL) * CB_DEV + child_slot % CB_DEV
    lefts = child_left.reshape(DEVICES, KC, B, R)
    rights = child_right.reshape(DEVICES, KC, R, B)
    rows_of = block_row.reshape(DEVICES, KC)
    cols_of = block_col.reshape(DEVICES, KC)

    def apply_group(front_grid, member):
        left_part, right_part, row_ids, col_ids = member
        product = jnp.einsum("nbr,nrc->nbc", left_part.astype(jnp.float32), right_part.astype(jnp.float32))
        return front_grid.at[row_ids, :, col_ids, :].add(product), None

    front_grid, unused = lax.scan(apply_group, front.reshape(NBR, B, NBC, B), (lefts, rights, rows_of, cols_of))
    extended = front_grid.reshape(NF, NC)
    pivoted = jnp.take(extended[:B], pivots, axis=0)
    lower_panel = jnp.dot(extended[:, :B], upper_inverse, precision=highest)
    upper_panel = jnp.dot(lower_inverse, pivoted, precision=highest)
    col_mask = jnp.arange(R)[None, :] < jnp.repeat(column_ranks, B)[:, None]
    row_mask = jnp.arange(R)[:, None] < jnp.repeat(row_ranks, B)[None, :]
    column_factors = jnp.where(col_mask, jnp.dot(lower_panel, column_basis, precision=highest), 0.0)
    row_factors = jnp.where(row_mask, jnp.dot(row_basis.T, upper_panel, precision=highest), 0.0)
    coupling = jnp.dot(column_basis.T, row_basis, precision=highest)
    scaled = jnp.dot(column_factors, coupling, precision=highest)
    schur = extended - jnp.dot(scaled, row_factors, precision=highest)
    top_row = jnp.concatenate([pivoted[:, :B], upper_panel[:, B:]], axis=1)
    bottom = jnp.concatenate([lower_panel[B:], schur[B:, B:]], axis=1)
    return jnp.concatenate([top_row, bottom], axis=0)
```

```python
import functools

import jax
import jax.numpy as jnp
from jax import lax
from jax.experimental import pallas as pl
from jax.experimental.pallas import tpu as pltpu
from jax.sharding import PartitionSpec as P

MESH = pl.DeviceIdType.MESH
HBM = pl.BlockSpec(memory_space=pl.ANY)
SMEM = pl.BlockSpec(memory_space=pltpu.SMEM)
VMEM = pl.BlockSpec(memory_space=pltpu.VMEM)
DMA = pltpu.SemaphoreType.DMA
CAP = 2
STACK = 4
STRIDE = 37
RING = 4
CHIPS = RING**3
LEAD = 16
LIMIT = 56 * 1024 * 1024
HIGHEST = lax.Precision.HIGHEST


def dot(a, b, dims=((1,), (0,)), precision=None):
    return lax.dot_general(
        a, b, (dims, ((), ())), precision=precision, preferred_element_type=jnp.float32
    )


def pack_kernel(
    devices, owner, owner_row, slot_row, left, right, packed, table, staged, named, placed, in_sem,
    out_sem,
):
    count, rank = left.shape[0], left.shape[1]
    chips = devices // 2
    chunks = in_sem.shape[0]
    each = count // chunks

    def load(k):
        part = pl.ds(k * each, each)
        return (
            pltpu.make_async_copy(left.at[part], staged.at[part, pl.ds(0, rank)], in_sem.at[k, 0]),
            pltpu.make_async_copy(right.at[part], staged.at[part, pl.ds(rank, rank)], in_sem.at[k, 1]),
        )

    for k in range(chunks):
        for copy in load(k):
            copy.start()

    def clear(o, c):
        named[o] = 0
        placed[o] = 0
        return c

    lax.fori_loop(0, devices, clear, 0, unroll=8)

    def tally(i, c):
        named[owner[i]] += 1
        return c

    lax.fori_loop(0, count, tally, 0, unroll=4)

    shape = (devices, 1, count)
    place = lax.broadcasted_iota(jnp.int32, shape, 2)
    device = lax.broadcasted_iota(jnp.int32, shape, 0)
    owners = owner_row[...][None]
    code = (place * 64 + slot_row[...][None]).astype(jnp.float32)

    def ends(which):
        least = jnp.min(jnp.where(which, code, 65536.0), axis=2, keepdims=True)
        most = jnp.max(jnp.where(which, code, -1.0), axis=2, keepdims=True)
        return least, most

    least, most = ends(owners == device)
    low_least, low_most = ends(owners == device - (device & 1))
    core = device[:, :, 0:1] & 1
    first = jnp.where(most >= 0.0, least.astype(jnp.int32) & 63, -1)
    second = jnp.where(most > least, most.astype(jnp.int32) & 63, -1)
    late = jnp.logical_and(core == 1, low_most > low_least)
    last = jnp.where(late, second, -1)
    flag = jnp.max(last.astype(jnp.float32), axis=0, keepdims=True).astype(jnp.int32)
    lane = lax.broadcasted_iota(jnp.int32, table.shape, 2)
    line = jnp.where(lane == 0, first, jnp.where(lane == 1, jnp.where(late, -1, second), -1))
    table[...] = jnp.where(lane == 2, last, jnp.where(lane == 3, flag, line))

    for k in range(chunks):
        for copy in load(k):
            copy.wait()

        def send(i, c):
            o = owner[i]
            p = placed[o]
            placed[o] = 1
            chip = o // 2
            late = jnp.logical_and(o % 2 == 1, named[o - o % 2] == 2)
            extra = jnp.where(late, devices + chips + chip, devices + chip)
            at = jnp.where(p == 0, o, extra)
            pltpu.make_async_copy(staged.at[i], packed.at[at], out_sem).start()
            return c

        lax.fori_loop(k * each, (k + 1) * each, send, 0)
    pltpu.make_async_copy(staged, packed.at[pl.ds(0, count)], out_sem).wait()


def pack(owner, slots, left, right, devices):
    count, rank, size = left.shape
    return pl.pallas_call(
        functools.partial(pack_kernel, devices),
        out_shape=(
            jax.ShapeDtypeStruct((2 * devices, 2 * rank, size), left.dtype),
            jax.ShapeDtypeStruct((devices, 1, 128), jnp.int32),
        ),
        in_specs=[SMEM, VMEM, VMEM, HBM, HBM],
        out_specs=(HBM, VMEM),
        scratch_shapes=[
            pltpu.VMEM((count, 2 * rank, size), left.dtype),
            pltpu.SMEM((devices,), jnp.int32),
            pltpu.SMEM((devices,), jnp.int32),
            DMA((4, 2)),
            DMA,
        ],
        compiler_params=pltpu.CompilerParams(vmem_limit_bytes=LIMIT),
        name="pack",
    )(owner, owner[None, :], slots[None, :], left, right)


def position():
    r, q = lax.axis_index("row"), lax.axis_index("col")
    return r // 2, q // 4, lax.rem(q // 2, 2) * 2 + lax.rem(r, 2), lax.rem(q, 2)


def place_of(x, y, z, core):
    x, y, z = lax.rem(x, RING), lax.rem(y, RING), lax.rem(z, RING)
    return x * 2 + lax.rem(z, 2), y * 4 + (z // 2) * 2 + core


def step_of(k):
    d = lax.rem(k * STRIDE, CHIPS)
    steps = (d // (RING * RING), lax.rem(d // RING, RING), lax.rem(d, RING))
    far = [s // 2 - s // 3 for s in steps]
    both = far[0] + far[1] + far[2] > 0
    up = 1 - lax.rem(steps[0] + steps[1] + steps[2], 2)
    return d, steps, far, both, up


def legs(steps, far, up):
    ahead = [f * (3 - 2 * up) for f in far]
    return ahead, [s + 4 - a for s, a in zip(steps, ahead)]


def far_count():
    return sum(2 in (d // 16, d // 4 % 4, d % 4) for d in range(1, CHIPS))


def remote(src, dst, send, recv, device):
    return pltpu.make_async_remote_copy(
        src_ref=src, dst_ref=dst, send_sem=send, recv_sem=recv, device_id=device,
        device_id_type=MESH,
    )


def exchange_kernel(
    n_row, n_col, packed, table, got, got_table, relay, table_sems, block_sems, relay_sem,
    shared_sem, own_sem,
):
    devices = n_row * n_col
    x, y, z, core = position()
    mine = place_of(x, y, z, core)
    me = mine[0] * n_col + mine[1]
    sibling = place_of(x, y, z, 1 - core)
    sibling_id = sibling[0] * n_col + sibling[1]
    chip = me // 2
    barrier = pltpu.get_barrier_semaphore()
    a_send, a_recv, t_send, r_send, f_send, f_recv = [block_sems.at[i] for i in range(6)]

    own = (
        pltpu.make_async_copy(packed.at[me], got.at[0, me], own_sem.at[0]),
        pltpu.make_async_copy(packed.at[devices + chip], got.at[1, me], own_sem.at[1]),
        pltpu.make_async_copy(table.at[me], got_table.at[me], own_sem.at[2]),
    )
    for copy in own:
        copy.start()

    def others(body):
        def one(k, carry):
            o = lax.rem(me + k, devices)
            body(o, (o // n_col, lax.rem(o, n_col)))
            return carry

        lax.fori_loop(1, devices, one, 0)

    others(lambda o, at: pl.semaphore_signal(barrier, 1, device_id=at, device_id_type=MESH))
    pl.semaphore_wait(barrier, devices - 1)

    def at_step(steps, core):
        return place_of(x + steps[0], y + steps[1], z + steps[2], core)

    def number(device):
        return device[0] * n_col + device[1]

    def kinds(up):
        return (
            (0, 0, 1, a_send, lambda d: a_recv),
            (0, 1, 0, a_send, lambda d: a_recv),
            (1, core, up, t_send, lambda d: shared_sem.at[d]),
        )

    def source_block(layer, target):
        return packed.at[devices + number(target) // 2 if layer else number(target)]

    def first_leg(k):
        d, steps, far, both, up = step_of(k)
        for i, (layer, side, way, send, recv) in enumerate(kinds(up)):
            first, second = legs(steps, far, way)
            remote(
                source_block(layer, at_step(steps, side)), relay.at[i * CHIPS + d], send,
                relay_sem.at[i * CHIPS + d], at_step(first, core),
            ).start()

    def direct(k):
        d, steps, far, both, up = step_of(k)
        for layer, side, way, send, recv in kinds(up):
            target = at_step(steps, side)
            remote(source_block(layer, target), got.at[layer, me], send, recv(d), target).start()

    def second_leg(k):
        d, steps, far, both, up = step_of(k)

        @pl.when(both)
        def _():
            for i, (layer, side, way, send, recv) in enumerate(kinds(up)):
                first, second = legs(steps, far, way)
                source = number(at_step([4 - f for f in first], core))
                target = at_step(second, side)
                held = relay.at[i * CHIPS + d]
                remote(held, held, r_send, relay_sem.at[i * CHIPS + d], target).wait_recv()
                remote(held, got.at[layer, source], r_send, recv(d), target).start()

    def hand_over(k):
        d, steps, far, both, up = step_of(k)
        source = number(place_of(x + RING - steps[0], y + RING - steps[1], z + RING - steps[2], core))
        remote(got.at[1, source], got.at[1, source], f_send, shared_sem.at[d], sibling).wait_recv()
        remote(got.at[1, source], got.at[1, source], f_send, f_recv, sibling).start()

    others(
        lambda o, at: remote(
            table.at[o], got_table.at[me], table_sems.at[0], table_sems.at[1], at
        ).start()
    )
    remote(packed.at[sibling_id], got.at[0, me], a_send, a_recv, sibling).start()
    remote(packed.at[devices + chip], got.at[1, me], f_send, f_recv, sibling).start()
    def far_step(k, carry):
        both = step_of(k)[3]

        @pl.when(both)
        def _():
            first_leg(k)

        return carry

    def far_relay(k, carry):
        far_step(k, carry)
        second_leg(k - LEAD)
        return carry

    def relay_only(k, carry):
        second_leg(k)
        return carry

    def near_step(k, carry):
        both = step_of(k)[3]
        pl.when(jnp.logical_not(both))(lambda: direct(k))
        return carry

    def end(k, carry):
        hand_over(k)
        return carry

    lax.fori_loop(1, LEAD + 1, far_step, 0)
    lax.fori_loop(LEAD + 1, CHIPS, far_relay, 0)
    lax.fori_loop(1, CHIPS // 2, near_step, 0)
    lax.fori_loop(CHIPS - LEAD, CHIPS, relay_only, 0)
    lax.fori_loop(CHIPS // 2, CHIPS, near_step, 0)
    lax.fori_loop(1, CHIPS, end, 0)
    for copy in own:
        copy.wait()

    def settle(ref, count, sem):
        part = ref.at[pl.ds(0, count)]
        pltpu.make_async_copy(part, part, sem).wait()

    settle(got_table, devices - 1, table_sems.at[1])
    settle(table, devices - 1, table_sems.at[0])
    settle(got.at[0], devices - 1, a_recv)
    settle(got.at[1], CHIPS, f_recv)
    settle(packed, devices - 1, a_send)
    settle(packed, CHIPS - 1, t_send)
    settle(relay, 3 * far_count(), r_send)
    settle(got.at[1], CHIPS, f_send)


def exchange(packed, table, n_row, n_col):
    devices = n_row * n_col
    block = packed.shape[1:]
    return pl.pallas_call(
        functools.partial(exchange_kernel, n_row, n_col),
        out_shape=(
            jax.ShapeDtypeStruct((3, devices) + block, packed.dtype),
            jax.ShapeDtypeStruct(table.shape, table.dtype),
            jax.ShapeDtypeStruct((3 * CHIPS,) + block, packed.dtype),
        ),
        in_specs=[HBM, HBM],
        out_specs=(HBM, HBM, HBM),
        scratch_shapes=[DMA((2,)), DMA((6,)), DMA((3 * CHIPS,)), DMA((CHIPS,)), DMA((3,))],
        compiler_params=pltpu.CompilerParams(collective_id=2, has_side_effects=True),
        name="exchange",
    )(packed, table)


def last_kernel(n_row, n_col, packed, got_in, got, relay, sems, relay_sem, own_sem):
    devices = n_row * n_col
    x, y, z, core = position()
    mine = place_of(x, y, z, core)
    me = mine[0] * n_col + mine[1]
    first_block = devices + CHIPS
    barrier = pltpu.get_barrier_semaphore()

    def at_step(steps, core):
        return place_of(x + steps[0], y + steps[1], z + steps[2], core)

    def number(device):
        return device[0] * n_col + device[1]

    def greet(at):
        pl.semaphore_signal(barrier, 1, device_id=at, device_id_type=MESH)

    def near(k, carry):
        d, steps, far, both, up = step_of(k)

        @pl.when(jnp.logical_and(core == 1, jnp.logical_not(both)))
        def _():
            greet(at_step(steps, 0))
            greet(at_step(steps, 1))

        return carry

    def relayed(k, carry):
        bits = (k // 8, lax.rem(k // 4, 2), lax.rem(k // 2, 2))
        way = lax.rem(k, 2)

        @pl.when(jnp.logical_and(core == 0, k != 15))
        def _():
            greet(at_step([b * (3 - 2 * way) for b in bits], 0))

        return carry

    lax.fori_loop(1, CHIPS, near, 0)
    lax.fori_loop(2, 16, relayed, 0)

    @pl.when(core == 1)
    def _():
        greet(place_of(x, y, z, 0))
        pl.semaphore_wait(barrier, 26)

    @pl.when(core == 0)
    def _():
        pl.semaphore_wait(barrier, 26 + 13 + 1)

    def block_for(target):
        return packed.at[first_block + number(target) // 2]

    def first_leg(k, carry):
        d, steps, far, both, up = step_of(k)

        @pl.when(both)
        def _():
            first, second = legs(steps, far, up)
            remote(
                block_for(at_step(steps, 1)), relay.at[d], sems.at[0], relay_sem.at[d],
                at_step(first, core),
            ).start()

        return carry

    def direct(k, carry):
        d, steps, far, both, up = step_of(k)

        @pl.when(jnp.logical_not(both))
        def _():
            target = at_step(steps, 1)
            remote(block_for(target), got.at[2, me], sems.at[0], sems.at[1], target).start()

        return carry

    def second_leg(k, carry):
        d, steps, far, both, up = step_of(k)

        @pl.when(both)
        def _():
            first, second = legs(steps, far, up)
            source = number(at_step([4 - f for f in first], core))
            target = at_step(second, 1)
            held = relay.at[d]
            remote(held, held, sems.at[2], relay_sem.at[d], target).wait_recv()
            remote(held, got.at[2, source], sems.at[2], sems.at[1], target).start()

        return carry

    lax.fori_loop(1, CHIPS, first_leg, 0)
    lax.fori_loop(1, CHIPS, direct, 0)
    lax.fori_loop(1, CHIPS, second_leg, 0)

    def settle(ref, count, sem):
        part = ref.at[pl.ds(0, count)]
        pltpu.make_async_copy(part, part, sem).wait()

    settle(relay, far_count(), sems.at[2])

    @pl.when(core == 0)
    def _():
        to = place_of(x, y, z, 1)
        remote(packed.at[first_block + me // 2], got.at[2, me], sems.at[0], sems.at[1], to).start()
        settle(packed, CHIPS, sems.at[0])

    @pl.when(core == 1)
    def _():
        own = pltpu.make_async_copy(packed.at[first_block + me // 2], got.at[2, me], own_sem)
        own.start()
        own.wait()
        settle(packed, CHIPS - 1, sems.at[0])
        settle(got.at[2], devices - 1, sems.at[1])


def exchange_last(packed, got, n_row, n_col):
    return pl.pallas_call(
        functools.partial(last_kernel, n_row, n_col),
        out_shape=(
            jax.ShapeDtypeStruct(got.shape, got.dtype),
            jax.ShapeDtypeStruct((CHIPS,) + packed.shape[1:], packed.dtype),
        ),
        in_specs=[HBM, HBM],
        out_specs=(HBM, HBM),
        input_output_aliases={1: 0},
        scratch_shapes=[DMA((3,)), DMA((CHIPS,)), DMA],
        compiler_params=pltpu.CompilerParams(collective_id=3, has_side_effects=True),
        name="exchange_last",
    )(packed, got)[0]


def fetch_target(t, at, total, counts, order, base, got, buffer, sem):
    base[t] = at

    def one(e, c):
        pltpu.make_async_copy(got.at[order[t * total + e]], buffer.at[at + e], sem).start()
        return c

    lax.fori_loop(0, counts[t], one, 0)
    return at + counts[t]


def await_target(t, counts, got, buffer, sem):
    def one(e, c):
        pltpu.make_async_copy(got.at[0], buffer.at[0], sem).wait()
        return c

    lax.fori_loop(0, counts[t], one, 0)


def product(t, e, counts, base, buffer):
    rank = buffer.shape[1] // 2
    n, begin = counts[t], base[t]
    picked = [
        jnp.where(e * STACK + k < n, begin + e * STACK + k, buffer.shape[0] - 1) for k in range(STACK)
    ]
    lefts = jnp.concatenate([buffer[s, 0:rank, :] for s in picked], axis=0)
    rights = jnp.concatenate([buffer[s, rank:, :] for s in picked], axis=0)
    return dot(lefts, rights, ((0,), (0,)))


def add_rest(t, counts, base, buffer, sum_ref, rows, cols):
    def chunk(e, c):
        sum_ref[rows, cols] += product(t, e, counts, base, buffer)
        return c

    lax.fori_loop(1, (counts[t] + STACK - 1) // STACK, chunk, 0)


def split(x):
    high = x.astype(jnp.bfloat16)
    return high, (x - high.astype(jnp.float32)).astype(jnp.bfloat16)


def permutation(pivots):
    size = pivots.shape[1]
    places = lax.broadcasted_iota(jnp.int32, (size, size), 0)
    return (places == pivots).astype(jnp.float32)


def panel_kernel(
    total, table, got, front, pivots, upper_inverse, lower_inverse, column_basis, row_basis,
    column_ranks, row_ranks, a_out, b_out, counts, order, left_sum, top_sum, buffer, top_weights,
    left_weights, coupling, base, sem, front_sem,
):
    size, rank = upper_inverse.shape[0], column_basis.shape[0]
    row_blocks, col_blocks = front.shape[0] // size, front.shape[1] // size
    targets = row_blocks * col_blocks
    devices = table.shape[0]
    is_top, is_left = lax.axis_index("row") == 0, lax.axis_index("col") == 0
    load_left = pltpu.make_async_copy(front.at[:, pl.ds(0, size)], left_sum, front_sem.at[0])
    load_top = pltpu.make_async_copy(front.at[pl.ds(0, size)], top_sum, front_sem.at[1])
    pl.when(is_left)(load_left.start)
    pl.when(is_top)(load_top.start)

    for t in range(targets + 1):
        counts[t] = 0

    def note(s, p):
        t = table[s, 0, p]
        t = jnp.where(t < 0, targets, t)
        n = counts[t]
        order[t * total + n] = p * devices + s
        counts[t] = n + 1

    def tally(s, flags):
        note(s, 0)
        note(s, 1)
        return jnp.maximum(flags, table[s, 0, 3])

    def tally_last(s, c):
        note(s, 2)
        return c

    flags = lax.fori_loop(0, devices, tally, -1, unroll=4)
    lax.fori_loop(0, jnp.where(flags >= 0, devices, 0), tally_last, 0)

    @pl.when(jnp.logical_or(is_top, is_left))
    def _():
        buffer[buffer.shape[0] - 1] = jnp.zeros(buffer.shape[1:], buffer.dtype)

        def fetch(t, at):
            return fetch_target(t, at, total, counts, order, base, got, buffer, sem)

        def fetch_left(i, at):
            return fetch(i * col_blocks, at)

        at = lax.fori_loop(0, jnp.where(is_left, row_blocks, 0), fetch_left, 0)
        lax.fori_loop(jnp.where(is_left, 1, 0), jnp.where(is_top, col_blocks, 0), fetch, at)

    @pl.when(is_top)
    def _():
        weights = dot(row_basis[...], lower_inverse[...], precision=HIGHEST)
        weights = dot(weights, permutation(pivots[...]), ((1,), (1,)), precision=HIGHEST)
        top_weights[0:rank] = weights
        top_weights[rank:] = weights

    @pl.when(is_left)
    def _():
        left_weights[...] = dot(
            upper_inverse[...], column_basis[...], ((1,), (1,)), precision=HIGHEST
        )
        coupled = dot(column_basis[...], row_basis[...], ((1,), (1,)), precision=HIGHEST)
        coupling[...] = jnp.concatenate([coupled, coupled], axis=1)

    @pl.when(jnp.logical_or(is_top, is_left))
    def _():
        def ready(t):
            await_target(t, counts, got, buffer, sem)

        def ready_left(i, c):
            ready(i * col_blocks)
            return c

        def ready_top(t, c):
            ready(t)
            return c

        lax.fori_loop(0, jnp.where(is_left, row_blocks, 0), ready_left, 0)
        lax.fori_loop(jnp.where(is_left, 1, 0), jnp.where(is_top, col_blocks, 0), ready_top, 0)

    @pl.when(is_top)
    def _():
        row = lax.broadcasted_iota(jnp.int32, (2 * rank, size), 0)
        load_top.wait()
        for j in range(col_blocks):
            cols = slice(j * size, (j + 1) * size)
            top_sum[:, cols] += product(j, 0, counts, base, buffer)
        for j in range(col_blocks):
            add_rest(j, counts, base, buffer, top_sum, slice(0, size), slice(j * size, (j + 1) * size))
        for j in range(col_blocks):
            cols = slice(j * size, (j + 1) * size)
            factor = dot(top_weights[...], top_sum[:, cols], precision=HIGHEST)
            factor = jnp.where(lax.rem(row, rank) < row_ranks[j], factor, 0.0)
            high, low = split(factor)
            value = jnp.where(row < rank, high.astype(jnp.float32), low.astype(jnp.float32))
            for h in range(size // 128):
                b_out[j * (size // 128) + h] = value[:, h * 128 : (h + 1) * 128].astype(jnp.bfloat16)

    @pl.when(is_left)
    def _():
        lane = lax.broadcasted_iota(jnp.int32, (size, 2 * rank), 1)
        load_left.wait()

        def add(i, c):
            rows = pl.ds(pl.multiple_of(i * size, size), size)
            left_sum[rows, :] += product(i * col_blocks, 0, counts, base, buffer)
            return c

        lax.fori_loop(0, row_blocks, add, 0, unroll=4)

        def add_more(i, c):
            rows = pl.ds(pl.multiple_of(i * size, size), size)
            add_rest(i * col_blocks, counts, base, buffer, left_sum, rows, slice(0, size))
            return c

        lax.fori_loop(0, row_blocks, add_more, 0)

        def block(i, c):
            rows = pl.ds(pl.multiple_of(i * size, size), size)
            factor = dot(left_sum[rows, :], left_weights[...], precision=HIGHEST)
            factor = jnp.where(lane[:, 0:rank] < column_ranks[i], factor, 0.0)
            high, low = split(dot(factor, coupling[...], precision=HIGHEST))
            value = jnp.where(lane < rank, high.astype(jnp.float32), low.astype(jnp.float32))
            for h in range(size // 128):
                a_out[i * (size // 128) + h] = value[h * 128 : (h + 1) * 128].astype(jnp.bfloat16)
            return c

        lax.fori_loop(0, row_blocks, block, 0, unroll=4)


def panel(
    table, got, front, pivots, upper_inverse, lower_inverse, column_basis, row_basis, column_ranks,
    row_ranks,
):
    depth, size = got.shape[1:]
    total = table.shape[0] * CAP
    rows, cols = front.shape
    targets = (rows // size) * (cols // size)
    return pl.pallas_call(
        functools.partial(panel_kernel, total),
        out_shape=(
            jax.ShapeDtypeStruct((rows // 128, 128, 128), jnp.bfloat16),
            jax.ShapeDtypeStruct((cols // 128, 128, 128), jnp.bfloat16),
            jax.ShapeDtypeStruct((targets + 1,), jnp.int32),
            jax.ShapeDtypeStruct(((targets + 2) * total,), jnp.int32),
        ),
        in_specs=[SMEM, HBM, HBM, VMEM, VMEM, VMEM, VMEM, VMEM, SMEM, SMEM],
        out_specs=(VMEM, VMEM, SMEM, SMEM),
        scratch_shapes=[
            pltpu.VMEM((rows, size), jnp.float32),
            pltpu.VMEM((size, cols), jnp.float32),
            pltpu.VMEM((total + 1, depth, size), jnp.bfloat16),
            pltpu.VMEM((depth, size), jnp.float32),
            pltpu.VMEM((size, depth // 2), jnp.float32),
            pltpu.VMEM((depth // 2, depth), jnp.float32),
            pltpu.SMEM((targets,), jnp.int32),
            DMA,
            DMA((2,)),
        ],
        compiler_params=pltpu.CompilerParams(vmem_limit_bytes=LIMIT),
        name="panel",
    )(
        table, got, front, pivots, upper_inverse, lower_inverse, column_basis, row_basis,
        column_ranks, row_ranks,
    )


def spread_kernel(
    n_row, n_col, a_src, b_src, a_all, b_all, a_part_send, a_part_recv, b_part_send, b_part_recv,
    a_send, a_recv, b_send, b_recv, swap_sem, own_sem,
):
    r, c = lax.axis_index("row"), lax.axis_index("col")
    half = n_col // 2
    chip, core = c // 2, lax.rem(c, 2)
    sibling = (r, chip * 2 + 1 - core)
    barrier = pltpu.get_barrier_semaphore()

    def mates(n, me, body):
        def one(k, carry):
            body(lax.rem(me + k, n))
            return carry

        lax.fori_loop(1, n, one, 0)

    mates(n_col, c, lambda o: pl.semaphore_signal(barrier, 1, device_id=(r, o), device_id_type=MESH))
    mates(n_row, r, lambda o: pl.semaphore_signal(barrier, 1, device_id=(o, c), device_id_type=MESH))
    pl.semaphore_wait(barrier, n_col + n_row - 2)

    def piece(o):
        return lax.rem(o, 2) * half + o // 2

    def a_part(o):
        return remote(a_src.at[piece(o)], a_all.at[piece(o)], a_part_send.at[o], a_part_recv, (r, o))

    def b_part(o):
        return remote(b_src.at[o], b_all.at[o], b_part_send.at[o], b_part_recv, (o, c))

    def a_full(h):
        at = piece(c)
        return remote(a_all.at[at], a_all.at[at], a_send.at[h], a_recv.at[chip], (r, h * 2 + core))

    def a_from(h):
        at = core * half + h
        return remote(a_all.at[at], a_all.at[at], a_send.at[h], a_recv.at[h], (r, h * 2 + core))

    def b_full(o):
        return remote(b_all.at[r], b_all.at[r], b_send.at[o], b_recv.at[r], (o, c))

    def b_from(o):
        return remote(b_all.at[o], b_all.at[o], b_send.at[o], b_recv.at[o], (o, c))

    def swap(side):
        part = a_all.at[pl.ds(side * half, half)]
        return remote(part, part, swap_sem.at[0], swap_sem.at[1], sibling)

    @pl.when(c == 0)
    def _():
        mates(n_col, c, lambda o: a_part(o).start())
        own = pltpu.make_async_copy(a_src.at[0], a_all.at[0], own_sem.at[0])
        own.start()
        own.wait()

    @pl.when(r == 0)
    def _():
        mates(n_row, r, lambda o: b_part(o).start())
        own = pltpu.make_async_copy(b_src.at[0], b_all.at[0], own_sem.at[1])
        own.start()
        own.wait()

    @pl.when(c != 0)
    def _():
        a_part(c).wait_recv()

    mates(half, chip, lambda h: a_full(h).start())

    @pl.when(r != 0)
    def _():
        b_part(r).wait_recv()

    mates(n_row, r, lambda o: b_full(o).start())
    mates(half, chip, lambda h: a_from(h).wait_recv())
    swap(core).start()
    mates(n_row, r, lambda o: b_from(o).wait_recv())
    swap(1 - core).wait_recv()
    mates(half, chip, lambda h: a_full(h).wait_send())
    mates(n_row, r, lambda o: b_full(o).wait_send())
    swap(core).wait_send()

    @pl.when(c == 0)
    def _():
        mates(n_col, c, lambda o: a_part(o).wait_send())

    @pl.when(r == 0)
    def _():
        mates(n_row, r, lambda o: b_part(o).wait_send())


def spread(a_src, b_src, n_row, n_col):
    return pl.pallas_call(
        functools.partial(spread_kernel, n_row, n_col),
        out_shape=(
            jax.ShapeDtypeStruct(a_src.shape, a_src.dtype),
            jax.ShapeDtypeStruct(b_src.shape, b_src.dtype),
        ),
        in_specs=[VMEM, VMEM],
        out_specs=(VMEM, VMEM),
        scratch_shapes=[
            DMA((n_col,)), DMA, DMA((n_row,)), DMA,
            DMA((n_col // 2,)), DMA((n_col // 2,)), DMA((n_row,)), DMA((n_row,)), DMA((2,)), DMA((2,)),
        ],
        compiler_params=pltpu.CompilerParams(collective_id=1, has_side_effects=True),
        name="spread",
    )(a_src, b_src)


def finish_kernel(
    total, counts, order, got, front, a_all, b_all, pivots, upper_inverse, lower_inverse, out,
    extended, buffer, b_cat, inverse_parts, corner, base, sem, front_sem, out_sem,
):
    size = upper_inverse.shape[0]
    row_blocks, col_blocks = front.shape[0] // size, front.shape[1] // size
    lanes = a_all.shape[2]
    rank = lanes // 2
    pieces = size // lanes
    is_top, is_left = lax.axis_index("row") == 0, lax.axis_index("col") == 0

    def rows(i):
        return pl.ds(pl.multiple_of(i * size, size), size)

    def load(i):
        return pltpu.make_async_copy(front.at[rows(i)], extended.at[rows(i)], front_sem.at[i])

    def store(i):
        return pltpu.make_async_copy(extended.at[rows(i)], out.at[rows(i)], out_sem.at[i])

    load(0).start()

    def fetch(i, at):
        for j in range(col_blocks):
            at = fetch_target(
                i * col_blocks + j, at, total, counts, order, base, got, buffer, sem.at[i]
            )
        pl.when(i + 1 < row_blocks)(lambda: load(i + 1).start())
        return at

    lax.fori_loop(0, row_blocks, fetch, 0)
    buffer[buffer.shape[0] - 1] = jnp.zeros(buffer.shape[1:], buffer.dtype)

    @pl.when(is_left)
    def _():
        high, low = split(upper_inverse[...])
        inverse_parts[0:size] = high
        inverse_parts[size : 2 * size] = low
        inverse_parts[2 * size :] = high

    for k in range(b_all.shape[0]):
        cols = slice(k * lanes, (k + 1) * lanes)
        high, low = b_all[k, 0:rank, :], b_all[k, rank:, :]
        if k < pieces:
            high = jnp.where(is_left, jnp.zeros_like(high), high)
            low = jnp.where(is_left, jnp.zeros_like(low), low)
        for h in range(2):
            b_cat[h * rank : (h + 1) * rank, cols] = high
            b_cat[(2 + h) * rank : (3 + h) * rank, cols] = low

    def step(i, c):
        load(i).wait()
        for j in range(col_blocks):
            await_target(i * col_blocks + j, counts, got, buffer, sem.at[i])
        a = jnp.concatenate([a_all[i * pieces + k] for k in range(pieces)], axis=0)
        a = jnp.concatenate([a, a], axis=1)
        a = jnp.where(jnp.logical_and(is_top, i == 0), jnp.zeros_like(a), a)
        for j in range(col_blocks):
            cols = slice(j * size, (j + 1) * size)
            added = product(i * col_blocks + j, 0, counts, base, buffer)
            extended[rows(i), cols] += added - dot(a, b_cat[:, cols])
        for j in range(col_blocks):
            cols = slice(j * size, (j + 1) * size)
            add_rest(i * col_blocks + j, counts, base, buffer, extended, rows(i), cols)

        @pl.when(jnp.logical_and(is_left, jnp.logical_not(jnp.logical_and(is_top, i == 0))))
        def _():
            high, low = split(extended[rows(i), 0:size])
            extended[rows(i), 0:size] = dot(
                jnp.concatenate([high, high, low], axis=1), inverse_parts[...]
            )

        @pl.when(jnp.logical_and(is_top, i == 0))
        def _():
            permute = permutation(pivots[...])
            corner[...] = dot(permute, extended[0:size, 0:size], ((0,), (0,)), precision=HIGHEST)
            weights = dot(lower_inverse[...], permute, ((1,), (1,)), precision=HIGHEST)
            for j in range(col_blocks):
                cols = slice(j * size, (j + 1) * size)
                upper = dot(weights, extended[0:size, cols], precision=HIGHEST)
                if j == 0:
                    upper = jnp.where(is_left, corner[...], upper)
                extended[0:size, cols] = upper

        store(i).start()
        return c

    lax.fori_loop(0, row_blocks, step, 0)
    for i in range(row_blocks):
        store(i).wait()


def finish(counts, order, got, front, a_all, b_all, pivots, upper_inverse, lower_inverse, total):
    depth, size = got.shape[1:]
    rows, cols = front.shape
    row_blocks = rows // size
    targets = row_blocks * (cols // size)
    return pl.pallas_call(
        functools.partial(finish_kernel, total),
        out_shape=jax.ShapeDtypeStruct(front.shape, jnp.float32),
        in_specs=[SMEM, SMEM, HBM, HBM, VMEM, VMEM, VMEM, VMEM, VMEM],
        out_specs=HBM,
        scratch_shapes=[
            pltpu.VMEM(front.shape, jnp.float32),
            pltpu.VMEM((total + 1, depth, size), jnp.bfloat16),
            pltpu.VMEM((2 * depth, cols), jnp.bfloat16),
            pltpu.VMEM((3 * size, size), jnp.bfloat16),
            pltpu.VMEM((size, size), jnp.float32),
            pltpu.SMEM((targets,), jnp.int32),
            DMA((row_blocks,)), DMA((row_blocks,)), DMA((row_blocks,)),
        ],
        compiler_params=pltpu.CompilerParams(vmem_limit_bytes=LIMIT),
        name="finish",
    )(counts, order, got, front, a_all, b_all, pivots, upper_inverse, lower_inverse)


def shards(
    front, child_left, child_right, child_owner, child_slot, pivots, upper_inverse, lower_inverse,
    column_basis, row_basis, column_ranks, row_ranks,
):
    n_row, n_col = lax.axis_size("row"), lax.axis_size("col")
    devices = n_row * n_col
    packed, table = pack(
        child_owner[:, 0], child_slot, jnp.swapaxes(child_left, 1, 2), child_right, devices
    )
    got, got_table, relayed = exchange(packed, table, n_row, n_col)
    rounds = (jnp.max(got_table[:, 0, 3]) >= 0).astype(jnp.int32)
    got = lax.fori_loop(0, rounds, lambda i, g: exchange_last(packed, g, n_row, n_col), got)
    got = got.reshape((3 * devices,) + got.shape[2:])
    a_src, b_src, counts, order = panel(
        got_table, got, front, pivots[None, :], upper_inverse, lower_inverse, column_basis.T,
        row_basis.T, column_ranks, row_ranks,
    )
    a_all, b_all = spread(a_src, b_src, n_row, n_col)
    return finish(
        counts, order, got, front, a_all, b_all, pivots[None, :], upper_inverse, lower_inverse,
        devices * CAP,
    )


def solution(mesh):
    in_specs = (
        P("row", "col"),
        P(("row", "col"), None, None),
        P(("row", "col"), None, None),
        P(("row", "col"), None),
        P(("row", "col")),
        P(),
        P(),
        P(),
        P(),
        P(),
        P("row"),
        P("col"),
    )
    out_specs = P("row", "col")
    return jax.shard_map(shards, mesh=mesh, in_specs=in_specs, out_specs=out_specs, check_vma=False)
```

```python
import functools

import jax
import jax.numpy as jnp
from jax import lax
from jax.experimental import pallas as pl
from jax.experimental.pallas import tpu as pltpu
from jax.sharding import PartitionSpec as P

MESH = pl.DeviceIdType.MESH
HBM = pl.BlockSpec(memory_space=pl.ANY)
SMEM = pl.BlockSpec(memory_space=pltpu.SMEM)
VMEM = pl.BlockSpec(memory_space=pltpu.VMEM)
DMA = pltpu.SemaphoreType.DMA
CAP = 2
STACK = 4
STRIDE = 37
RING = 4
CHIPS = RING**3
LEAD = 16
LIMIT = 56 * 1024 * 1024
HIGHEST = lax.Precision.HIGHEST


def dot(a, b, dims=((1,), (0,)), precision=None):
    return lax.dot_general(
        a, b, (dims, ((), ())), precision=precision, preferred_element_type=jnp.float32
    )


def pack_kernel(
    devices, owner, owner_row, slot_row, left, right, packed, table, staged, named, placed, in_sem,
    out_sem,
):
    count, rank = left.shape[0], left.shape[1]
    chips = devices // 2
    chunks = in_sem.shape[0]
    each = count // chunks

    def load(k):
        part = pl.ds(k * each, each)
        return (
            pltpu.make_async_copy(left.at[part], staged.at[part, pl.ds(0, rank)], in_sem.at[k, 0]),
            pltpu.make_async_copy(right.at[part], staged.at[part, pl.ds(rank, rank)], in_sem.at[k, 1]),
        )

    for k in range(chunks):
        for copy in load(k):
            copy.start()

    def clear(o, c):
        named[o] = 0
        placed[o] = 0
        return c

    lax.fori_loop(0, devices, clear, 0, unroll=8)

    def tally(i, c):
        named[owner[i]] += 1
        return c

    lax.fori_loop(0, count, tally, 0, unroll=4)

    shape = (devices, 1, count)
    place = lax.broadcasted_iota(jnp.int32, shape, 2)
    device = lax.broadcasted_iota(jnp.int32, shape, 0)
    owners = owner_row[...][None]
    code = (place * 64 + slot_row[...][None]).astype(jnp.float32)

    def ends(which):
        least = jnp.min(jnp.where(which, code, 65536.0), axis=2, keepdims=True)
        most = jnp.max(jnp.where(which, code, -1.0), axis=2, keepdims=True)
        return least, most

    least, most = ends(owners == device)
    low_least, low_most = ends(owners == device - (device & 1))
    core = device[:, :, 0:1] & 1
    first = jnp.where(most >= 0.0, least.astype(jnp.int32) & 63, -1)
    second = jnp.where(most > least, most.astype(jnp.int32) & 63, -1)
    late = jnp.logical_and(core == 1, low_most > low_least)
    last = jnp.where(late, second, -1)
    flag = jnp.max(last.astype(jnp.float32), axis=0, keepdims=True).astype(jnp.int32)
    lane = lax.broadcasted_iota(jnp.int32, table.shape, 2)
    line = jnp.where(lane == 0, first, jnp.where(lane == 1, jnp.where(late, -1, second), -1))
    table[...] = jnp.where(lane == 2, last, jnp.where(lane == 3, flag, line))

    for k in range(chunks):
        for copy in load(k):
            copy.wait()

        def send(i, c):
            o = owner[i]
            p = placed[o]
            placed[o] = 1
            core = o & 1
            x, y, z = o >> 5, (o >> 2) & 3, (o & 2) | ((o >> 4) & 1)
            late = jnp.logical_and(core == 1, named[o - core] == 2)
            first = jnp.where(core == 0, x * 16 + y * 4 + z, chips + y * 16 + z * 4 + x)
            second = 2 * chips + z * 16 + x * 4 + y
            extra = jnp.where(late, 3 * chips + (o >> 1), second)
            at = jnp.where(p == 0, first, extra)
            pltpu.make_async_copy(staged.at[i], packed.at[at], out_sem).start()
            return c

        lax.fori_loop(k * each, (k + 1) * each, send, 0)
    pltpu.make_async_copy(staged, packed.at[pl.ds(0, count)], out_sem).wait()


def pack(owner, slots, left, right, devices):
    count, rank, size = left.shape
    return pl.pallas_call(
        functools.partial(pack_kernel, devices),
        out_shape=(
            jax.ShapeDtypeStruct((2 * devices, 2 * rank, size), left.dtype),
            jax.ShapeDtypeStruct((devices, 1, 128), jnp.int32),
        ),
        in_specs=[SMEM, VMEM, VMEM, HBM, HBM],
        out_specs=(HBM, VMEM),
        scratch_shapes=[
            pltpu.VMEM((count, 2 * rank, size), left.dtype),
            pltpu.SMEM((devices,), jnp.int32),
            pltpu.SMEM((devices,), jnp.int32),
            DMA((4, 2)),
            DMA,
        ],
        compiler_params=pltpu.CompilerParams(vmem_limit_bytes=LIMIT),
        name="pack",
    )(owner, owner[None, :], slots[None, :], left, right)


def position():
    r, q = lax.axis_index("row"), lax.axis_index("col")
    return r // 2, q // 4, lax.rem(q // 2, 2) * 2 + lax.rem(r, 2), lax.rem(q, 2)


def place_of(x, y, z, core):
    x, y, z = lax.rem(x, RING), lax.rem(y, RING), lax.rem(z, RING)
    return x * 2 + lax.rem(z, 2), y * 4 + (z // 2) * 2 + core


def step_of(k):
    d = lax.rem(k * STRIDE, CHIPS)
    steps = (d // (RING * RING), lax.rem(d // RING, RING), lax.rem(d, RING))
    far = [s // 2 - s // 3 for s in steps]
    both = far[0] + far[1] + far[2] > 0
    up = 1 - lax.rem(steps[0] + steps[1] + steps[2], 2)
    return d, steps, far, both, up


def legs(steps, far, up):
    ahead = [f * (3 - 2 * up) for f in far]
    return ahead, [s + 4 - a for s, a in zip(steps, ahead)]


def far_count():
    return sum(2 in (d // 16, d // 4 % 4, d % 4) for d in range(1, CHIPS))


def remote(src, dst, send, recv, device):
    return pltpu.make_async_remote_copy(
        src_ref=src, dst_ref=dst, send_sem=send, recv_sem=recv, device_id=device,
        device_id_type=MESH,
    )


class Ring:
    def __init__(self, at, go, source, target, relay, send_sem, recv_sem, origin=0):
        self.at, self.go, self.source, self.target = at, go, source, target
        self.relay, self.send_sem, self.recv_sem, self.origin = relay, send_sem, recv_sem, origin

    def copy(self, src, dst, i, way):
        return remote(src, dst, self.send_sem.at[i], self.recv_sem.at[i], self.go(1 if way == 0 else 3))

    def by(self, d):
        return lax.rem(self.at + d, RING)

    def begin(self):
        for way in range(2):
            self.copy(self.source(self.by(2), way), self.relay(way), 4 + way, way).start()
        for way, d in ((0, 1), (1, 3)):
            self.copy(self.source(self.by(d), None), self.target(self.at, None), way, way).start()

    def begin_sent(self):
        for way in range(2):
            self.copy(self.source(self.by(2), way), self.relay(way), 4 + way, way).wait_send()
        for way, d in ((0, 1), (1, 3)):
            self.copy(self.source(self.by(d), None), self.target(self.at, None), way, way).wait_send()

    def forward(self):
        for way, d in ((0, 3), (1, 1)):
            held = self.relay(way)
            self.copy(held, held, 4 + way, way).wait_recv()
            self.copy(held, self.target(self.by(d), way), 2 + way, way).start()

    def forward_sent(self):
        for way, d in ((0, 3), (1, 1)):
            self.copy(self.relay(way), self.target(self.by(d), way), 2 + way, way).wait_send()

    def arrived(self):
        for way, d in ((0, 3), (1, 1)):
            part = self.target(self.by(d), None)
            self.copy(part, part, way, way).wait_recv()
        for way in range(2):
            part = self.target(self.by(2), way)
            self.copy(part, part, 2 + way, way).wait_recv()


def exchange_kernel(
    n_row, n_col, packed, table, got, got_table, a_one, a_two, t_one, t_two, a_relay_one,
    a_relay_two, a_relay_three, t_relay_one, t_relay_two, t_relay_three, a_stage_one, a_stage_two,
    a_stage_three, t_stage, t_last, table_sems, send_sems, recv_sems, hand_sems, own_sems,
):
    devices = n_row * n_col
    x, y, z, core = position()
    here = (x, y, z)
    mine = place_of(x, y, z, core)
    me = mine[0] * n_col + mine[1]
    sibling = place_of(x, y, z, 1 - core)
    barrier = pltpu.get_barrier_semaphore()

    def others(body):
        def one(k, carry):
            o = lax.rem(me + k, devices)
            body(o, (o // n_col, lax.rem(o, n_col)))
            return carry

        lax.fori_loop(1, devices, one, 0)

    own_table = pltpu.make_async_copy(table.at[me], got_table.at[me], own_sems.at[6])
    own_table.start()
    others(lambda o, at: pl.semaphore_signal(barrier, 1, device_id=at, device_id_type=MESH))
    pl.semaphore_wait(barrier, devices - 1)

    def along(axis, to_core):
        def go(d):
            return place_of(*[here[i] + (d if i == axis else 0) for i in range(3)], to_core)

        return here[axis], go

    def along_mine(phase):
        axes = [lax.rem(phase + core, 3) == i for i in range(3)]
        picked = [axes[i].astype(jnp.int32) for i in range(3)]
        at = sum(p * h for p, h in zip(picked, here))
        return at, lambda d: place_of(*[h + d * p for p, h in zip(picked, here)], core)

    def half(ref_at, width):
        return lambda i, h: ref_at(i, pl.ds(0, 2 * width) if h is None else pl.ds(h * width, width))

    def first_rings(kind):
        at, go = along(kind, kind)
        return Ring(
            at, go, half(lambda j, s: packed.at[kind, j, s], 2),
            half(lambda i, s: a_one.at[i * 2 + core, s], 2), lambda way: a_relay_one.at[way, core],
            send_sems.at[kind], recv_sems.at[core],
        )

    def first_mine(origin):
        at, go = along_mine(0)
        return Ring(
            at, go, None, half(lambda i, s: a_one.at[i * 2 + origin, s], 2),
            lambda way: a_relay_one.at[way, origin], send_sems.at[2 + origin], recv_sems.at[origin],
        )

    at, go = along_mine(1)
    a_second = Ring(
        at, go, half(lambda j, s: a_one.at[s, j], 4), half(lambda i, s: a_two.at[i, s], 4),
        lambda way: a_relay_two.at[way], send_sems.at[4], recv_sems.at[2],
    )
    at, go = along_mine(2)
    a_third = Ring(
        at, go, half(lambda j, s: a_two.at[s, slice(None), j], 2), half(lambda i, s: got.at[i, s], 2),
        lambda way: a_relay_three.at[way], send_sems.at[5], recv_sems.at[3],
    )
    t_first = Ring(
        *along(2, core), half(lambda j, s: packed.at[2, j, s], 2), half(lambda i, s: t_one.at[i, s], 2),
        lambda way: t_relay_one.at[way], send_sems.at[6], recv_sems.at[4],
    )

    def t_two_part(i, h):
        begin = lax.rem(i, 2) * 4
        part = pl.ds(begin, 4) if h is None else pl.ds(begin + 2 * h, 2)
        return t_two.at[i // 2, part]

    t_second = Ring(
        *along(0, core), half(lambda j, s: t_one.at[s, j], 2), t_two_part,
        lambda way: t_relay_two.at[way], send_sems.at[7], recv_sems.at[5],
    )

    def t_got(side):
        def part(i, h):
            begin = lax.rem(i, 2) * 2
            rows = pl.ds(begin, 2) if h is None else pl.ds(begin + h, 1)
            return got.at[4 + side * 2 + i // 2, rows]

        return part

    t_third = Ring(
        *along(1, core), half(lambda j, s: t_two.at[s, slice(None), j], 1), t_got(core),
        lambda way: t_relay_three.at[way], send_sems.at[8], recv_sems.at[6],
    )

    class Keep:
        def __init__(self, src, stage, dst, i):
            self.load = pltpu.make_async_copy(src, stage, own_sems.at[i])
            self.store = pltpu.make_async_copy(stage, dst, own_sems.at[i])

        def run(self):
            self.load.wait()
            self.store.start()

    def keep(ring, stage, i):
        return Keep(ring.source(ring.at, None), stage, ring.target(ring.at, None), i)

    def to_sibling(kind):
        ring = first_rings(kind)
        return remote(
            ring.source(ring.at, None), ring.target(ring.at, None), hand_sems.at[0, 4],
            hand_sems.at[1, 4], sibling,
        )

    others(
        lambda o, at: remote(
            table.at[o], got_table.at[me], table_sems.at[0], table_sems.at[1], at
        ).start()
    )
    first_rings(0).begin()
    first_rings(1).begin()
    t_first.begin()
    for kind in range(2):
        ring = first_rings(kind)

        @pl.when(core == kind)
        def _():
            Keep(ring.source(ring.at, None), a_stage_one, ring.target(ring.at, None), 0).load.start()

        @pl.when(core != kind)
        def _():
            to_sibling(kind).start()

    t_keep = keep(t_first, t_stage.at[0], 1)
    t_keep.load.start()
    for kind in range(2):
        ring = first_rings(kind)

        @pl.when(core == kind)
        def _():
            Keep(ring.source(ring.at, None), a_stage_one, ring.target(ring.at, None), 0).run()

    t_keep.run()
    for origin in range(2):
        first_mine(origin).forward()
    t_first.forward()
    for origin in range(2):
        first_mine(origin).arrived()
    for kind in range(2):
        ring = first_rings(kind)

        @pl.when(core == kind)
        def _():
            Keep(ring.source(ring.at, None), a_stage_one, ring.target(ring.at, None), 0).store.wait()

        @pl.when(core != kind)
        def _():
            to_sibling(kind).wait_send()

        @pl.when(core == kind)
        def _():
            to_sibling(kind).wait_recv()

    a_second.begin()
    a_keep = keep(a_second, a_stage_two, 2)
    a_keep.load.start()
    t_first.arrived()
    t_keep.store.wait()
    t_second.begin()
    t_keep = keep(t_second, t_stage.at[1], 3)
    t_keep.load.start()
    a_keep.run()
    t_keep.run()
    a_second.forward()
    t_second.forward()
    a_second.arrived()
    a_keep.store.wait()
    a_third.begin()
    a_keep = keep(a_third, a_stage_three, 4)
    a_keep.load.start()
    t_second.arrived()
    t_keep.store.wait()
    t_third.begin()
    last = Keep(t_third.source(y, None), t_last, t_third.target(y, None), 5)
    last.load.start()
    a_keep.run()
    last.run()
    t_third.forward()
    a_third.forward()
    last.store.wait()

    def hand(side, d):
        part = t_got(side)(lax.rem(y + d, RING), None)
        return remote(part, part, hand_sems.at[0, d], hand_sems.at[1, d], sibling)

    hand(core, 0).start()
    t_third.arrived()
    for d in range(1, RING):
        hand(core, d).start()
    a_third.arrived()
    a_keep.store.wait()
    for d in range(RING):
        hand(1 - core, d).wait_recv()
    own_table.wait()
    first_rings(0).begin_sent()
    first_rings(1).begin_sent()
    for origin in range(2):
        first_mine(origin).forward_sent()
    for ring in (t_first, a_second, t_second, a_third, t_third):
        ring.begin_sent()
        ring.forward_sent()
    for d in range(RING):
        hand(core, d).wait_send()
    rest = pl.ds(0, devices - 1)
    pltpu.make_async_copy(table.at[rest], got_table.at[rest], table_sems.at[1]).wait()
    pltpu.make_async_copy(table.at[rest], got_table.at[rest], table_sems.at[0]).wait()


def exchange(packed, table, n_row, n_col):
    block = packed.shape[4:]

    def held(*shape):
        return jax.ShapeDtypeStruct(shape + block, packed.dtype)

    def stage(*shape):
        return pltpu.VMEM(shape + block, packed.dtype)

    return pl.pallas_call(
        functools.partial(exchange_kernel, n_row, n_col),
        out_shape=(
            held(12, 4, 8), jax.ShapeDtypeStruct(table.shape, table.dtype),
            held(8, 4, 4), held(4, 8, 4), held(4, 4, 4), held(2, 8, 4),
            held(2, 2, 2, 4), held(2, 4, 4), held(2, 2, 8), held(2, 2, 4), held(2, 2, 4), held(2, 1, 8),
        ),
        in_specs=[HBM, HBM],
        out_specs=(HBM,) * 12,
        scratch_shapes=[
            stage(4, 4), stage(8, 4), stage(4, 8), stage(2, 4, 4), stage(2, 8),
            DMA((2,)), DMA((9, 6)), DMA((7, 6)), DMA((2, 5)), DMA((7,)),
        ],
        compiler_params=pltpu.CompilerParams(
            collective_id=2, has_side_effects=True, vmem_limit_bytes=LIMIT
        ),
        name="exchange",
    )(packed, table)[:2]


def last_kernel(n_row, n_col, packed, got_in, got, relay, sems, relay_sem, own_sem):
    devices = n_row * n_col
    x, y, z, core = position()
    mine = place_of(x, y, z, core)
    me = mine[0] * n_col + mine[1]
    barrier = pltpu.get_barrier_semaphore()

    def at_step(steps, core):
        return place_of(x + steps[0], y + steps[1], z + steps[2], core)

    def number(device):
        return device[0] * n_col + device[1]

    def greet(at):
        pl.semaphore_signal(barrier, 1, device_id=at, device_id_type=MESH)

    def near(k, carry):
        d, steps, far, both, up = step_of(k)

        @pl.when(jnp.logical_and(core == 1, jnp.logical_not(both)))
        def _():
            greet(at_step(steps, 0))
            greet(at_step(steps, 1))

        return carry

    def relayed(k, carry):
        bits = (k // 8, lax.rem(k // 4, 2), lax.rem(k // 2, 2))
        way = lax.rem(k, 2)

        @pl.when(jnp.logical_and(core == 0, k != 15))
        def _():
            greet(at_step([b * (3 - 2 * way) for b in bits], 0))

        return carry

    lax.fori_loop(1, CHIPS, near, 0)
    lax.fori_loop(2, 16, relayed, 0)

    @pl.when(core == 1)
    def _():
        greet(place_of(x, y, z, 0))
        pl.semaphore_wait(barrier, 26)

    @pl.when(core == 0)
    def _():
        pl.semaphore_wait(barrier, 26 + 13 + 1)

    def block_for(target):
        chip = number(target) // 2
        return packed.at[3, chip // 16, lax.rem(chip // 4, 4), lax.rem(chip, 4)]

    def landing(source):
        return got.at[8 + source // 32, lax.rem(source // 8, 4), lax.rem(source, 8)]

    def first_leg(k, carry):
        d, steps, far, both, up = step_of(k)

        @pl.when(both)
        def _():
            first, second = legs(steps, far, up)
            remote(
                block_for(at_step(steps, 1)), relay.at[d], sems.at[0], relay_sem.at[d],
                at_step(first, core),
            ).start()

        return carry

    def direct(k, carry):
        d, steps, far, both, up = step_of(k)

        @pl.when(jnp.logical_not(both))
        def _():
            target = at_step(steps, 1)
            remote(block_for(target), landing(me), sems.at[0], sems.at[1], target).start()

        return carry

    def second_leg(k, carry):
        d, steps, far, both, up = step_of(k)

        @pl.when(both)
        def _():
            first, second = legs(steps, far, up)
            source = number(at_step([4 - f for f in first], core))
            target = at_step(second, 1)
            held = relay.at[d]
            remote(held, held, sems.at[2], relay_sem.at[d], target).wait_recv()
            remote(held, landing(source), sems.at[2], sems.at[1], target).start()

        return carry

    lax.fori_loop(1, CHIPS, first_leg, 0)
    lax.fori_loop(1, CHIPS, direct, 0)
    lax.fori_loop(1, CHIPS, second_leg, 0)

    def settle(ref, count, sem):
        part = ref.at[pl.ds(0, count)]
        pltpu.make_async_copy(part, part, sem).wait()

    settle(relay, far_count(), sems.at[2])

    @pl.when(core == 0)
    def _():
        to = place_of(x, y, z, 1)
        remote(block_for(to), landing(me), sems.at[0], sems.at[1], to).start()
        settle(relay, CHIPS, sems.at[0])

    @pl.when(core == 1)
    def _():
        own = pltpu.make_async_copy(block_for(mine), landing(me), own_sem)
        own.start()
        own.wait()
        settle(relay, CHIPS - 1, sems.at[0])
        settle(relay, devices - 1, sems.at[1])


def exchange_last(packed, got, n_row, n_col):
    return pl.pallas_call(
        functools.partial(last_kernel, n_row, n_col),
        out_shape=(
            jax.ShapeDtypeStruct(got.shape, got.dtype),
            jax.ShapeDtypeStruct((2 * CHIPS,) + packed.shape[4:], packed.dtype),
        ),
        in_specs=[HBM, HBM],
        out_specs=(HBM, HBM),
        input_output_aliases={1: 0},
        scratch_shapes=[DMA((3,)), DMA((CHIPS,)), DMA],
        compiler_params=pltpu.CompilerParams(collective_id=3, has_side_effects=True),
        name="exchange_last",
    )(packed, got)[0]


def fetch_target(t, at, total, counts, order, base, got, buffer, sem):
    base[t] = at

    def one(e, c):
        pltpu.make_async_copy(got.at[order[t * total + e]], buffer.at[at + e], sem).start()
        return c

    lax.fori_loop(0, counts[t], one, 0)
    return at + counts[t]


def await_target(t, counts, got, buffer, sem):
    def one(e, c):
        pltpu.make_async_copy(got.at[0], buffer.at[0], sem).wait()
        return c

    lax.fori_loop(0, counts[t], one, 0)


def product(t, e, counts, base, buffer):
    rank = buffer.shape[1] // 2
    n, begin = counts[t], base[t]
    picked = [
        jnp.where(e * STACK + k < n, begin + e * STACK + k, buffer.shape[0] - 1) for k in range(STACK)
    ]
    lefts = jnp.concatenate([buffer[s, 0:rank, :] for s in picked], axis=0)
    rights = jnp.concatenate([buffer[s, rank:, :] for s in picked], axis=0)
    return dot(lefts, rights, ((0,), (0,)))


def add_rest(t, counts, base, buffer, sum_ref, rows, cols):
    def chunk(e, c):
        sum_ref[rows, cols] += product(t, e, counts, base, buffer)
        return c

    lax.fori_loop(1, (counts[t] + STACK - 1) // STACK, chunk, 0)


def split(x):
    high = x.astype(jnp.bfloat16)
    return high, (x - high.astype(jnp.float32)).astype(jnp.bfloat16)


def permutation(pivots):
    size = pivots.shape[1]
    places = lax.broadcasted_iota(jnp.int32, (size, size), 0)
    return (places == pivots).astype(jnp.float32)


def panel_kernel(
    total, table, got, front, pivots, upper_inverse, lower_inverse, column_basis, row_basis,
    column_ranks, row_ranks, a_out, b_out, counts, order, left_sum, top_sum, buffer, top_weights,
    left_weights, coupling, base, sem, front_sem,
):
    size, rank = upper_inverse.shape[0], column_basis.shape[0]
    row_blocks, col_blocks = front.shape[0] // size, front.shape[1] // size
    targets = row_blocks * col_blocks
    devices = table.shape[0]
    is_top, is_left = lax.axis_index("row") == 0, lax.axis_index("col") == 0
    load_left = pltpu.make_async_copy(front.at[:, pl.ds(0, size)], left_sum, front_sem.at[0])
    load_top = pltpu.make_async_copy(front.at[pl.ds(0, size)], top_sum, front_sem.at[1])
    pl.when(is_left)(load_left.start)
    pl.when(is_top)(load_top.start)

    for t in range(targets + 1):
        counts[t] = 0

    def note(s, p, at):
        t = table[s, 0, p]
        t = jnp.where(t < 0, targets, t)
        n = counts[t]
        order[t * total + n] = at
        counts[t] = n + 1

    core = lax.rem(lax.axis_index("col"), 2)
    wx, wy, wz = 2 + core * 30, 8 - core * 6, 32 - core * 24

    def tally(r, flags):
        x, low = r // 2, lax.rem(r, 2)
        for q in range(devices // 8):
            s = r * (devices // 8) + q
            y, z, c = q // 4, (q // 2) % 2 * 2 + low, q % 2
            note(s, 0, x * wx + y * wy + z * wz + c)
            note(s, 1, devices + c * CHIPS + y * 16 + x * 4 + z)
            flags = jnp.maximum(flags, table[s, 0, 3])
        return flags

    def tally_last(s, c):
        note(s, 2, 2 * devices + s)
        return c

    flags = lax.fori_loop(0, 8, tally, -1)
    lax.fori_loop(0, jnp.where(flags >= 0, devices, 0), tally_last, 0)

    @pl.when(jnp.logical_or(is_top, is_left))
    def _():
        buffer[buffer.shape[0] - 1] = jnp.zeros(buffer.shape[1:], buffer.dtype)

        def fetch(t, at):
            return fetch_target(t, at, total, counts, order, base, got, buffer, sem)

        def fetch_left(i, at):
            return fetch(i * col_blocks, at)

        at = lax.fori_loop(0, jnp.where(is_left, row_blocks, 0), fetch_left, 0)
        lax.fori_loop(jnp.where(is_left, 1, 0), jnp.where(is_top, col_blocks, 0), fetch, at)

    @pl.when(is_top)
    def _():
        weights = dot(row_basis[...], lower_inverse[...], precision=HIGHEST)
        weights = dot(weights, permutation(pivots[...]), ((1,), (1,)), precision=HIGHEST)
        top_weights[0:rank] = weights
        top_weights[rank:] = weights

    @pl.when(is_left)
    def _():
        left_weights[...] = dot(
            upper_inverse[...], column_basis[...], ((1,), (1,)), precision=HIGHEST
        )
        coupled = dot(column_basis[...], row_basis[...], ((1,), (1,)), precision=HIGHEST)
        coupling[...] = jnp.concatenate([coupled, coupled], axis=1)

    @pl.when(jnp.logical_or(is_top, is_left))
    def _():
        def ready(t):
            await_target(t, counts, got, buffer, sem)

        def ready_left(i, c):
            ready(i * col_blocks)
            return c

        def ready_top(t, c):
            ready(t)
            return c

        lax.fori_loop(0, jnp.where(is_left, row_blocks, 0), ready_left, 0)
        lax.fori_loop(jnp.where(is_left, 1, 0), jnp.where(is_top, col_blocks, 0), ready_top, 0)

    @pl.when(is_top)
    def _():
        row = lax.broadcasted_iota(jnp.int32, (2 * rank, size), 0)
        load_top.wait()
        for j in range(col_blocks):
            cols = slice(j * size, (j + 1) * size)
            top_sum[:, cols] += product(j, 0, counts, base, buffer)
        for j in range(col_blocks):
            add_rest(j, counts, base, buffer, top_sum, slice(0, size), slice(j * size, (j + 1) * size))
        for j in range(col_blocks):
            cols = slice(j * size, (j + 1) * size)
            factor = dot(top_weights[...], top_sum[:, cols], precision=HIGHEST)
            factor = jnp.where(lax.rem(row, rank) < row_ranks[j], factor, 0.0)
            high, low = split(factor)
            value = jnp.where(row < rank, high.astype(jnp.float32), low.astype(jnp.float32))
            for h in range(size // 128):
                b_out[j * (size // 128) + h] = value[:, h * 128 : (h + 1) * 128].astype(jnp.bfloat16)

    @pl.when(is_left)
    def _():
        lane = lax.broadcasted_iota(jnp.int32, (size, 2 * rank), 1)
        load_left.wait()

        def add(i, c):
            rows = pl.ds(pl.multiple_of(i * size, size), size)
            left_sum[rows, :] += product(i * col_blocks, 0, counts, base, buffer)
            return c

        lax.fori_loop(0, row_blocks, add, 0, unroll=4)

        def add_more(i, c):
            rows = pl.ds(pl.multiple_of(i * size, size), size)
            add_rest(i * col_blocks, counts, base, buffer, left_sum, rows, slice(0, size))
            return c

        lax.fori_loop(0, row_blocks, add_more, 0)

        def block(i, c):
            rows = pl.ds(pl.multiple_of(i * size, size), size)
            factor = dot(left_sum[rows, :], left_weights[...], precision=HIGHEST)
            factor = jnp.where(lane[:, 0:rank] < column_ranks[i], factor, 0.0)
            high, low = split(dot(factor, coupling[...], precision=HIGHEST))
            value = jnp.where(lane < rank, high.astype(jnp.float32), low.astype(jnp.float32))
            for h in range(size // 128):
                a_out[i * (size // 128) + h] = value[h * 128 : (h + 1) * 128].astype(jnp.bfloat16)
            return c

        lax.fori_loop(0, row_blocks, block, 0, unroll=4)


def panel(
    table, got, front, pivots, upper_inverse, lower_inverse, column_basis, row_basis, column_ranks,
    row_ranks,
):
    depth, size = got.shape[1:]
    total = table.shape[0] * CAP
    rows, cols = front.shape
    targets = (rows // size) * (cols // size)
    return pl.pallas_call(
        functools.partial(panel_kernel, total),
        out_shape=(
            jax.ShapeDtypeStruct((rows // 128, 128, 128), jnp.bfloat16),
            jax.ShapeDtypeStruct((cols // 128, 128, 128), jnp.bfloat16),
            jax.ShapeDtypeStruct((targets + 1,), jnp.int32),
            jax.ShapeDtypeStruct(((targets + 2) * total,), jnp.int32),
        ),
        in_specs=[SMEM, HBM, HBM, VMEM, VMEM, VMEM, VMEM, VMEM, SMEM, SMEM],
        out_specs=(VMEM, VMEM, SMEM, SMEM),
        scratch_shapes=[
            pltpu.VMEM((rows, size), jnp.float32),
            pltpu.VMEM((size, cols), jnp.float32),
            pltpu.VMEM((total + 1, depth, size), jnp.bfloat16),
            pltpu.VMEM((depth, size), jnp.float32),
            pltpu.VMEM((size, depth // 2), jnp.float32),
            pltpu.VMEM((depth // 2, depth), jnp.float32),
            pltpu.SMEM((targets,), jnp.int32),
            DMA,
            DMA((2,)),
        ],
        compiler_params=pltpu.CompilerParams(vmem_limit_bytes=LIMIT),
        name="panel",
    )(
        table, got, front, pivots, upper_inverse, lower_inverse, column_basis, row_basis,
        column_ranks, row_ranks,
    )


def spread_kernel(
    n_row, n_col, a_src, b_src, a_all, b_all, a_part_send, a_part_recv, b_part_send, b_part_recv,
    a_send, a_recv, b_send, b_recv, swap_sem, own_sem,
):
    r, c = lax.axis_index("row"), lax.axis_index("col")
    half = n_col // 2
    chip, core = c // 2, lax.rem(c, 2)
    sibling = (r, chip * 2 + 1 - core)
    barrier = pltpu.get_barrier_semaphore()

    def mates(n, me, body):
        def one(k, carry):
            body(lax.rem(me + k, n))
            return carry

        lax.fori_loop(1, n, one, 0)

    mates(n_col, c, lambda o: pl.semaphore_signal(barrier, 1, device_id=(r, o), device_id_type=MESH))
    mates(n_row, r, lambda o: pl.semaphore_signal(barrier, 1, device_id=(o, c), device_id_type=MESH))
    pl.semaphore_wait(barrier, n_col + n_row - 2)

    def piece(o):
        return lax.rem(o, 2) * half + o // 2

    def a_part(o):
        return remote(a_src.at[piece(o)], a_all.at[piece(o)], a_part_send.at[o], a_part_recv, (r, o))

    def b_part(o):
        return remote(b_src.at[o], b_all.at[o], b_part_send.at[o], b_part_recv, (o, c))

    def a_full(h):
        at = piece(c)
        return remote(a_all.at[at], a_all.at[at], a_send.at[h], a_recv.at[chip], (r, h * 2 + core))

    def a_from(h):
        at = core * half + h
        return remote(a_all.at[at], a_all.at[at], a_send.at[h], a_recv.at[h], (r, h * 2 + core))

    def b_full(o):
        return remote(b_all.at[r], b_all.at[r], b_send.at[o], b_recv.at[r], (o, c))

    def b_from(o):
        return remote(b_all.at[o], b_all.at[o], b_send.at[o], b_recv.at[o], (o, c))

    def swap(side):
        part = a_all.at[pl.ds(side * half, half)]
        return remote(part, part, swap_sem.at[0], swap_sem.at[1], sibling)

    @pl.when(c == 0)
    def _():
        mates(n_col, c, lambda o: a_part(o).start())
        own = pltpu.make_async_copy(a_src.at[0], a_all.at[0], own_sem.at[0])
        own.start()
        own.wait()

    @pl.when(r == 0)
    def _():
        mates(n_row, r, lambda o: b_part(o).start())
        own = pltpu.make_async_copy(b_src.at[0], b_all.at[0], own_sem.at[1])
        own.start()
        own.wait()

    @pl.when(c != 0)
    def _():
        a_part(c).wait_recv()

    mates(half, chip, lambda h: a_full(h).start())

    @pl.when(r != 0)
    def _():
        b_part(r).wait_recv()

    mates(n_row, r, lambda o: b_full(o).start())
    mates(half, chip, lambda h: a_from(h).wait_recv())
    swap(core).start()
    mates(n_row, r, lambda o: b_from(o).wait_recv())
    swap(1 - core).wait_recv()
    mates(half, chip, lambda h: a_full(h).wait_send())
    mates(n_row, r, lambda o: b_full(o).wait_send())
    swap(core).wait_send()

    @pl.when(c == 0)
    def _():
        mates(n_col, c, lambda o: a_part(o).wait_send())

    @pl.when(r == 0)
    def _():
        mates(n_row, r, lambda o: b_part(o).wait_send())


def spread(a_src, b_src, n_row, n_col):
    return pl.pallas_call(
        functools.partial(spread_kernel, n_row, n_col),
        out_shape=(
            jax.ShapeDtypeStruct(a_src.shape, a_src.dtype),
            jax.ShapeDtypeStruct(b_src.shape, b_src.dtype),
        ),
        in_specs=[VMEM, VMEM],
        out_specs=(VMEM, VMEM),
        scratch_shapes=[
            DMA((n_col,)), DMA, DMA((n_row,)), DMA,
            DMA((n_col // 2,)), DMA((n_col // 2,)), DMA((n_row,)), DMA((n_row,)), DMA((2,)), DMA((2,)),
        ],
        compiler_params=pltpu.CompilerParams(collective_id=1, has_side_effects=True),
        name="spread",
    )(a_src, b_src)


def finish_kernel(
    total, counts, order, got, front, a_all, b_all, pivots, upper_inverse, lower_inverse, out,
    extended, buffer, b_cat, inverse_parts, corner, base, sem, front_sem, out_sem,
):
    size = upper_inverse.shape[0]
    row_blocks, col_blocks = front.shape[0] // size, front.shape[1] // size
    lanes = a_all.shape[2]
    rank = lanes // 2
    pieces = size // lanes
    is_top, is_left = lax.axis_index("row") == 0, lax.axis_index("col") == 0

    def rows(i):
        return pl.ds(pl.multiple_of(i * size, size), size)

    def load(i):
        return pltpu.make_async_copy(front.at[rows(i)], extended.at[rows(i)], front_sem.at[i])

    def store(i):
        return pltpu.make_async_copy(extended.at[rows(i)], out.at[rows(i)], out_sem.at[i])

    load(0).start()

    def fetch(i, at):
        for j in range(col_blocks):
            at = fetch_target(
                i * col_blocks + j, at, total, counts, order, base, got, buffer, sem.at[i]
            )
        pl.when(i + 1 < row_blocks)(lambda: load(i + 1).start())
        return at

    lax.fori_loop(0, row_blocks, fetch, 0)
    buffer[buffer.shape[0] - 1] = jnp.zeros(buffer.shape[1:], buffer.dtype)

    @pl.when(is_left)
    def _():
        high, low = split(upper_inverse[...])
        inverse_parts[0:size] = high
        inverse_parts[size : 2 * size] = low
        inverse_parts[2 * size :] = high

    for k in range(b_all.shape[0]):
        cols = slice(k * lanes, (k + 1) * lanes)
        high, low = b_all[k, 0:rank, :], b_all[k, rank:, :]
        if k < pieces:
            high = jnp.where(is_left, jnp.zeros_like(high), high)
            low = jnp.where(is_left, jnp.zeros_like(low), low)
        for h in range(2):
            b_cat[h * rank : (h + 1) * rank, cols] = high
            b_cat[(2 + h) * rank : (3 + h) * rank, cols] = low

    def step(i, c):
        load(i).wait()
        for j in range(col_blocks):
            await_target(i * col_blocks + j, counts, got, buffer, sem.at[i])
        a = jnp.concatenate([a_all[i * pieces + k] for k in range(pieces)], axis=0)
        a = jnp.concatenate([a, a], axis=1)
        a = jnp.where(jnp.logical_and(is_top, i == 0), jnp.zeros_like(a), a)
        for j in range(col_blocks):
            cols = slice(j * size, (j + 1) * size)
            added = product(i * col_blocks + j, 0, counts, base, buffer)
            extended[rows(i), cols] += added - dot(a, b_cat[:, cols])
        for j in range(col_blocks):
            cols = slice(j * size, (j + 1) * size)
            add_rest(i * col_blocks + j, counts, base, buffer, extended, rows(i), cols)

        @pl.when(jnp.logical_and(is_left, jnp.logical_not(jnp.logical_and(is_top, i == 0))))
        def _():
            high, low = split(extended[rows(i), 0:size])
            extended[rows(i), 0:size] = dot(
                jnp.concatenate([high, high, low], axis=1), inverse_parts[...]
            )

        @pl.when(jnp.logical_and(is_top, i == 0))
        def _():
            permute = permutation(pivots[...])
            corner[...] = dot(permute, extended[0:size, 0:size], ((0,), (0,)), precision=HIGHEST)
            weights = dot(lower_inverse[...], permute, ((1,), (1,)), precision=HIGHEST)
            for j in range(col_blocks):
                cols = slice(j * size, (j + 1) * size)
                upper = dot(weights, extended[0:size, cols], precision=HIGHEST)
                if j == 0:
                    upper = jnp.where(is_left, corner[...], upper)
                extended[0:size, cols] = upper

        store(i).start()
        return c

    lax.fori_loop(0, row_blocks, step, 0)
    for i in range(row_blocks):
        store(i).wait()


def finish(counts, order, got, front, a_all, b_all, pivots, upper_inverse, lower_inverse, total):
    depth, size = got.shape[1:]
    rows, cols = front.shape
    row_blocks = rows // size
    targets = row_blocks * (cols // size)
    return pl.pallas_call(
        functools.partial(finish_kernel, total),
        out_shape=jax.ShapeDtypeStruct(front.shape, jnp.float32),
        in_specs=[SMEM, SMEM, HBM, HBM, VMEM, VMEM, VMEM, VMEM, VMEM],
        out_specs=HBM,
        scratch_shapes=[
            pltpu.VMEM(front.shape, jnp.float32),
            pltpu.VMEM((total + 1, depth, size), jnp.bfloat16),
            pltpu.VMEM((2 * depth, cols), jnp.bfloat16),
            pltpu.VMEM((3 * size, size), jnp.bfloat16),
            pltpu.VMEM((size, size), jnp.float32),
            pltpu.SMEM((targets,), jnp.int32),
            DMA((row_blocks,)), DMA((row_blocks,)), DMA((row_blocks,)),
        ],
        compiler_params=pltpu.CompilerParams(vmem_limit_bytes=LIMIT),
        name="finish",
    )(counts, order, got, front, a_all, b_all, pivots, upper_inverse, lower_inverse)


def shards(
    front, child_left, child_right, child_owner, child_slot, pivots, upper_inverse, lower_inverse,
    column_basis, row_basis, column_ranks, row_ranks,
):
    n_row, n_col = lax.axis_size("row"), lax.axis_size("col")
    devices = n_row * n_col
    packed, table = pack(
        child_owner[:, 0], child_slot, jnp.swapaxes(child_left, 1, 2), child_right, devices
    )
    packed = packed.reshape((4, RING, RING, RING) + packed.shape[1:])
    got, got_table = exchange(packed, table, n_row, n_col)
    rounds = (jnp.max(got_table[:, 0, 3]) >= 0).astype(jnp.int32)
    got = lax.fori_loop(0, rounds, lambda i, g: exchange_last(packed, g, n_row, n_col), got)
    got = got.reshape((3 * devices,) + got.shape[3:])
    a_src, b_src, counts, order = panel(
        got_table, got, front, pivots[None, :], upper_inverse, lower_inverse, column_basis.T,
        row_basis.T, column_ranks, row_ranks,
    )
    a_all, b_all = spread(a_src, b_src, n_row, n_col)
    return finish(
        counts, order, got, front, a_all, b_all, pivots[None, :], upper_inverse, lower_inverse,
        devices * CAP,
    )


def solution(mesh):
    in_specs = (
        P("row", "col"),
        P(("row", "col"), None, None),
        P(("row", "col"), None, None),
        P(("row", "col"), None),
        P(("row", "col")),
        P(),
        P(),
        P(),
        P(),
        P(),
        P("row"),
        P("col"),
    )
    out_specs = P("row", "col")
    return jax.shard_map(shards, mesh=mesh, in_specs=in_specs, out_specs=out_specs, check_vma=False)
```

```python
import functools

import jax
import jax.numpy as jnp
from jax import lax
from jax.experimental import pallas as pl
from jax.experimental.pallas import tpu as pltpu
from jax.sharding import PartitionSpec as P

MESH = pl.DeviceIdType.MESH
HBM = pl.BlockSpec(memory_space=pl.ANY)
SMEM = pl.BlockSpec(memory_space=pltpu.SMEM)
VMEM = pl.BlockSpec(memory_space=pltpu.VMEM)
DMA = pltpu.SemaphoreType.DMA
CAP = 2
STACK = 4
STRIDE = 37
RING = 4
CHIPS = RING**3
LEAD = 16
LIMIT = 56 * 1024 * 1024
HIGHEST = lax.Precision.HIGHEST


def dot(a, b, dims=((1,), (0,)), precision=None):
    return lax.dot_general(
        a, b, (dims, ((), ())), precision=precision, preferred_element_type=jnp.float32
    )


def pack_kernel(
    devices, owner, owner_row, slot_row, left, right, packed, table, staged, named, placed, in_sem,
    out_sem,
):
    count, rank = left.shape[0], left.shape[1]
    chips = devices // 2
    chunks = in_sem.shape[0]
    each = count // chunks

    def load(k):
        part = pl.ds(k * each, each)
        return (
            pltpu.make_async_copy(left.at[part], staged.at[part, pl.ds(0, rank)], in_sem.at[k, 0]),
            pltpu.make_async_copy(right.at[part], staged.at[part, pl.ds(rank, rank)], in_sem.at[k, 1]),
        )

    for k in range(chunks):
        for copy in load(k):
            copy.start()

    def clear(o, c):
        named[o] = 0
        placed[o] = 0
        return c

    lax.fori_loop(0, devices, clear, 0, unroll=8)

    def tally(i, c):
        named[owner[i]] += 1
        return c

    lax.fori_loop(0, count, tally, 0, unroll=4)

    shape = (devices, 1, count)
    place = lax.broadcasted_iota(jnp.int32, shape, 2)
    line = lax.broadcasted_iota(jnp.int32, shape, 0)
    core = line >> 6
    high, middle, low = (line >> 4) & 3, (line >> 2) & 3, line & 3
    x, y, z = (jnp.where(core == 0, a, b) for a, b in ((high, low), (middle, high), (low, middle)))
    device = x * 32 + (z & 1) * 16 + y * 4 + (z & 2) + core
    owners = owner_row[...][None]
    code = (place * 64 + slot_row[...][None]).astype(jnp.float32)

    def ends(which):
        least = jnp.min(jnp.where(which, code, 65536.0), axis=2, keepdims=True)
        most = jnp.max(jnp.where(which, code, -1.0), axis=2, keepdims=True)
        return least, most

    least, most = ends(owners == device)
    low_least, low_most = ends(owners == device - (device & 1))
    core = core[:, :, 0:1]
    first = jnp.where(most >= 0.0, least.astype(jnp.int32) & 63, -1)
    second = jnp.where(most > least, most.astype(jnp.int32) & 63, -1)
    late = jnp.logical_and(core == 1, low_most > low_least)
    last = jnp.where(late, second, -1)
    flag = jnp.max(last.astype(jnp.float32), axis=0, keepdims=True).astype(jnp.int32)
    lane = lax.broadcasted_iota(jnp.int32, table.shape, 2)
    line = jnp.where(lane == 0, first, jnp.where(lane == 1, jnp.where(late, -1, second), -1))
    table[...] = jnp.where(lane == 2, last, jnp.where(lane == 3, flag, line))

    for k in range(chunks):
        for copy in load(k):
            copy.wait()

        def send(i, c):
            o = owner[i]
            p = placed[o]
            placed[o] = 1
            core = o & 1
            x, y, z = o >> 5, (o >> 2) & 3, (o & 2) | ((o >> 4) & 1)
            late = jnp.logical_and(core == 1, named[o - core] == 2)
            first = jnp.where(core == 0, x * 16 + y * 4 + z, chips + y * 16 + z * 4 + x)
            second = 2 * chips + z * 16 + x * 4 + y
            extra = jnp.where(late, 3 * chips + (o >> 1), second)
            at = jnp.where(p == 0, first, extra)
            pltpu.make_async_copy(staged.at[i], packed.at[at], out_sem).start()
            return c

        lax.fori_loop(k * each, (k + 1) * each, send, 0)
    pltpu.make_async_copy(staged, packed.at[pl.ds(0, count)], out_sem).wait()


def pack(owner, slots, left, right, devices):
    count, rank, size = left.shape
    return pl.pallas_call(
        functools.partial(pack_kernel, devices),
        out_shape=(
            jax.ShapeDtypeStruct((2 * devices, 2 * rank, size), left.dtype),
            jax.ShapeDtypeStruct((devices, 1, 128), jnp.int32),
        ),
        in_specs=[SMEM, VMEM, VMEM, HBM, HBM],
        out_specs=(HBM, VMEM),
        scratch_shapes=[
            pltpu.VMEM((count, 2 * rank, size), left.dtype),
            pltpu.SMEM((devices,), jnp.int32),
            pltpu.SMEM((devices,), jnp.int32),
            DMA((4, 2)),
            DMA,
        ],
        compiler_params=pltpu.CompilerParams(vmem_limit_bytes=LIMIT),
        name="pack",
    )(owner, owner[None, :], slots[None, :], left, right)


def position():
    r, q = lax.axis_index("row"), lax.axis_index("col")
    return r // 2, q // 4, lax.rem(q // 2, 2) * 2 + lax.rem(r, 2), lax.rem(q, 2)


def place_of(x, y, z, core):
    x, y, z = lax.rem(x, RING), lax.rem(y, RING), lax.rem(z, RING)
    return x * 2 + lax.rem(z, 2), y * 4 + (z // 2) * 2 + core


def step_of(k):
    d = lax.rem(k * STRIDE, CHIPS)
    steps = (d // (RING * RING), lax.rem(d // RING, RING), lax.rem(d, RING))
    far = [s // 2 - s // 3 for s in steps]
    both = far[0] + far[1] + far[2] > 0
    up = 1 - lax.rem(steps[0] + steps[1] + steps[2], 2)
    return d, steps, far, both, up


def legs(steps, far, up):
    ahead = [f * (3 - 2 * up) for f in far]
    return ahead, [s + 4 - a for s, a in zip(steps, ahead)]


def far_count():
    return sum(2 in (d // 16, d // 4 % 4, d % 4) for d in range(1, CHIPS))


def remote(src, dst, send, recv, device):
    return pltpu.make_async_remote_copy(
        src_ref=src, dst_ref=dst, send_sem=send, recv_sem=recv, device_id=device,
        device_id_type=MESH,
    )


class Together:
    def __init__(self, *rings):
        self.rings = rings

    def __getattr__(self, name):
        def each():
            for ring in self.rings:
                getattr(ring, name)()

        return each


class Ring:
    def __init__(self, at, go, source, target, relay, send_sem, recv_sem, origin=0):
        self.at, self.go, self.source, self.target = at, go, source, target
        self.relay, self.send_sem, self.recv_sem, self.origin = relay, send_sem, recv_sem, origin

    def copy(self, src, dst, i, way):
        return remote(src, dst, self.send_sem.at[i], self.recv_sem.at[i], self.go(1 if way == 0 else 3))

    def by(self, d):
        return lax.rem(self.at + d, RING)

    def begin(self):
        for way in range(2):
            self.copy(self.source(self.by(2), way), self.relay(way), 4 + way, way).start()
        for way, d in ((0, 1), (1, 3)):
            self.copy(self.source(self.by(d), None), self.target(self.at, None), way, way).start()

    def begin_sent(self):
        for way in range(2):
            self.copy(self.source(self.by(2), way), self.relay(way), 4 + way, way).wait_send()
        for way, d in ((0, 1), (1, 3)):
            self.copy(self.source(self.by(d), None), self.target(self.at, None), way, way).wait_send()

    def forward(self):
        for way, d in ((0, 3), (1, 1)):
            held = self.relay(way)
            self.copy(held, held, 4 + way, way).wait_recv()
            self.copy(held, self.target(self.by(d), way), 2 + way, way).start()

    def forward_sent(self):
        for way, d in ((0, 3), (1, 1)):
            self.copy(self.relay(way), self.target(self.by(d), way), 2 + way, way).wait_send()

    def arrived(self):
        for way, d in ((0, 3), (1, 1)):
            part = self.target(self.by(d), None)
            self.copy(part, part, way, way).wait_recv()
        for way in range(2):
            part = self.target(self.by(2), way)
            self.copy(part, part, 2 + way, way).wait_recv()


def exchange_kernel(
    n_col, packed, table, got, got_table, a_one, a_two, t_one, t_two, a_relay_one,
    a_relay_two, a_relay_three, t_relay_one, t_relay_two, t_relay_three, l_one, l_two, l_relay_one,
    l_relay_two, l_relay_three, a_stage_one, a_stage_two, a_stage_three, t_stage, t_last, send_sems,
    recv_sems, hand_sems, own_sems,
):
    x, y, z, core = position()
    here = (x, y, z)
    sibling = place_of(x, y, z, 1 - core)
    barrier = pltpu.get_barrier_semaphore()

    def greet(at):
        pl.semaphore_signal(barrier, 1, device_id=at, device_id_type=MESH)

    greet(sibling)
    for axis in range(3):
        for d in (1, 3):
            for side in range(2):
                greet(place_of(*[here[i] + (d if i == axis else 0) for i in range(3)], side))
    pl.semaphore_wait(barrier, 13)

    def along(axis, to_core):
        def go(d):
            return place_of(*[here[i] + (d if i == axis else 0) for i in range(3)], to_core)

        return here[axis], go

    def along_mine(phase):
        axes = [lax.rem(phase + core, 3) == i for i in range(3)]
        picked = [axes[i].astype(jnp.int32) for i in range(3)]
        at = sum(p * h for p, h in zip(picked, here))
        return at, lambda d: place_of(*[h + d * p for p, h in zip(picked, here)], core)

    def half(ref_at, width):
        return lambda i, h: ref_at(i, pl.ds(0, 2 * width) if h is None else pl.ds(h * width, width))

    arrays = (
        (packed, got, a_one, a_two, a_relay_one, a_relay_two, a_relay_three, 0, 0),
        (table, got_table, l_one, l_two, l_relay_one, l_relay_two, l_relay_three, 9, 7),
    )

    def first_ring(kind, which):
        src, end, one, two, relay, relay_two, relay_three, sent, received = arrays[which]
        at, go = along(kind, kind)
        return Ring(
            at, go, half(lambda j, s: src.at[kind, j, s], 2),
            half(lambda i, s: one.at[i * 2 + core, s], 2), lambda way: relay.at[way, core],
            send_sems.at[sent + kind], recv_sems.at[received + core],
        )

    def first_rings(kind):
        return Together(first_ring(kind, 1), first_ring(kind, 0))

    def first_mine(origin):
        at, go = along_mine(0)

        def ring(src, end, one, two, relay, relay_two, relay_three, sent, received):
            return Ring(
                at, go, None, half(lambda i, s: one.at[i * 2 + origin, s], 2),
                lambda way: relay.at[way, origin], send_sems.at[sent + 2 + origin],
                recv_sems.at[received + origin],
            )

        return Together(ring(*arrays[1]), ring(*arrays[0]))

    def second_ring(which):
        src, end, one, two, relay, relay_two, relay_three, sent, received = arrays[which]
        return Ring(
            *along_mine(1), half(lambda j, s: one.at[s, j], 4), half(lambda i, s: two.at[i, s], 4),
            lambda way: relay_two.at[way], send_sems.at[sent + 4], recv_sems.at[received + 2],
        )

    def third_ring(which):
        src, end, one, two, relay, relay_two, relay_three, sent, received = arrays[which]
        return Ring(
            *along_mine(2), half(lambda j, s: two.at[s, slice(None), j], 2),
            half(lambda i, s: end.at[i, s], 2), lambda way: relay_three.at[way],
            send_sems.at[sent + 5], recv_sems.at[received + 3],
        )

    a_second, a_third = Together(second_ring(1), second_ring(0)), Together(third_ring(1), third_ring(0))
    t_first = Ring(
        *along(2, core), half(lambda j, s: packed.at[2, j, s], 2), half(lambda i, s: t_one.at[i, s], 2),
        lambda way: t_relay_one.at[way], send_sems.at[6], recv_sems.at[4],
    )

    def t_two_part(i, h):
        begin = lax.rem(i, 2) * 4
        part = pl.ds(begin, 4) if h is None else pl.ds(begin + 2 * h, 2)
        return t_two.at[i // 2, part]

    t_second = Ring(
        *along(0, core), half(lambda j, s: t_one.at[s, j], 2), t_two_part,
        lambda way: t_relay_two.at[way], send_sems.at[7], recv_sems.at[5],
    )

    def t_got(side):
        def part(i, h):
            begin = lax.rem(i, 2) * 2
            rows = pl.ds(begin, 2) if h is None else pl.ds(begin + h, 1)
            return got.at[4 + side * 2 + i // 2, rows]

        return part

    t_third = Ring(
        *along(1, core), half(lambda j, s: t_two.at[s, slice(None), j], 1), t_got(core),
        lambda way: t_relay_three.at[way], send_sems.at[8], recv_sems.at[6],
    )

    class Keep:
        def __init__(self, src, stage, dst, i):
            self.load = pltpu.make_async_copy(src, stage, own_sems.at[i])
            self.store = pltpu.make_async_copy(stage, dst, own_sems.at[i])

        def run(self):
            self.load.wait()
            self.store.start()

    def keep(ring, stage, i):
        return Keep(ring.source(ring.at, None), stage, ring.target(ring.at, None), i)

    def keep_line(ring):
        return pltpu.make_async_copy(
            ring.source(ring.at, None), ring.target(ring.at, None), own_sems.at[6]
        )

    def to_sibling(kind, which):
        ring = first_ring(kind, which)
        return remote(
            ring.source(ring.at, None), ring.target(ring.at, None), hand_sems.at[0, 4 + which],
            hand_sems.at[1, 4 + which], sibling,
        )

    first_rings(0).begin()
    first_rings(1).begin()
    t_first.begin()
    for kind in range(2):

        @pl.when(core == kind)
        def _():
            keep_line(first_ring(kind, 1)).start()
            keep(first_ring(kind, 0), a_stage_one, 0).load.start()

        @pl.when(core != kind)
        def _():
            to_sibling(kind, 1).start()
            to_sibling(kind, 0).start()

    t_keep = keep(t_first, t_stage.at[0], 1)
    t_keep.load.start()
    for kind in range(2):

        @pl.when(core == kind)
        def _():
            keep(first_ring(kind, 0), a_stage_one, 0).run()

    t_keep.run()
    for origin in range(2):
        first_mine(origin).forward()
    t_first.forward()
    for origin in range(2):
        first_mine(origin).arrived()
    for kind in range(2):

        @pl.when(core == kind)
        def _():
            keep(first_ring(kind, 0), a_stage_one, 0).store.wait()
            keep_line(first_ring(kind, 1)).wait()
            to_sibling(kind, 1).wait_recv()
            to_sibling(kind, 0).wait_recv()

        @pl.when(core != kind)
        def _():
            to_sibling(kind, 1).wait_send()
            to_sibling(kind, 0).wait_send()

    a_second.begin()
    a_keep, line_keep = keep(second_ring(0), a_stage_two, 2), keep_line(second_ring(1))
    a_keep.load.start()
    line_keep.start()
    t_first.arrived()
    t_keep.store.wait()
    t_second.begin()
    t_keep = keep(t_second, t_stage.at[1], 3)
    t_keep.load.start()
    a_keep.run()
    t_keep.run()
    a_second.forward()
    t_second.forward()
    a_second.arrived()
    a_keep.store.wait()
    line_keep.wait()
    a_third.begin()
    a_keep, line_keep = keep(third_ring(0), a_stage_three, 4), keep_line(third_ring(1))
    a_keep.load.start()
    line_keep.start()
    t_second.arrived()
    t_keep.store.wait()
    t_third.begin()
    last = Keep(t_third.source(y, None), t_last, t_third.target(y, None), 5)
    last.load.start()
    a_keep.run()
    last.run()
    t_third.forward()
    a_third.forward()
    last.store.wait()

    def hand(side, d):
        part = t_got(side)(lax.rem(y + d, RING), None)
        return remote(part, part, hand_sems.at[0, d], hand_sems.at[1, d], sibling)

    hand(core, 0).start()
    t_third.arrived()
    for d in range(1, RING):
        hand(core, d).start()
    a_third.arrived()
    a_keep.store.wait()
    line_keep.wait()
    for d in range(RING):
        hand(1 - core, d).wait_recv()
    first_rings(0).begin_sent()
    first_rings(1).begin_sent()
    for origin in range(2):
        first_mine(origin).forward_sent()
    for ring in (t_first, a_second, t_second, a_third, t_third):
        ring.begin_sent()
        ring.forward_sent()
    for d in range(RING):
        hand(core, d).wait_send()


def exchange(packed, table, n_col):
    block, line = packed.shape[4:], table.shape[4:]

    def held(*shape):
        return jax.ShapeDtypeStruct(shape + block, packed.dtype)

    def lines(*shape):
        return jax.ShapeDtypeStruct(shape + line, table.dtype)

    def stage(*shape):
        return pltpu.VMEM(shape + block, packed.dtype)

    out_shape = (
        held(12, 4, 8), lines(4, 4, 8),
        held(8, 4, 4), held(4, 8, 4), held(4, 4, 4), held(2, 8, 4),
        held(2, 2, 2, 4), held(2, 4, 4), held(2, 2, 8), held(2, 2, 4), held(2, 2, 4), held(2, 1, 8),
        lines(8, 4, 4), lines(4, 8, 4), lines(2, 2, 2, 4), lines(2, 4, 4), lines(2, 2, 8),
    )
    return pl.pallas_call(
        functools.partial(exchange_kernel, n_col),
        out_shape=out_shape,
        in_specs=[HBM, HBM],
        out_specs=(HBM,) * len(out_shape),
        scratch_shapes=[
            stage(4, 4), stage(8, 4), stage(4, 8), stage(2, 4, 4), stage(2, 8),
            DMA((15, 6)), DMA((11, 6)), DMA((2, 6)), DMA((7,)),
        ],
        compiler_params=pltpu.CompilerParams(
            collective_id=2, has_side_effects=True, vmem_limit_bytes=LIMIT
        ),
        name="exchange",
    )(packed, table)[:2]


def last_kernel(n_row, n_col, packed, got_in, got, relay, sems, relay_sem, own_sem):
    devices = n_row * n_col
    x, y, z, core = position()
    mine = place_of(x, y, z, core)
    me = mine[0] * n_col + mine[1]
    barrier = pltpu.get_barrier_semaphore()

    def at_step(steps, core):
        return place_of(x + steps[0], y + steps[1], z + steps[2], core)

    def number(device):
        return device[0] * n_col + device[1]

    def greet(at):
        pl.semaphore_signal(barrier, 1, device_id=at, device_id_type=MESH)

    def near(k, carry):
        d, steps, far, both, up = step_of(k)

        @pl.when(jnp.logical_and(core == 1, jnp.logical_not(both)))
        def _():
            greet(at_step(steps, 0))
            greet(at_step(steps, 1))

        return carry

    def relayed(k, carry):
        bits = (k // 8, lax.rem(k // 4, 2), lax.rem(k // 2, 2))
        way = lax.rem(k, 2)

        @pl.when(jnp.logical_and(core == 0, k != 15))
        def _():
            greet(at_step([b * (3 - 2 * way) for b in bits], 0))

        return carry

    lax.fori_loop(1, CHIPS, near, 0)
    lax.fori_loop(2, 16, relayed, 0)

    @pl.when(core == 1)
    def _():
        greet(place_of(x, y, z, 0))
        pl.semaphore_wait(barrier, 26)

    @pl.when(core == 0)
    def _():
        pl.semaphore_wait(barrier, 26 + 13 + 1)

    def block_for(target):
        chip = number(target) // 2
        return packed.at[3, chip // 16, lax.rem(chip // 4, 4), lax.rem(chip, 4)]

    def landing(source):
        return got.at[8 + source // 32, lax.rem(source // 8, 4), lax.rem(source, 8)]

    def first_leg(k, carry):
        d, steps, far, both, up = step_of(k)

        @pl.when(both)
        def _():
            first, second = legs(steps, far, up)
            remote(
                block_for(at_step(steps, 1)), relay.at[d], sems.at[0], relay_sem.at[d],
                at_step(first, core),
            ).start()

        return carry

    def direct(k, carry):
        d, steps, far, both, up = step_of(k)

        @pl.when(jnp.logical_not(both))
        def _():
            target = at_step(steps, 1)
            remote(block_for(target), landing(me), sems.at[0], sems.at[1], target).start()

        return carry

    def second_leg(k, carry):
        d, steps, far, both, up = step_of(k)

        @pl.when(both)
        def _():
            first, second = legs(steps, far, up)
            source = number(at_step([4 - f for f in first], core))
            target = at_step(second, 1)
            held = relay.at[d]
            remote(held, held, sems.at[2], relay_sem.at[d], target).wait_recv()
            remote(held, landing(source), sems.at[2], sems.at[1], target).start()

        return carry

    lax.fori_loop(1, CHIPS, first_leg, 0)
    lax.fori_loop(1, CHIPS, direct, 0)
    lax.fori_loop(1, CHIPS, second_leg, 0)

    def settle(ref, count, sem):
        part = ref.at[pl.ds(0, count)]
        pltpu.make_async_copy(part, part, sem).wait()

    settle(relay, far_count(), sems.at[2])

    @pl.when(core == 0)
    def _():
        to = place_of(x, y, z, 1)
        remote(block_for(to), landing(me), sems.at[0], sems.at[1], to).start()
        settle(relay, CHIPS, sems.at[0])

    @pl.when(core == 1)
    def _():
        own = pltpu.make_async_copy(block_for(mine), landing(me), own_sem)
        own.start()
        own.wait()
        settle(relay, CHIPS - 1, sems.at[0])
        settle(relay, devices - 1, sems.at[1])


def exchange_last(packed, got, n_row, n_col):
    return pl.pallas_call(
        functools.partial(last_kernel, n_row, n_col),
        out_shape=(
            jax.ShapeDtypeStruct(got.shape, got.dtype),
            jax.ShapeDtypeStruct((2 * CHIPS,) + packed.shape[4:], packed.dtype),
        ),
        in_specs=[HBM, HBM],
        out_specs=(HBM, HBM),
        input_output_aliases={1: 0},
        scratch_shapes=[DMA((3,)), DMA((CHIPS,)), DMA],
        compiler_params=pltpu.CompilerParams(collective_id=3, has_side_effects=True),
        name="exchange_last",
    )(packed, got)[0]


def fetch_target(t, at, total, counts, order, base, got, buffer, sem):
    base[t] = at

    def one(e, c):
        pltpu.make_async_copy(got.at[order[t * total + e]], buffer.at[at + e], sem).start()
        return c

    lax.fori_loop(0, counts[t], one, 0)
    return at + counts[t]


def await_target(t, counts, got, buffer, sem):
    def one(e, c):
        pltpu.make_async_copy(got.at[0], buffer.at[0], sem).wait()
        return c

    lax.fori_loop(0, counts[t], one, 0)


def product(t, e, counts, base, buffer):
    rank = buffer.shape[1] // 2
    n, begin = counts[t], base[t]
    picked = [
        jnp.where(e * STACK + k < n, begin + e * STACK + k, buffer.shape[0] - 1) for k in range(STACK)
    ]
    lefts = jnp.concatenate([buffer[s, 0:rank, :] for s in picked], axis=0)
    rights = jnp.concatenate([buffer[s, rank:, :] for s in picked], axis=0)
    return dot(lefts, rights, ((0,), (0,)))


def add_rest(t, counts, base, buffer, sum_ref, rows, cols):
    def chunk(e, c):
        sum_ref[rows, cols] += product(t, e, counts, base, buffer)
        return c

    lax.fori_loop(1, (counts[t] + STACK - 1) // STACK, chunk, 0)


def split(x):
    high = x.astype(jnp.bfloat16)
    return high, (x - high.astype(jnp.float32)).astype(jnp.bfloat16)


def permutation(pivots):
    size = pivots.shape[1]
    places = lax.broadcasted_iota(jnp.int32, (size, size), 0)
    return (places == pivots).astype(jnp.float32)


def panel_kernel(
    total, table, most, got, front, pivots, upper_inverse, lower_inverse, column_basis, row_basis,
    column_ranks, row_ranks, a_out, b_out, counts, order, left_sum, top_sum, buffer, top_weights,
    left_weights, coupling, base, sem, front_sem,
):
    size, rank = upper_inverse.shape[0], column_basis.shape[0]
    row_blocks, col_blocks = front.shape[0] // size, front.shape[1] // size
    targets = row_blocks * col_blocks
    devices = table.shape[0]
    is_top, is_left = lax.axis_index("row") == 0, lax.axis_index("col") == 0
    load_left = pltpu.make_async_copy(front.at[:, pl.ds(0, size)], left_sum, front_sem.at[0])
    load_top = pltpu.make_async_copy(front.at[pl.ds(0, size)], top_sum, front_sem.at[1])
    pl.when(is_left)(load_left.start)
    pl.when(is_top)(load_top.start)

    for t in range(targets + 1):
        counts[t] = 0

    def note(s, p, at):
        t = table[s, 0, p]
        t = jnp.where(t < 0, targets, t)
        n = counts[t]
        order[t * total + n] = at
        counts[t] = n + 1

    core = lax.rem(lax.axis_index("col"), 2)
    w_high, w_middle, w_low = 1 + core * 3, 16 - core * 15, 4 + core * 12

    def digits(k):
        return k // 32, lax.rem(k // 8, 4), lax.rem(k // 2, 4), lax.rem(k, 2)

    def tally(k, c):
        note(k, 0, k)
        return c

    def tally_shared(k, c):
        high, middle, low, side = digits(k)
        note(k, 1, devices + side * CHIPS + high * w_high + middle * w_middle + low * w_low)
        return c

    def tally_last(k, c):
        high, middle, low, side = digits(k)
        x, y, z = (jnp.where(core == 0, a, b) for a, b in ((low, high), (middle, low), (high, middle)))
        note(k, 2, 2 * devices + x * 32 + lax.rem(z, 2) * 16 + y * 4 + (z // 2) * 2 + side)
        return c

    lax.fori_loop(0, devices, tally, 0, unroll=8)
    lax.fori_loop(0, jnp.where(most[1] >= 0, devices, 0), tally_shared, 0)
    lax.fori_loop(0, jnp.where(most[2] >= 0, devices, 0), tally_last, 0)

    @pl.when(jnp.logical_or(is_top, is_left))
    def _():
        buffer[buffer.shape[0] - 1] = jnp.zeros(buffer.shape[1:], buffer.dtype)

        def fetch(t, at):
            return fetch_target(t, at, total, counts, order, base, got, buffer, sem)

        def fetch_left(i, at):
            return fetch(i * col_blocks, at)

        at = lax.fori_loop(0, jnp.where(is_left, row_blocks, 0), fetch_left, 0)
        lax.fori_loop(jnp.where(is_left, 1, 0), jnp.where(is_top, col_blocks, 0), fetch, at)

    @pl.when(is_top)
    def _():
        weights = dot(row_basis[...], lower_inverse[...], precision=HIGHEST)
        weights = dot(weights, permutation(pivots[...]), ((1,), (1,)), precision=HIGHEST)
        top_weights[0:rank] = weights
        top_weights[rank:] = weights

    @pl.when(is_left)
    def _():
        left_weights[...] = dot(
            upper_inverse[...], column_basis[...], ((1,), (1,)), precision=HIGHEST
        )
        coupled = dot(column_basis[...], row_basis[...], ((1,), (1,)), precision=HIGHEST)
        coupling[...] = jnp.concatenate([coupled, coupled], axis=1)

    @pl.when(jnp.logical_or(is_top, is_left))
    def _():
        def ready(t):
            await_target(t, counts, got, buffer, sem)

        def ready_left(i, c):
            ready(i * col_blocks)
            return c

        def ready_top(t, c):
            ready(t)
            return c

        lax.fori_loop(0, jnp.where(is_left, row_blocks, 0), ready_left, 0)
        lax.fori_loop(jnp.where(is_left, 1, 0), jnp.where(is_top, col_blocks, 0), ready_top, 0)

    @pl.when(is_top)
    def _():
        row = lax.broadcasted_iota(jnp.int32, (2 * rank, size), 0)
        load_top.wait()
        for j in range(col_blocks):
            cols = slice(j * size, (j + 1) * size)
            top_sum[:, cols] += product(j, 0, counts, base, buffer)
        for j in range(col_blocks):
            add_rest(j, counts, base, buffer, top_sum, slice(0, size), slice(j * size, (j + 1) * size))
        for j in range(col_blocks):
            cols = slice(j * size, (j + 1) * size)
            factor = dot(top_weights[...], top_sum[:, cols], precision=HIGHEST)
            factor = jnp.where(lax.rem(row, rank) < row_ranks[j], factor, 0.0)
            high, low = split(factor)
            value = jnp.where(row < rank, high.astype(jnp.float32), low.astype(jnp.float32))
            for h in range(size // 128):
                b_out[j * (size // 128) + h] = value[:, h * 128 : (h + 1) * 128].astype(jnp.bfloat16)

    @pl.when(is_left)
    def _():
        lane = lax.broadcasted_iota(jnp.int32, (size, 2 * rank), 1)
        load_left.wait()

        def add(i, c):
            rows = pl.ds(pl.multiple_of(i * size, size), size)
            left_sum[rows, :] += product(i * col_blocks, 0, counts, base, buffer)
            return c

        lax.fori_loop(0, row_blocks, add, 0, unroll=4)

        def add_more(i, c):
            rows = pl.ds(pl.multiple_of(i * size, size), size)
            add_rest(i * col_blocks, counts, base, buffer, left_sum, rows, slice(0, size))
            return c

        lax.fori_loop(0, row_blocks, add_more, 0)

        def block(i, c):
            rows = pl.ds(pl.multiple_of(i * size, size), size)
            factor = dot(left_sum[rows, :], left_weights[...], precision=HIGHEST)
            factor = jnp.where(lane[:, 0:rank] < column_ranks[i], factor, 0.0)
            high, low = split(dot(factor, coupling[...], precision=HIGHEST))
            value = jnp.where(lane < rank, high.astype(jnp.float32), low.astype(jnp.float32))
            for h in range(size // 128):
                a_out[i * (size // 128) + h] = value[h * 128 : (h + 1) * 128].astype(jnp.bfloat16)
            return c

        lax.fori_loop(0, row_blocks, block, 0, unroll=4)


def panel(
    table, most, got, front, pivots, upper_inverse, lower_inverse, column_basis, row_basis, column_ranks,
    row_ranks,
):
    depth, size = got.shape[1:]
    total = table.shape[0] * CAP
    rows, cols = front.shape
    targets = (rows // size) * (cols // size)
    return pl.pallas_call(
        functools.partial(panel_kernel, total),
        out_shape=(
            jax.ShapeDtypeStruct((rows // 128, 128, 128), jnp.bfloat16),
            jax.ShapeDtypeStruct((cols // 128, 128, 128), jnp.bfloat16),
            jax.ShapeDtypeStruct((targets + 1,), jnp.int32),
            jax.ShapeDtypeStruct(((targets + 2) * total,), jnp.int32),
        ),
        in_specs=[SMEM, SMEM, HBM, HBM, VMEM, VMEM, VMEM, VMEM, VMEM, SMEM, SMEM],
        out_specs=(VMEM, VMEM, SMEM, SMEM),
        scratch_shapes=[
            pltpu.VMEM((rows, size), jnp.float32),
            pltpu.VMEM((size, cols), jnp.float32),
            pltpu.VMEM((total + 1, depth, size), jnp.bfloat16),
            pltpu.VMEM((depth, size), jnp.float32),
            pltpu.VMEM((size, depth // 2), jnp.float32),
            pltpu.VMEM((depth // 2, depth), jnp.float32),
            pltpu.SMEM((targets,), jnp.int32),
            DMA,
            DMA((2,)),
        ],
        compiler_params=pltpu.CompilerParams(vmem_limit_bytes=LIMIT),
        name="panel",
    )(
        table, most, got, front, pivots, upper_inverse, lower_inverse, column_basis, row_basis,
        column_ranks, row_ranks,
    )


def spread_kernel(
    n_row, n_col, a_src, b_src, a_all, b_all, a_part_send, a_part_recv, b_part_send, b_part_recv,
    a_send, a_recv, b_send, b_recv, swap_sem, own_sem,
):
    r, c = lax.axis_index("row"), lax.axis_index("col")
    half = n_col // 2
    chip, core = c // 2, lax.rem(c, 2)
    sibling = (r, chip * 2 + 1 - core)
    barrier = pltpu.get_barrier_semaphore()

    def mates(n, me, body):
        def one(k, carry):
            body(lax.rem(me + k, n))
            return carry

        lax.fori_loop(1, n, one, 0)

    mates(n_col, c, lambda o: pl.semaphore_signal(barrier, 1, device_id=(r, o), device_id_type=MESH))
    mates(n_row, r, lambda o: pl.semaphore_signal(barrier, 1, device_id=(o, c), device_id_type=MESH))
    pl.semaphore_wait(barrier, n_col + n_row - 2)

    def piece(o):
        return lax.rem(o, 2) * half + o // 2

    def a_part(o):
        return remote(a_src.at[piece(o)], a_all.at[piece(o)], a_part_send.at[o], a_part_recv, (r, o))

    def b_part(o):
        return remote(b_src.at[o], b_all.at[o], b_part_send.at[o], b_part_recv, (o, c))

    def a_full(h):
        at = piece(c)
        return remote(a_all.at[at], a_all.at[at], a_send.at[h], a_recv.at[chip], (r, h * 2 + core))

    def a_from(h):
        at = core * half + h
        return remote(a_all.at[at], a_all.at[at], a_send.at[h], a_recv.at[h], (r, h * 2 + core))

    def b_full(o):
        return remote(b_all.at[r], b_all.at[r], b_send.at[o], b_recv.at[r], (o, c))

    def b_from(o):
        return remote(b_all.at[o], b_all.at[o], b_send.at[o], b_recv.at[o], (o, c))

    def swap(side):
        part = a_all.at[pl.ds(side * half, half)]
        return remote(part, part, swap_sem.at[0], swap_sem.at[1], sibling)

    own_a = pltpu.make_async_copy(a_src.at[0], a_all.at[0], own_sem.at[0])
    own_b = pltpu.make_async_copy(b_src.at[0], b_all.at[0], own_sem.at[1])

    @pl.when(c == 0)
    def _():
        own_a.start()
        mates(n_col, c, lambda o: a_part(o).start())

    @pl.when(r == 0)
    def _():
        own_b.start()
        mates(n_row, r, lambda o: b_part(o).start())

    pl.when(c == 0)(own_a.wait)
    pl.when(c != 0)(lambda: a_part(c).wait_recv())
    mates(half, chip, lambda h: a_full(h).start())
    pl.when(r == 0)(own_b.wait)
    pl.when(r != 0)(lambda: b_part(r).wait_recv())
    mates(n_row, r, lambda o: b_full(o).start())
    mates(half, chip, lambda h: a_from(h).wait_recv())
    swap(core).start()
    mates(n_row, r, lambda o: b_from(o).wait_recv())
    swap(1 - core).wait_recv()
    mates(half, chip, lambda h: a_full(h).wait_send())
    mates(n_row, r, lambda o: b_full(o).wait_send())
    swap(core).wait_send()

    @pl.when(c == 0)
    def _():
        mates(n_col, c, lambda o: a_part(o).wait_send())

    @pl.when(r == 0)
    def _():
        mates(n_row, r, lambda o: b_part(o).wait_send())


def spread(a_src, b_src, n_row, n_col):
    return pl.pallas_call(
        functools.partial(spread_kernel, n_row, n_col),
        out_shape=(
            jax.ShapeDtypeStruct(a_src.shape, a_src.dtype),
            jax.ShapeDtypeStruct(b_src.shape, b_src.dtype),
        ),
        in_specs=[HBM, HBM],
        out_specs=(HBM, HBM),
        scratch_shapes=[
            DMA((n_col,)), DMA, DMA((n_row,)), DMA,
            DMA((n_col // 2,)), DMA((n_col // 2,)), DMA((n_row,)), DMA((n_row,)), DMA((2,)), DMA((2,)),
        ],
        compiler_params=pltpu.CompilerParams(collective_id=1, has_side_effects=True),
        name="spread",
    )(a_src, b_src)


def finish_kernel(
    total, counts, order, most, got, front, a_in, b_in, pivots, upper_inverse, lower_inverse, out,
    extended, buffer, a_all, b_all, b_cat, inverse_parts, corner, got_sem, factor_sem, front_sem,
    out_sem,
):
    size = upper_inverse.shape[0]
    row_blocks, col_blocks = front.shape[0] // size, front.shape[1] // size
    lanes = a_all.shape[2]
    rank = lanes // 2
    pieces = size // lanes
    devices = total // CAP
    is_top, is_left = lax.axis_index("row") == 0, lax.axis_index("col") == 0

    def rows(i):
        return pl.ds(pl.multiple_of(i * size, size), size)

    def load(i):
        return pltpu.make_async_copy(front.at[rows(i)], extended.at[rows(i)], front_sem.at[i])

    def store(i):
        return pltpu.make_async_copy(extended.at[rows(i)], out.at[rows(i)], out_sem.at[i])

    def fetch(layer):
        part = pl.ds(layer * devices, devices)
        return pltpu.make_async_copy(got.at[part], buffer.at[part], got_sem.at[layer])

    def fetch_all(act):
        act(fetch(0))
        for layer in range(1, 3):
            pl.when(most[layer] >= 0)(lambda: act(fetch(layer)))

    factors = (
        pltpu.make_async_copy(a_in, a_all, factor_sem.at[0]),
        pltpu.make_async_copy(b_in, b_all, factor_sem.at[1]),
    )
    for copy in factors:
        copy.start()
    load(0).start()
    fetch_all(lambda copy: copy.start())
    for i in range(1, row_blocks):
        load(i).start()
    buffer[buffer.shape[0] - 1] = jnp.zeros(buffer.shape[1:], buffer.dtype)

    @pl.when(is_left)
    def _():
        high, low = split(upper_inverse[...])
        inverse_parts[0:size] = high
        inverse_parts[size : 2 * size] = low
        inverse_parts[2 * size :] = high

    for copy in factors:
        copy.wait()
    for k in range(b_all.shape[0]):
        cols = slice(k * lanes, (k + 1) * lanes)
        high, low = b_all[k, 0:rank, :], b_all[k, rank:, :]
        if k < pieces:
            high = jnp.where(is_left, jnp.zeros_like(high), high)
            low = jnp.where(is_left, jnp.zeros_like(low), low)
        for h in range(2):
            b_cat[h * rank : (h + 1) * rank, cols] = high
            b_cat[(2 + h) * rank : (3 + h) * rank, cols] = low

    def chunk(t, e):
        picked = []
        for k in range(STACK):
            at = e * STACK + k
            s = order[t * total + jnp.minimum(at, total - 1)]
            picked.append(jnp.where(at < counts[t], s, buffer.shape[0] - 1))
        lefts = jnp.concatenate([buffer[s, 0:rank, :] for s in picked], axis=0)
        rights = jnp.concatenate([buffer[s, rank:, :] for s in picked], axis=0)
        return dot(lefts, rights, ((0,), (0,)))

    fetch_all(lambda copy: copy.wait())

    def step(i, c):
        load(i).wait()
        a = jnp.concatenate([a_all[i * pieces + k] for k in range(pieces)], axis=0)
        a = jnp.concatenate([a, a], axis=1)
        a = jnp.where(jnp.logical_and(is_top, i == 0), jnp.zeros_like(a), a)
        for j in range(col_blocks):
            cols = slice(j * size, (j + 1) * size)
            added = chunk(i * col_blocks + j, 0)
            extended[rows(i), cols] += added - dot(a, b_cat[:, cols])

        def more(e, c):
            for j in range(col_blocks):
                cols = slice(j * size, (j + 1) * size)
                extended[rows(i), cols] += chunk(i * col_blocks + j, e)
            return c

        longest = counts[i * col_blocks]
        for j in range(1, col_blocks):
            longest = jnp.maximum(longest, counts[i * col_blocks + j])
        lax.fori_loop(1, (longest + STACK - 1) // STACK, more, 0)

        @pl.when(jnp.logical_and(is_left, jnp.logical_not(jnp.logical_and(is_top, i == 0))))
        def _():
            high, low = split(extended[rows(i), 0:size])
            extended[rows(i), 0:size] = dot(
                jnp.concatenate([high, high, low], axis=1), inverse_parts[...]
            )

        @pl.when(jnp.logical_and(is_top, i == 0))
        def _():
            permute = permutation(pivots[...])
            corner[...] = dot(permute, extended[0:size, 0:size], ((0,), (0,)), precision=HIGHEST)
            weights = dot(lower_inverse[...], permute, ((1,), (1,)), precision=HIGHEST)
            for j in range(col_blocks):
                cols = slice(j * size, (j + 1) * size)
                upper = dot(weights, extended[0:size, cols], precision=HIGHEST)
                if j == 0:
                    upper = jnp.where(is_left, corner[...], upper)
                extended[0:size, cols] = upper

        store(i).start()
        return c

    lax.fori_loop(0, row_blocks, step, 0)
    for i in range(row_blocks):
        store(i).wait()


def finish(counts, order, most, got, front, a_all, b_all, pivots, upper_inverse, lower_inverse, total):
    depth, size = got.shape[1:]
    rows, cols = front.shape
    row_blocks = rows // size
    return pl.pallas_call(
        functools.partial(finish_kernel, total),
        out_shape=jax.ShapeDtypeStruct(front.shape, jnp.float32),
        in_specs=[SMEM, SMEM, SMEM, HBM, HBM, HBM, HBM, VMEM, VMEM, VMEM],
        out_specs=HBM,
        scratch_shapes=[
            pltpu.VMEM(front.shape, jnp.float32),
            pltpu.VMEM((got.shape[0] + 1, depth, size), jnp.bfloat16),
            pltpu.VMEM(a_all.shape, jnp.bfloat16),
            pltpu.VMEM(b_all.shape, jnp.bfloat16),
            pltpu.VMEM((2 * depth, cols), jnp.bfloat16),
            pltpu.VMEM((3 * size, size), jnp.bfloat16),
            pltpu.VMEM((size, size), jnp.float32),
            DMA((3,)), DMA((2,)), DMA((row_blocks,)), DMA((row_blocks,)),
        ],
        compiler_params=pltpu.CompilerParams(vmem_limit_bytes=LIMIT),
        name="finish",
    )(counts, order, most, got, front, a_all, b_all, pivots, upper_inverse, lower_inverse)


def shards(
    front, child_left, child_right, child_owner, child_slot, pivots, upper_inverse, lower_inverse,
    column_basis, row_basis, column_ranks, row_ranks,
):
    n_row, n_col = lax.axis_size("row"), lax.axis_size("col")
    devices = n_row * n_col
    packed, table = pack(
        child_owner[:, 0], child_slot, jnp.swapaxes(child_left, 1, 2), child_right, devices
    )
    packed = packed.reshape((4, RING, RING, RING) + packed.shape[1:])
    table = table.reshape((2, RING, RING, RING) + table.shape[1:])
    got, got_table = exchange(packed, table, n_col)
    got_table = got_table.reshape((devices,) + got_table.shape[3:])
    most = jnp.max(got_table[:, 0, 0:4], axis=0)
    rounds = (most[3] >= 0).astype(jnp.int32)
    got = lax.fori_loop(0, rounds, lambda i, g: exchange_last(packed, g, n_row, n_col), got)
    got = got.reshape((3 * devices,) + got.shape[3:])
    a_src, b_src, counts, order = panel(
        got_table, most, got, front, pivots[None, :], upper_inverse, lower_inverse, column_basis.T,
        row_basis.T, column_ranks, row_ranks,
    )
    a_all, b_all = spread(a_src, b_src, n_row, n_col)
    return finish(
        counts, order, most, got, front, a_all, b_all, pivots[None, :], upper_inverse, lower_inverse,
        devices * CAP,
    )


def solution(mesh):
    in_specs = (
        P("row", "col"),
        P(("row", "col"), None, None),
        P(("row", "col"), None, None),
        P(("row", "col"), None),
        P(("row", "col")),
        P(),
        P(),
        P(),
        P(),
        P(),
        P("row"),
        P("col"),
    )
    out_specs = P("row", "col")
    return jax.shard_map(shards, mesh=mesh, in_specs=in_specs, out_specs=out_specs, check_vma=False)
```

```python
import functools

import jax
import jax.numpy as jnp
from jax import lax
from jax.experimental import pallas as pl
from jax.experimental.pallas import tpu as pltpu
from jax.sharding import PartitionSpec as P

MESH = pl.DeviceIdType.MESH
HBM = pl.BlockSpec(memory_space=pl.ANY)
SMEM = pl.BlockSpec(memory_space=pltpu.SMEM)
VMEM = pl.BlockSpec(memory_space=pltpu.VMEM)
DMA = pltpu.SemaphoreType.DMA
CAP = 2
STACK = 4
STRIDE = 37
RING = 4
CHIPS = RING**3
LEAD = 16
LIMIT = 56 * 1024 * 1024
HIGHEST = lax.Precision.HIGHEST


def dot(a, b, dims=((1,), (0,)), precision=None):
    return lax.dot_general(
        a, b, (dims, ((), ())), precision=precision, preferred_element_type=jnp.float32
    )


def pack_kernel(
    devices, owner, owner_row, slot_row, left, right, packed, table, staged, named, placed, in_sem,
    out_sem,
):
    count, rank = left.shape[0], left.shape[1]
    chips = devices // 2
    chunks = in_sem.shape[0]
    each = count // chunks

    def load(k):
        part = pl.ds(k * each, each)
        return (
            pltpu.make_async_copy(left.at[part], staged.at[part, pl.ds(0, rank)], in_sem.at[k, 0]),
            pltpu.make_async_copy(right.at[part], staged.at[part, pl.ds(rank, rank)], in_sem.at[k, 1]),
        )

    for k in range(chunks):
        for copy in load(k):
            copy.start()

    def clear(o, c):
        named[o] = 0
        placed[o] = 0
        return c

    lax.fori_loop(0, devices, clear, 0, unroll=8)

    def tally(i, c):
        named[owner[i]] += 1
        return c

    lax.fori_loop(0, count, tally, 0, unroll=4)

    shape = (devices, 1, count)
    place = lax.broadcasted_iota(jnp.int32, shape, 2)
    line = lax.broadcasted_iota(jnp.int32, shape, 0)
    core = line >> 6
    high, middle, low = (line >> 4) & 3, (line >> 2) & 3, line & 3
    x, y, z = (jnp.where(core == 0, a, b) for a, b in ((high, low), (middle, high), (low, middle)))
    device = x * 32 + (z & 1) * 16 + y * 4 + (z & 2) + core
    owners = owner_row[...][None]
    code = (place * 64 + slot_row[...][None]).astype(jnp.float32)

    def ends(which):
        least = jnp.min(jnp.where(which, code, 65536.0), axis=2, keepdims=True)
        most = jnp.max(jnp.where(which, code, -1.0), axis=2, keepdims=True)
        return least, most

    least, most = ends(owners == device)
    low_least, low_most = ends(owners == device - (device & 1))
    core = core[:, :, 0:1]
    first = jnp.where(most >= 0.0, least.astype(jnp.int32) & 63, -1)
    second = jnp.where(most > least, most.astype(jnp.int32) & 63, -1)
    late = jnp.logical_and(core == 1, low_most > low_least)
    last = jnp.where(late, second, -1)
    flag = jnp.max(last.astype(jnp.float32), axis=0, keepdims=True).astype(jnp.int32)
    lane = lax.broadcasted_iota(jnp.int32, table.shape, 2)
    line = jnp.where(lane == 0, first, jnp.where(lane == 1, jnp.where(late, -1, second), -1))
    table[...] = jnp.where(lane == 2, last, jnp.where(lane == 3, flag, line))

    for k in range(chunks):
        for copy in load(k):
            copy.wait()

        def send(i, c):
            o = owner[i]
            p = placed[o]
            placed[o] = 1
            core = o & 1
            x, y, z = o >> 5, (o >> 2) & 3, (o & 2) | ((o >> 4) & 1)
            late = jnp.logical_and(core == 1, named[o - core] == 2)
            first = jnp.where(core == 0, x * 16 + y * 4 + z, chips + y * 16 + z * 4 + x)
            second = 2 * chips + z * 16 + x * 4 + y
            extra = jnp.where(late, 3 * chips + (o >> 1), second)
            at = jnp.where(p == 0, first, extra)
            pltpu.make_async_copy(staged.at[i], packed.at[at], out_sem).start()
            return c

        lax.fori_loop(k * each, (k + 1) * each, send, 0)
    pltpu.make_async_copy(staged, packed.at[pl.ds(0, count)], out_sem).wait()


def pack(owner, slots, left, right, devices):
    count, rank, size = left.shape
    return pl.pallas_call(
        functools.partial(pack_kernel, devices),
        out_shape=(
            jax.ShapeDtypeStruct((2 * devices, 2 * rank, size), left.dtype),
            jax.ShapeDtypeStruct((devices, 1, 128), jnp.int32),
        ),
        in_specs=[SMEM, VMEM, VMEM, HBM, HBM],
        out_specs=(HBM, VMEM),
        scratch_shapes=[
            pltpu.VMEM((count, 2 * rank, size), left.dtype),
            pltpu.SMEM((devices,), jnp.int32),
            pltpu.SMEM((devices,), jnp.int32),
            DMA((4, 2)),
            DMA,
        ],
        compiler_params=pltpu.CompilerParams(vmem_limit_bytes=LIMIT),
        name="pack",
    )(owner, owner[None, :], slots[None, :], left, right)


def position():
    r, q = lax.axis_index("row"), lax.axis_index("col")
    return r // 2, q // 4, lax.rem(q // 2, 2) * 2 + lax.rem(r, 2), lax.rem(q, 2)


def place_of(x, y, z, core):
    x, y, z = lax.rem(x, RING), lax.rem(y, RING), lax.rem(z, RING)
    return x * 2 + lax.rem(z, 2), y * 4 + (z // 2) * 2 + core


def step_of(k):
    d = lax.rem(k * STRIDE, CHIPS)
    steps = (d // (RING * RING), lax.rem(d // RING, RING), lax.rem(d, RING))
    far = [s // 2 - s // 3 for s in steps]
    both = far[0] + far[1] + far[2] > 0
    up = 1 - lax.rem(steps[0] + steps[1] + steps[2], 2)
    return d, steps, far, both, up


def legs(steps, far, up):
    ahead = [f * (3 - 2 * up) for f in far]
    return ahead, [s + 4 - a for s, a in zip(steps, ahead)]


def far_count():
    return sum(2 in (d // 16, d // 4 % 4, d % 4) for d in range(1, CHIPS))


def remote(src, dst, send, recv, device):
    return pltpu.make_async_remote_copy(
        src_ref=src, dst_ref=dst, send_sem=send, recv_sem=recv, device_id=device,
        device_id_type=MESH,
    )


class Together:
    def __init__(self, *rings):
        self.rings = rings

    def __getattr__(self, name):
        def each():
            for ring in self.rings:
                getattr(ring, name)()

        return each


class Ring:
    def __init__(self, at, go, source, target, relay, send_sem, recv_sem, origin=0):
        self.at, self.go, self.source, self.target = at, go, source, target
        self.relay, self.send_sem, self.recv_sem, self.origin = relay, send_sem, recv_sem, origin

    def copy(self, src, dst, i, way):
        return remote(src, dst, self.send_sem.at[i], self.recv_sem.at[i], self.go(1 if way == 0 else 3))

    def by(self, d):
        return lax.rem(self.at + d, RING)

    def begin(self):
        for way in range(2):
            self.copy(self.source(self.by(2), way), self.relay(way), 4 + way, way).start()
        for way, d in ((0, 1), (1, 3)):
            self.copy(self.source(self.by(d), None), self.target(self.at, None), way, way).start()

    def begin_sent(self):
        for way in range(2):
            self.copy(self.source(self.by(2), way), self.relay(way), 4 + way, way).wait_send()
        for way, d in ((0, 1), (1, 3)):
            self.copy(self.source(self.by(d), None), self.target(self.at, None), way, way).wait_send()

    def forward(self):
        for way, d in ((0, 3), (1, 1)):
            held = self.relay(way)
            self.copy(held, held, 4 + way, way).wait_recv()
            self.copy(held, self.target(self.by(d), way), 2 + way, way).start()

    def forward_sent(self):
        for way, d in ((0, 3), (1, 1)):
            self.copy(self.relay(way), self.target(self.by(d), way), 2 + way, way).wait_send()

    def arrived(self):
        for way, d in ((0, 3), (1, 1)):
            part = self.target(self.by(d), None)
            self.copy(part, part, way, way).wait_recv()
        for way in range(2):
            part = self.target(self.by(2), way)
            self.copy(part, part, 2 + way, way).wait_recv()


def exchange_kernel(
    n_col, packed, table, got, got_table, a_one, a_two, t_one, t_two, a_relay_one,
    a_relay_two, a_relay_three, t_relay_one, t_relay_two, t_relay_three, l_one, l_two, l_relay_one,
    l_relay_two, l_relay_three, a_stage_one, a_stage_two, a_stage_three, t_stage, t_last, send_sems,
    recv_sems, hand_sems, own_sems,
):
    x, y, z, core = position()
    here = (x, y, z)
    sibling = place_of(x, y, z, 1 - core)
    barrier = pltpu.get_barrier_semaphore()

    def greet(at):
        pl.semaphore_signal(barrier, 1, device_id=at, device_id_type=MESH)

    greet(sibling)
    for axis in range(3):
        for d in (1, 3):
            for side in range(2):
                greet(place_of(*[here[i] + (d if i == axis else 0) for i in range(3)], side))
    pl.semaphore_wait(barrier, 13)

    def along(axis, to_core):
        def go(d):
            return place_of(*[here[i] + (d if i == axis else 0) for i in range(3)], to_core)

        return here[axis], go

    def along_mine(phase):
        axes = [lax.rem(phase + core, 3) == i for i in range(3)]
        picked = [axes[i].astype(jnp.int32) for i in range(3)]
        at = sum(p * h for p, h in zip(picked, here))
        return at, lambda d: place_of(*[h + d * p for p, h in zip(picked, here)], core)

    def half(ref_at, width):
        return lambda i, h: ref_at(i, pl.ds(0, 2 * width) if h is None else pl.ds(h * width, width))

    arrays = (
        (packed, got, a_one, a_two, a_relay_one, a_relay_two, a_relay_three, 0, 0),
        (table, got_table, l_one, l_two, l_relay_one, l_relay_two, l_relay_three, 9, 7),
    )

    def first_ring(kind, which):
        src, end, one, two, relay, relay_two, relay_three, sent, received = arrays[which]
        at, go = along(kind, kind)
        return Ring(
            at, go, half(lambda j, s: src.at[kind, j, s], 2),
            half(lambda i, s: one.at[i * 2 + core, s], 2), lambda way: relay.at[way, core],
            send_sems.at[sent + kind], recv_sems.at[received + core],
        )

    def first_rings(kind):
        return Together(first_ring(kind, 1), first_ring(kind, 0))

    def first_mine(origin):
        at, go = along_mine(0)

        def ring(src, end, one, two, relay, relay_two, relay_three, sent, received):
            return Ring(
                at, go, None, half(lambda i, s: one.at[i * 2 + origin, s], 2),
                lambda way: relay.at[way, origin], send_sems.at[sent + 2 + origin],
                recv_sems.at[received + origin],
            )

        return Together(ring(*arrays[1]), ring(*arrays[0]))

    def second_ring(which):
        src, end, one, two, relay, relay_two, relay_three, sent, received = arrays[which]
        return Ring(
            *along_mine(1), half(lambda j, s: one.at[s, j], 4), half(lambda i, s: two.at[i, s], 4),
            lambda way: relay_two.at[way], send_sems.at[sent + 4], recv_sems.at[received + 2],
        )

    def third_ring(which):
        src, end, one, two, relay, relay_two, relay_three, sent, received = arrays[which]
        return Ring(
            *along_mine(2), half(lambda j, s: two.at[s, slice(None), j], 2),
            half(lambda i, s: end.at[i, s], 2), lambda way: relay_three.at[way],
            send_sems.at[sent + 5], recv_sems.at[received + 3],
        )

    a_second, a_third = Together(second_ring(1), second_ring(0)), Together(third_ring(1), third_ring(0))
    t_first = Ring(
        *along(2, core), half(lambda j, s: packed.at[2, j, s], 2), half(lambda i, s: t_one.at[i, s], 2),
        lambda way: t_relay_one.at[way], send_sems.at[6], recv_sems.at[4],
    )

    def t_two_part(i, h):
        begin = lax.rem(i, 2) * 4
        part = pl.ds(begin, 4) if h is None else pl.ds(begin + 2 * h, 2)
        return t_two.at[i // 2, part]

    t_second = Ring(
        *along(0, core), half(lambda j, s: t_one.at[s, j], 2), t_two_part,
        lambda way: t_relay_two.at[way], send_sems.at[7], recv_sems.at[5],
    )

    def t_got(side):
        def part(i, h):
            begin = lax.rem(i, 2) * 2
            rows = pl.ds(begin, 2) if h is None else pl.ds(begin + h, 1)
            return got.at[4 + side * 2 + i // 2, rows]

        return part

    t_third = Ring(
        *along(1, core), half(lambda j, s: t_two.at[s, slice(None), j], 1), t_got(core),
        lambda way: t_relay_three.at[way], send_sems.at[8], recv_sems.at[6],
    )

    class Keep:
        def __init__(self, src, stage, dst, i):
            self.load = pltpu.make_async_copy(src, stage, own_sems.at[i])
            self.store = pltpu.make_async_copy(stage, dst, own_sems.at[i])

        def run(self):
            self.load.wait()
            self.store.start()

    def keep(ring, stage, i):
        return Keep(ring.source(ring.at, None), stage, ring.target(ring.at, None), i)

    def keep_line(ring):
        return pltpu.make_async_copy(
            ring.source(ring.at, None), ring.target(ring.at, None), own_sems.at[6]
        )

    def to_sibling(kind, which):
        ring = first_ring(kind, which)
        return remote(
            ring.source(ring.at, None), ring.target(ring.at, None), hand_sems.at[0, 4 + which],
            hand_sems.at[1, 4 + which], sibling,
        )

    first_rings(0).begin()
    first_rings(1).begin()
    t_first.begin()
    for kind in range(2):

        @pl.when(core == kind)
        def _():
            keep_line(first_ring(kind, 1)).start()
            keep(first_ring(kind, 0), a_stage_one, 0).load.start()

        @pl.when(core != kind)
        def _():
            to_sibling(kind, 1).start()
            to_sibling(kind, 0).start()

    t_keep = keep(t_first, t_stage.at[0], 1)
    t_keep.load.start()
    for kind in range(2):

        @pl.when(core == kind)
        def _():
            keep(first_ring(kind, 0), a_stage_one, 0).run()

    t_keep.run()
    for origin in range(2):
        first_mine(origin).forward()
    t_first.forward()
    for origin in range(2):
        first_mine(origin).arrived()
    for kind in range(2):

        @pl.when(core == kind)
        def _():
            keep(first_ring(kind, 0), a_stage_one, 0).store.wait()
            keep_line(first_ring(kind, 1)).wait()
            to_sibling(kind, 1).wait_recv()
            to_sibling(kind, 0).wait_recv()

        @pl.when(core != kind)
        def _():
            to_sibling(kind, 1).wait_send()
            to_sibling(kind, 0).wait_send()

    a_second.begin()
    a_keep, line_keep = keep(second_ring(0), a_stage_two, 2), keep_line(second_ring(1))
    a_keep.load.start()
    line_keep.start()
    t_first.arrived()
    t_keep.store.wait()
    t_second.begin()
    t_keep = keep(t_second, t_stage.at[1], 3)
    t_keep.load.start()
    a_keep.run()
    t_keep.run()
    a_second.forward()
    t_second.forward()
    a_second.arrived()
    a_keep.store.wait()
    line_keep.wait()
    a_third.begin()
    a_keep, line_keep = keep(third_ring(0), a_stage_three, 4), keep_line(third_ring(1))
    a_keep.load.start()
    line_keep.start()
    t_second.arrived()
    t_keep.store.wait()
    t_third.begin()
    last = Keep(t_third.source(y, None), t_last, t_third.target(y, None), 5)
    last.load.start()
    a_keep.run()
    last.run()
    t_third.forward()
    a_third.forward()
    last.store.wait()

    def hand(side, d):
        part = t_got(side)(lax.rem(y + d, RING), None)
        return remote(part, part, hand_sems.at[0, d], hand_sems.at[1, d], sibling)

    hand(core, 0).start()
    t_third.arrived()
    for d in range(1, RING):
        hand(core, d).start()
    a_third.arrived()
    a_keep.store.wait()
    line_keep.wait()
    for d in range(RING):
        hand(1 - core, d).wait_recv()
    first_rings(0).begin_sent()
    first_rings(1).begin_sent()
    for origin in range(2):
        first_mine(origin).forward_sent()
    for ring in (t_first, a_second, t_second, a_third, t_third):
        ring.begin_sent()
        ring.forward_sent()
    for d in range(RING):
        hand(core, d).wait_send()


def exchange(packed, table, n_col):
    block, line = packed.shape[4:], table.shape[4:]

    def held(*shape):
        return jax.ShapeDtypeStruct(shape + block, packed.dtype)

    def lines(*shape):
        return jax.ShapeDtypeStruct(shape + line, table.dtype)

    def stage(*shape):
        return pltpu.VMEM(shape + block, packed.dtype)

    out_shape = (
        held(12, 4, 8), lines(4, 4, 8),
        held(8, 4, 4), held(4, 8, 4), held(4, 4, 4), held(2, 8, 4),
        held(2, 2, 2, 4), held(2, 4, 4), held(2, 2, 8), held(2, 2, 4), held(2, 2, 4), held(2, 1, 8),
        lines(8, 4, 4), lines(4, 8, 4), lines(2, 2, 2, 4), lines(2, 4, 4), lines(2, 2, 8),
    )
    return pl.pallas_call(
        functools.partial(exchange_kernel, n_col),
        out_shape=out_shape,
        in_specs=[HBM, HBM],
        out_specs=(HBM,) * len(out_shape),
        scratch_shapes=[
            stage(4, 4), stage(8, 4), stage(4, 8), stage(2, 4, 4), stage(2, 8),
            DMA((15, 6)), DMA((11, 6)), DMA((2, 6)), DMA((7,)),
        ],
        compiler_params=pltpu.CompilerParams(
            collective_id=2, has_side_effects=True, vmem_limit_bytes=LIMIT
        ),
        name="exchange",
    )(packed, table)[:2]


def last_kernel(n_row, n_col, packed, got_in, got, relay, sems, relay_sem, own_sem):
    devices = n_row * n_col
    x, y, z, core = position()
    mine = place_of(x, y, z, core)
    me = mine[0] * n_col + mine[1]
    barrier = pltpu.get_barrier_semaphore()

    def at_step(steps, core):
        return place_of(x + steps[0], y + steps[1], z + steps[2], core)

    def number(device):
        return device[0] * n_col + device[1]

    def greet(at):
        pl.semaphore_signal(barrier, 1, device_id=at, device_id_type=MESH)

    def near(k, carry):
        d, steps, far, both, up = step_of(k)

        @pl.when(jnp.logical_and(core == 1, jnp.logical_not(both)))
        def _():
            greet(at_step(steps, 0))
            greet(at_step(steps, 1))

        return carry

    def relayed(k, carry):
        bits = (k // 8, lax.rem(k // 4, 2), lax.rem(k // 2, 2))
        way = lax.rem(k, 2)

        @pl.when(jnp.logical_and(core == 0, k != 15))
        def _():
            greet(at_step([b * (3 - 2 * way) for b in bits], 0))

        return carry

    lax.fori_loop(1, CHIPS, near, 0)
    lax.fori_loop(2, 16, relayed, 0)

    @pl.when(core == 1)
    def _():
        greet(place_of(x, y, z, 0))
        pl.semaphore_wait(barrier, 26)

    @pl.when(core == 0)
    def _():
        pl.semaphore_wait(barrier, 26 + 13 + 1)

    def block_for(target):
        chip = number(target) // 2
        return packed.at[3, chip // 16, lax.rem(chip // 4, 4), lax.rem(chip, 4)]

    def landing(source):
        return got.at[8 + source // 32, lax.rem(source // 8, 4), lax.rem(source, 8)]

    def first_leg(k, carry):
        d, steps, far, both, up = step_of(k)

        @pl.when(both)
        def _():
            first, second = legs(steps, far, up)
            remote(
                block_for(at_step(steps, 1)), relay.at[d], sems.at[0], relay_sem.at[d],
                at_step(first, core),
            ).start()

        return carry

    def direct(k, carry):
        d, steps, far, both, up = step_of(k)

        @pl.when(jnp.logical_not(both))
        def _():
            target = at_step(steps, 1)
            remote(block_for(target), landing(me), sems.at[0], sems.at[1], target).start()

        return carry

    def second_leg(k, carry):
        d, steps, far, both, up = step_of(k)

        @pl.when(both)
        def _():
            first, second = legs(steps, far, up)
            source = number(at_step([4 - f for f in first], core))
            target = at_step(second, 1)
            held = relay.at[d]
            remote(held, held, sems.at[2], relay_sem.at[d], target).wait_recv()
            remote(held, landing(source), sems.at[2], sems.at[1], target).start()

        return carry

    lax.fori_loop(1, CHIPS, first_leg, 0)
    lax.fori_loop(1, CHIPS, direct, 0)
    lax.fori_loop(1, CHIPS, second_leg, 0)

    def settle(ref, count, sem):
        part = ref.at[pl.ds(0, count)]
        pltpu.make_async_copy(part, part, sem).wait()

    settle(relay, far_count(), sems.at[2])

    @pl.when(core == 0)
    def _():
        to = place_of(x, y, z, 1)
        remote(block_for(to), landing(me), sems.at[0], sems.at[1], to).start()
        settle(relay, CHIPS, sems.at[0])

    @pl.when(core == 1)
    def _():
        own = pltpu.make_async_copy(block_for(mine), landing(me), own_sem)
        own.start()
        own.wait()
        settle(relay, CHIPS - 1, sems.at[0])
        settle(relay, devices - 1, sems.at[1])


def exchange_last(packed, got, n_row, n_col):
    return pl.pallas_call(
        functools.partial(last_kernel, n_row, n_col),
        out_shape=(
            jax.ShapeDtypeStruct(got.shape, got.dtype),
            jax.ShapeDtypeStruct((2 * CHIPS,) + packed.shape[4:], packed.dtype),
        ),
        in_specs=[HBM, HBM],
        out_specs=(HBM, HBM),
        input_output_aliases={1: 0},
        scratch_shapes=[DMA((3,)), DMA((CHIPS,)), DMA],
        compiler_params=pltpu.CompilerParams(collective_id=3, has_side_effects=True),
        name="exchange_last",
    )(packed, got)[0]


def fetch_target(t, at, total, counts, order, base, got, buffer, sem):
    base[t] = at

    def one(e, c):
        pltpu.make_async_copy(got.at[order[t, e]], buffer.at[at + e], sem).start()
        return c

    lax.fori_loop(0, counts[t, 0], one, 0)
    return at + counts[t, 0]


def await_target(t, counts, got, buffer, sem):
    def one(e, c):
        pltpu.make_async_copy(got.at[0], buffer.at[0], sem).wait()
        return c

    lax.fori_loop(0, counts[t, 0], one, 0)


def product(t, e, counts, base, buffer):
    rank = buffer.shape[1] // 2
    n, begin = counts[t, 0], base[t]
    picked = [
        jnp.where(e * STACK + k < n, begin + e * STACK + k, buffer.shape[0] - 1) for k in range(STACK)
    ]
    lefts = jnp.concatenate([buffer[s, 0:rank, :] for s in picked], axis=0)
    rights = jnp.concatenate([buffer[s, rank:, :] for s in picked], axis=0)
    return dot(lefts, rights, ((0,), (0,)))


def add_rest(t, counts, base, buffer, sum_ref, rows, cols):
    def chunk(e, c):
        sum_ref[rows, cols] += product(t, e, counts, base, buffer)
        return c

    lax.fori_loop(1, (counts[t, 0] + STACK - 1) // STACK, chunk, 0)


def split(x):
    high = x.astype(jnp.bfloat16)
    return high, (x - high.astype(jnp.float32)).astype(jnp.bfloat16)


def dot3(a, b):
    a_high, a_low = split(a)
    b_high, b_low = split(b)
    return dot(a_high, b_high) + (dot(a_high, b_low) + dot(a_low, b_high))


def permutation(pivots):
    size = pivots.shape[1]
    places = lax.broadcasted_iota(jnp.int32, (size, size), 0)
    return (places == pivots).astype(jnp.float32)


def panel_kernel(
    total, table, got, front, pivots, upper_inverse, lower_inverse, column_basis, row_basis,
    column_ranks, row_ranks, a_out, b_out, counts, order, left_sum, top_sum, buffer, top_weights,
    left_weights, coupling, order_rows, count_rows, base, sem, front_sem, sort_sem,
):
    size, rank = upper_inverse.shape[0], column_basis.shape[0]
    row_blocks, col_blocks = front.shape[0] // size, front.shape[1] // size
    targets = row_blocks * col_blocks
    devices = total // CAP
    is_top, is_left = lax.axis_index("row") == 0, lax.axis_index("col") == 0
    load_left = pltpu.make_async_copy(front.at[:, pl.ds(0, size)], left_sum, front_sem.at[0])
    load_top = pltpu.make_async_copy(front.at[pl.ds(0, size)], top_sum, front_sem.at[1])
    pl.when(is_left)(load_left.start)
    pl.when(is_top)(load_top.start)

    core = lax.rem(lax.axis_index("col"), 2)
    k = lax.broadcasted_iota(jnp.int32, (1, devices), 1)
    high, middle, low, side = k >> 5, (k >> 3) & 3, (k >> 1) & 3, k & 1
    x, y, z = (jnp.where(core == 0, a, b) for a, b in ((low, high), (middle, low), (high, middle)))
    shared = devices + side * CHIPS + y * 16 + x * 4 + z
    last = 2 * devices + x * 32 + (z & 1) * 16 + y * 4 + (z & 2) + side
    block = jnp.concatenate([k, shared, last], axis=1)
    target = jnp.concatenate([table[p : p + 1, :] for p in range(3)], axis=1)
    entries = block.shape[1]
    member = lax.broadcasted_iota(jnp.int32, (targets, entries), 0) == target
    member_one = member.astype(jnp.float32)
    before = (
        lax.broadcasted_iota(jnp.int32, (entries, entries), 0)
        < lax.broadcasted_iota(jnp.int32, (entries, entries), 1)
    ).astype(jnp.bfloat16)
    earlier = dot(member_one.astype(jnp.bfloat16), before)
    rank_of = jnp.sum(jnp.where(member, earlier, 0.0), axis=0, keepdims=True)
    chosen = lax.broadcasted_iota(jnp.int32, (total, entries), 0) == rank_of.astype(jnp.int32)
    upper_part = jnp.where(member, (block >> 7).astype(jnp.float32), 0.0).astype(jnp.bfloat16)
    lower_part = jnp.where(member, (block & 127).astype(jnp.float32), 0.0).astype(jnp.bfloat16)
    chosen = chosen.astype(jnp.float32).astype(jnp.bfloat16)
    listed = dot(upper_part, chosen, ((1,), (1,))) * 128.0 + dot(lower_part, chosen, ((1,), (1,)))
    order_rows[...] = listed.astype(jnp.int32)
    tally = jnp.sum(member_one, axis=1, keepdims=True).astype(jnp.int32)
    count_rows[...] = jnp.broadcast_to(tally, count_rows.shape)
    copies = (
        pltpu.make_async_copy(order_rows, order, sort_sem.at[0]),
        pltpu.make_async_copy(count_rows, counts, sort_sem.at[1]),
    )
    for copy in copies:
        copy.start()
    for copy in copies:
        copy.wait()

    @pl.when(jnp.logical_or(is_top, is_left))
    def _():
        buffer[buffer.shape[0] - 1] = jnp.zeros(buffer.shape[1:], buffer.dtype)

        def fetch(t, at):
            return fetch_target(t, at, total, counts, order, base, got, buffer, sem)

        def fetch_left(i, at):
            return fetch(i * col_blocks, at)

        at = lax.fori_loop(0, jnp.where(is_left, row_blocks, 0), fetch_left, 0)
        lax.fori_loop(jnp.where(is_left, 1, 0), jnp.where(is_top, col_blocks, 0), fetch, at)

    @pl.when(is_top)
    def _():
        weights = dot(row_basis[...], lower_inverse[...], precision=HIGHEST)
        weights = dot(weights, permutation(pivots[...]), ((1,), (1,)), precision=HIGHEST)
        top_weights[0:rank] = weights
        top_weights[rank:] = weights

    @pl.when(is_left)
    def _():
        left_weights[...] = dot(
            upper_inverse[...], column_basis[...], ((1,), (1,)), precision=HIGHEST
        )
        coupled = dot(column_basis[...], row_basis[...], ((1,), (1,)), precision=HIGHEST)
        coupling[...] = jnp.concatenate([coupled, coupled], axis=1)

    @pl.when(jnp.logical_or(is_top, is_left))
    def _():
        def ready(t):
            await_target(t, counts, got, buffer, sem)

        def ready_left(i, c):
            ready(i * col_blocks)
            return c

        def ready_top(t, c):
            ready(t)
            return c

        lax.fori_loop(0, jnp.where(is_left, row_blocks, 0), ready_left, 0)
        lax.fori_loop(jnp.where(is_left, 1, 0), jnp.where(is_top, col_blocks, 0), ready_top, 0)

    @pl.when(is_top)
    def _():
        row = lax.broadcasted_iota(jnp.int32, (2 * rank, size), 0)
        load_top.wait()
        for j in range(col_blocks):
            cols = slice(j * size, (j + 1) * size)
            top_sum[:, cols] += product(j, 0, counts, base, buffer)
        for j in range(col_blocks):
            add_rest(j, counts, base, buffer, top_sum, slice(0, size), slice(j * size, (j + 1) * size))
        for j in range(col_blocks):
            cols = slice(j * size, (j + 1) * size)
            factor = dot3(top_weights[...], top_sum[:, cols])
            factor = jnp.where(lax.rem(row, rank) < row_ranks[j], factor, 0.0)
            high, low = split(factor)
            value = jnp.where(row < rank, high.astype(jnp.float32), low.astype(jnp.float32))
            for h in range(size // 128):
                b_out[j * (size // 128) + h] = value[:, h * 128 : (h + 1) * 128].astype(jnp.bfloat16)

    @pl.when(is_left)
    def _():
        lane = lax.broadcasted_iota(jnp.int32, (size, 2 * rank), 1)
        load_left.wait()

        def add(i, c):
            rows = pl.ds(pl.multiple_of(i * size, size), size)
            left_sum[rows, :] += product(i * col_blocks, 0, counts, base, buffer)
            return c

        lax.fori_loop(0, row_blocks, add, 0, unroll=4)

        def add_more(i, c):
            rows = pl.ds(pl.multiple_of(i * size, size), size)
            add_rest(i * col_blocks, counts, base, buffer, left_sum, rows, slice(0, size))
            return c

        lax.fori_loop(0, row_blocks, add_more, 0)

        def block(i, c):
            rows = pl.ds(pl.multiple_of(i * size, size), size)
            factor = dot3(left_sum[rows, :], left_weights[...])
            factor = jnp.where(lane[:, 0:rank] < column_ranks[i], factor, 0.0)
            high, low = split(dot3(factor, coupling[...]))
            value = jnp.where(lane < rank, high.astype(jnp.float32), low.astype(jnp.float32))
            for h in range(size // 128):
                a_out[i * (size // 128) + h] = value[h * 128 : (h + 1) * 128].astype(jnp.bfloat16)
            return c

        lax.fori_loop(0, row_blocks, block, 0, unroll=4)


def panel(
    table, got, front, pivots, upper_inverse, lower_inverse, column_basis, row_basis, column_ranks,
    row_ranks,
):
    depth, size = got.shape[1:]
    total = table.shape[1] * CAP
    rows, cols = front.shape
    targets = (rows // size) * (cols // size)
    return pl.pallas_call(
        functools.partial(panel_kernel, total),
        out_shape=(
            jax.ShapeDtypeStruct((rows // 128, 128, 128), jnp.bfloat16),
            jax.ShapeDtypeStruct((cols // 128, 128, 128), jnp.bfloat16),
            jax.ShapeDtypeStruct((targets, 128), jnp.int32),
            jax.ShapeDtypeStruct((targets, total), jnp.int32),
        ),
        in_specs=[VMEM, HBM, HBM, VMEM, VMEM, VMEM, VMEM, VMEM, SMEM, SMEM],
        out_specs=(VMEM, VMEM, SMEM, SMEM),
        scratch_shapes=[
            pltpu.VMEM((rows, size), jnp.float32),
            pltpu.VMEM((size, cols), jnp.float32),
            pltpu.VMEM((total + 1, depth, size), jnp.bfloat16),
            pltpu.VMEM((depth, size), jnp.float32),
            pltpu.VMEM((size, depth // 2), jnp.float32),
            pltpu.VMEM((depth // 2, depth), jnp.float32),
            pltpu.VMEM((targets, total), jnp.int32),
            pltpu.VMEM((targets, 128), jnp.int32),
            pltpu.SMEM((targets,), jnp.int32),
            DMA,
            DMA((2,)),
            DMA((2,)),
        ],
        compiler_params=pltpu.CompilerParams(vmem_limit_bytes=LIMIT),
        name="panel",
    )(
        table, got, front, pivots, upper_inverse, lower_inverse, column_basis, row_basis,
        column_ranks, row_ranks,
    )


def spread_kernel(
    n_row, n_col, a_src, b_src, a_all, b_all, a_part_send, a_part_recv, b_part_send, b_part_recv,
    a_send, a_recv, b_send, b_recv, swap_sem, own_sem,
):
    r, c = lax.axis_index("row"), lax.axis_index("col")
    half = n_col // 2
    chip, core = c // 2, lax.rem(c, 2)
    sibling = (r, chip * 2 + 1 - core)
    barrier = pltpu.get_barrier_semaphore()

    def mates(n, me, body):
        def one(k, carry):
            body(lax.rem(me + k, n))
            return carry

        lax.fori_loop(1, n, one, 0)

    mates(n_col, c, lambda o: pl.semaphore_signal(barrier, 1, device_id=(r, o), device_id_type=MESH))
    mates(n_row, r, lambda o: pl.semaphore_signal(barrier, 1, device_id=(o, c), device_id_type=MESH))
    pl.semaphore_wait(barrier, n_col + n_row - 2)

    def piece(o):
        return lax.rem(o, 2) * half + o // 2

    def a_part(o):
        return remote(a_src.at[piece(o)], a_all.at[piece(o)], a_part_send.at[o], a_part_recv, (r, o))

    def b_part(o):
        return remote(b_src.at[o], b_all.at[o], b_part_send.at[o], b_part_recv, (o, c))

    def a_full(h):
        at = piece(c)
        return remote(a_all.at[at], a_all.at[at], a_send.at[h], a_recv.at[chip], (r, h * 2 + core))

    def a_from(h):
        at = core * half + h
        return remote(a_all.at[at], a_all.at[at], a_send.at[h], a_recv.at[h], (r, h * 2 + core))

    def b_full(o):
        return remote(b_all.at[r], b_all.at[r], b_send.at[o], b_recv.at[r], (o, c))

    def b_from(o):
        return remote(b_all.at[o], b_all.at[o], b_send.at[o], b_recv.at[o], (o, c))

    def swap(side):
        part = a_all.at[pl.ds(side * half, half)]
        return remote(part, part, swap_sem.at[0], swap_sem.at[1], sibling)

    own_a = pltpu.make_async_copy(a_src.at[0], a_all.at[0], own_sem.at[0])
    own_b = pltpu.make_async_copy(b_src.at[0], b_all.at[0], own_sem.at[1])

    @pl.when(c == 0)
    def _():
        own_a.start()
        mates(n_col, c, lambda o: a_part(o).start())

    @pl.when(r == 0)
    def _():
        own_b.start()
        mates(n_row, r, lambda o: b_part(o).start())

    pl.when(c == 0)(own_a.wait)
    pl.when(c != 0)(lambda: a_part(c).wait_recv())
    mates(half, chip, lambda h: a_full(h).start())
    pl.when(r == 0)(own_b.wait)
    pl.when(r != 0)(lambda: b_part(r).wait_recv())
    mates(n_row, r, lambda o: b_full(o).start())
    mates(half, chip, lambda h: a_from(h).wait_recv())
    swap(core).start()
    mates(n_row, r, lambda o: b_from(o).wait_recv())
    swap(1 - core).wait_recv()
    mates(half, chip, lambda h: a_full(h).wait_send())
    mates(n_row, r, lambda o: b_full(o).wait_send())
    swap(core).wait_send()

    @pl.when(c == 0)
    def _():
        mates(n_col, c, lambda o: a_part(o).wait_send())

    @pl.when(r == 0)
    def _():
        mates(n_row, r, lambda o: b_part(o).wait_send())


def spread(a_src, b_src, n_row, n_col):
    return pl.pallas_call(
        functools.partial(spread_kernel, n_row, n_col),
        out_shape=(
            jax.ShapeDtypeStruct(a_src.shape, a_src.dtype),
            jax.ShapeDtypeStruct(b_src.shape, b_src.dtype),
        ),
        in_specs=[VMEM, VMEM],
        out_specs=(VMEM, VMEM),
        scratch_shapes=[
            DMA((n_col,)), DMA, DMA((n_row,)), DMA,
            DMA((n_col // 2,)), DMA((n_col // 2,)), DMA((n_row,)), DMA((n_row,)), DMA((2,)), DMA((2,)),
        ],
        compiler_params=pltpu.CompilerParams(collective_id=1, has_side_effects=True),
        name="spread",
    )(a_src, b_src)


def finish_kernel(
    total, counts, order, most, got, front, a_in, b_in, pivots, upper_inverse, lower_inverse, out,
    extended, buffer, a_all, b_all, b_cat, inverse_parts, corner, got_sem, factor_sem, front_sem,
    out_sem,
):
    size = upper_inverse.shape[0]
    row_blocks, col_blocks = front.shape[0] // size, front.shape[1] // size
    lanes = a_all.shape[2]
    rank = lanes // 2
    pieces = size // lanes
    devices = total // CAP
    is_top, is_left = lax.axis_index("row") == 0, lax.axis_index("col") == 0

    def rows(i):
        return pl.ds(pl.multiple_of(i * size, size), size)

    def load(i):
        return pltpu.make_async_copy(front.at[rows(i)], extended.at[rows(i)], front_sem.at[i])

    def store(i):
        return pltpu.make_async_copy(extended.at[rows(i)], out.at[rows(i)], out_sem.at[i])

    def fetch(layer):
        part = pl.ds(layer * devices, devices)
        return pltpu.make_async_copy(got.at[part], buffer.at[part], got_sem.at[layer])

    def fetch_all(act):
        act(fetch(0))
        for layer in range(1, 3):
            pl.when(most[layer] >= 0)(lambda: act(fetch(layer)))

    factors = (
        pltpu.make_async_copy(a_in, a_all, factor_sem.at[0]),
        pltpu.make_async_copy(b_in, b_all, factor_sem.at[1]),
    )
    for copy in factors:
        copy.start()
    for i in range(row_blocks):
        load(i).start()
    fetch_all(lambda copy: copy.start())
    buffer[buffer.shape[0] - 1] = jnp.zeros(buffer.shape[1:], buffer.dtype)

    @pl.when(is_left)
    def _():
        high, low = split(upper_inverse[...])
        inverse_parts[0:size] = high
        inverse_parts[size : 2 * size] = low
        inverse_parts[2 * size :] = high

    for copy in factors:
        copy.wait()
    for k in range(b_all.shape[0]):
        cols = slice(k * lanes, (k + 1) * lanes)
        high, low = b_all[k, 0:rank, :], b_all[k, rank:, :]
        if k < pieces:
            high = jnp.where(is_left, jnp.zeros_like(high), high)
            low = jnp.where(is_left, jnp.zeros_like(low), low)
        for h in range(2):
            b_cat[h * rank : (h + 1) * rank, cols] = high
            b_cat[(2 + h) * rank : (3 + h) * rank, cols] = low

    def chunk(t, e):
        picked = []
        for k in range(STACK):
            at = e * STACK + k
            s = order[t, jnp.minimum(at, total - 1)]
            picked.append(jnp.where(at < counts[t, 0], s, buffer.shape[0] - 1))
        lefts = jnp.concatenate([buffer[s, 0:rank, :] for s in picked], axis=0)
        rights = jnp.concatenate([buffer[s, rank:, :] for s in picked], axis=0)
        return dot(lefts, rights, ((0,), (0,)))

    def update(i, c):
        load(i).wait()
        a = jnp.concatenate([a_all[i * pieces + k] for k in range(pieces)], axis=0)
        a = jnp.concatenate([a, a], axis=1)
        a = jnp.where(jnp.logical_and(is_top, i == 0), jnp.zeros_like(a), a)
        for j in range(col_blocks):
            cols = slice(j * size, (j + 1) * size)
            extended[rows(i), cols] -= dot(a, b_cat[:, cols])
        return c

    lax.fori_loop(0, row_blocks, update, 0)
    fetch_all(lambda copy: copy.wait())

    def step(i, c):
        def more(e, c):
            for j in range(col_blocks):
                cols = slice(j * size, (j + 1) * size)
                extended[rows(i), cols] += chunk(i * col_blocks + j, e)
            return c

        longest = counts[i * col_blocks, 0]
        for j in range(1, col_blocks):
            longest = jnp.maximum(longest, counts[i * col_blocks + j, 0])
        lax.fori_loop(0, (longest + STACK - 1) // STACK, more, 0)

        @pl.when(jnp.logical_and(is_left, jnp.logical_not(jnp.logical_and(is_top, i == 0))))
        def _():
            high, low = split(extended[rows(i), 0:size])
            extended[rows(i), 0:size] = dot(
                jnp.concatenate([high, high, low], axis=1), inverse_parts[...]
            )

        @pl.when(jnp.logical_and(is_top, i == 0))
        def _():
            permute = permutation(pivots[...])
            corner[...] = dot(permute, extended[0:size, 0:size], ((0,), (0,)), precision=HIGHEST)
            weights = dot(lower_inverse[...], permute, ((1,), (1,)), precision=HIGHEST)
            for j in range(col_blocks):
                cols = slice(j * size, (j + 1) * size)
                upper = dot(weights, extended[0:size, cols], precision=HIGHEST)
                if j == 0:
                    upper = jnp.where(is_left, corner[...], upper)
                extended[0:size, cols] = upper

        store(i).start()
        return c

    lax.fori_loop(0, row_blocks, step, 0)
    for i in range(row_blocks):
        store(i).wait()


def finish(counts, order, most, got, front, a_all, b_all, pivots, upper_inverse, lower_inverse, total):
    depth, size = got.shape[1:]
    rows, cols = front.shape
    row_blocks = rows // size
    return pl.pallas_call(
        functools.partial(finish_kernel, total),
        out_shape=jax.ShapeDtypeStruct(front.shape, jnp.float32),
        in_specs=[SMEM, SMEM, SMEM, HBM, HBM, HBM, HBM, VMEM, VMEM, VMEM],
        out_specs=HBM,
        scratch_shapes=[
            pltpu.VMEM(front.shape, jnp.float32),
            pltpu.VMEM((got.shape[0] + 1, depth, size), jnp.bfloat16),
            pltpu.VMEM(a_all.shape, jnp.bfloat16),
            pltpu.VMEM(b_all.shape, jnp.bfloat16),
            pltpu.VMEM((2 * depth, cols), jnp.bfloat16),
            pltpu.VMEM((3 * size, size), jnp.bfloat16),
            pltpu.VMEM((size, size), jnp.float32),
            DMA((3,)), DMA((2,)), DMA((row_blocks,)), DMA((row_blocks,)),
        ],
        compiler_params=pltpu.CompilerParams(vmem_limit_bytes=LIMIT),
        name="finish",
    )(counts, order, most, got, front, a_all, b_all, pivots, upper_inverse, lower_inverse)


def shards(
    front, child_left, child_right, child_owner, child_slot, pivots, upper_inverse, lower_inverse,
    column_basis, row_basis, column_ranks, row_ranks,
):
    n_row, n_col = lax.axis_size("row"), lax.axis_size("col")
    devices = n_row * n_col
    packed, table = pack(
        child_owner[:, 0], child_slot, jnp.swapaxes(child_left, 1, 2), child_right, devices
    )
    packed = packed.reshape((4, RING, RING, RING) + packed.shape[1:])
    table = table.reshape((2, RING, RING, RING) + table.shape[1:])
    got, got_table = exchange(packed, table, n_col)
    got_table = got_table.reshape((devices,) + got_table.shape[3:])
    lines = got_table[:, 0, 0:8].T
    most = jnp.max(lines, axis=1)
    rounds = (most[3] >= 0).astype(jnp.int32)
    got = lax.fori_loop(0, rounds, lambda i, g: exchange_last(packed, g, n_row, n_col), got)
    got = got.reshape((3 * devices,) + got.shape[3:])
    a_src, b_src, counts, order = panel(
        lines, got, front, pivots[None, :], upper_inverse, lower_inverse, column_basis.T,
        row_basis.T, column_ranks, row_ranks,
    )
    a_all, b_all = spread(a_src, b_src, n_row, n_col)
    return finish(
        counts, order, most, got, front, a_all, b_all, pivots[None, :], upper_inverse, lower_inverse,
        devices * CAP,
    )


def solution(mesh):
    in_specs = (
        P("row", "col"),
        P(("row", "col"), None, None),
        P(("row", "col"), None, None),
        P(("row", "col"), None),
        P(("row", "col")),
        P(),
        P(),
        P(),
        P(),
        P(),
        P("row"),
        P("col"),
    )
    out_specs = P("row", "col")
    return jax.shard_map(shards, mesh=mesh, in_specs=in_specs, out_specs=out_specs, check_vma=False)
```

```python
import functools

import jax
import jax.numpy as jnp
from jax import lax
from jax.experimental import pallas as pl
from jax.experimental.pallas import tpu as pltpu
from jax.sharding import PartitionSpec as P

MESH = pl.DeviceIdType.MESH
HBM = pl.BlockSpec(memory_space=pl.ANY)
SMEM = pl.BlockSpec(memory_space=pltpu.SMEM)
VMEM = pl.BlockSpec(memory_space=pltpu.VMEM)
DMA = pltpu.SemaphoreType.DMA
CAP = 2
STACK = 4
STRIDE = 37
RING = 4
CHIPS = RING**3
LEAD = 16
LIMIT = 56 * 1024 * 1024
HIGHEST = lax.Precision.HIGHEST


def dot(a, b, dims=((1,), (0,)), precision=None):
    return lax.dot_general(
        a, b, (dims, ((), ())), precision=precision, preferred_element_type=jnp.float32
    )


def pack_kernel(
    devices, owner, owner_row, slot_row, left, right, packed, table, spare, staged, named, placed,
    used, in_sem, out_sem, spare_sem,
):
    count, rank = left.shape[0], left.shape[1]
    chips = devices // 2
    chunks = in_sem.shape[0]
    each = count // chunks

    def load(k):
        part = pl.ds(k * each, each)
        return (
            pltpu.make_async_copy(left.at[part], staged.at[part, pl.ds(0, rank)], in_sem.at[k, 0]),
            pltpu.make_async_copy(right.at[part], staged.at[part, pl.ds(rank, rank)], in_sem.at[k, 1]),
        )

    for k in range(chunks):
        for copy in load(k):
            copy.start()

    def clear(o, c):
        named[o] = 0
        placed[o] = 0
        return c

    lax.fori_loop(0, devices, clear, 0, unroll=8)
    used[0] = 0

    def tally(i, c):
        named[owner[i]] += 1
        return c

    lax.fori_loop(0, count, tally, 0, unroll=4)

    shape = (devices, 1, count)
    place = lax.broadcasted_iota(jnp.int32, shape, 2)
    line = lax.broadcasted_iota(jnp.int32, shape, 0)
    core = line >> 6
    high, middle, low = (line >> 4) & 3, (line >> 2) & 3, line & 3
    x, y, z = (jnp.where(core == 0, a, b) for a, b in ((high, low), (middle, high), (low, middle)))
    device = x * 32 + (z & 1) * 16 + y * 4 + (z & 2) + core
    owners = owner_row[...][None]
    code = (place * 64 + slot_row[...][None]).astype(jnp.float32)

    def ends(which):
        least = jnp.min(jnp.where(which, code, 65536.0), axis=2, keepdims=True)
        most = jnp.max(jnp.where(which, code, -1.0), axis=2, keepdims=True)
        return least, most

    least, most = ends(owners == device)
    low_least, low_most = ends(owners == device - (device & 1))
    core = core[:, :, 0:1]
    first = jnp.where(most >= 0.0, least.astype(jnp.int32) & 63, -1)
    second = jnp.where(most > least, most.astype(jnp.int32) & 63, -1)
    late = jnp.logical_and(core == 1, low_most > low_least)
    last = jnp.where(late, second, -1)
    flag = jnp.sum(jnp.where(last >= 0, 1.0, 0.0), axis=0, keepdims=True).astype(jnp.int32)
    lane = lax.broadcasted_iota(jnp.int32, table.shape, 2)
    line = jnp.where(lane == 0, first, jnp.where(lane == 1, jnp.where(late, -1, second), -1))
    table[...] = jnp.where(lane == 2, last, jnp.where(lane == 3, flag, line))

    for k in range(chunks):
        for copy in load(k):
            copy.wait()

        def send(i, c):
            o = owner[i]
            p = placed[o]
            placed[o] = 1
            core = o & 1
            x, y, z = o >> 5, (o >> 2) & 3, (o & 2) | ((o >> 4) & 1)
            late = jnp.logical_and(core == 1, named[o - core] == 2)
            first = jnp.where(core == 0, x * 16 + y * 4 + z, chips + y * 16 + z * 4 + x)
            second = 2 * chips + z * 16 + x * 4 + y
            extra = jnp.where(late, 3 * chips + (o >> 1), second)
            at = jnp.where(p == 0, first, extra)
            pltpu.make_async_copy(staged.at[i], packed.at[at], out_sem).start()

            @pl.when(jnp.logical_and(jnp.logical_and(late, p != 0), used[0] == 0))
            def _():
                pltpu.make_async_copy(staged.at[i], spare, spare_sem).start()
                used[0] = 1

            return c

        lax.fori_loop(k * each, (k + 1) * each, send, 0)
    pltpu.make_async_copy(staged, packed.at[pl.ds(0, count)], out_sem).wait()
    pl.when(used[0] == 1)(pltpu.make_async_copy(staged.at[0], spare, spare_sem).wait)


def pack(owner, slots, left, right, devices):
    count, rank, size = left.shape
    return pl.pallas_call(
        functools.partial(pack_kernel, devices),
        out_shape=(
            jax.ShapeDtypeStruct((2 * devices, 2 * rank, size), left.dtype),
            jax.ShapeDtypeStruct((devices, 1, 128), jnp.int32),
            jax.ShapeDtypeStruct((2 * rank, size), left.dtype),
        ),
        in_specs=[SMEM, VMEM, VMEM, HBM, HBM],
        out_specs=(HBM, VMEM, HBM),
        scratch_shapes=[
            pltpu.VMEM((count, 2 * rank, size), left.dtype),
            pltpu.SMEM((devices,), jnp.int32),
            pltpu.SMEM((devices,), jnp.int32),
            pltpu.SMEM((1,), jnp.int32),
            DMA((4, 2)),
            DMA,
            DMA,
        ],
        compiler_params=pltpu.CompilerParams(vmem_limit_bytes=LIMIT),
        name="pack",
    )(owner, owner[None, :], slots[None, :], left, right)


def position():
    r, q = lax.axis_index("row"), lax.axis_index("col")
    return r // 2, q // 4, lax.rem(q // 2, 2) * 2 + lax.rem(r, 2), lax.rem(q, 2)


def place_of(x, y, z, core):
    x, y, z = lax.rem(x, RING), lax.rem(y, RING), lax.rem(z, RING)
    return x * 2 + lax.rem(z, 2), y * 4 + (z // 2) * 2 + core


def step_of(k):
    d = lax.rem(k * STRIDE, CHIPS)
    steps = (d // (RING * RING), lax.rem(d // RING, RING), lax.rem(d, RING))
    far = [s // 2 - s // 3 for s in steps]
    both = far[0] + far[1] + far[2] > 0
    up = 1 - lax.rem(steps[0] + steps[1] + steps[2], 2)
    return d, steps, far, both, up


def legs(steps, far, up):
    ahead = [f * (3 - 2 * up) for f in far]
    return ahead, [s + 4 - a for s, a in zip(steps, ahead)]


def far_count():
    return sum(2 in (d // 16, d // 4 % 4, d % 4) for d in range(1, CHIPS))


def remote(src, dst, send, recv, device):
    return pltpu.make_async_remote_copy(
        src_ref=src, dst_ref=dst, send_sem=send, recv_sem=recv, device_id=device,
        device_id_type=MESH,
    )


class Ring:
    def __init__(self, at, go, source, target, relay, send_sem, recv_sem, origin=0):
        self.at, self.go, self.source, self.target = at, go, source, target
        self.relay, self.send_sem, self.recv_sem, self.origin = relay, send_sem, recv_sem, origin

    def copy(self, src, dst, i, way):
        return remote(src, dst, self.send_sem.at[i], self.recv_sem.at[i], self.go(1 if way == 0 else 3))

    def by(self, d):
        return lax.rem(self.at + d, RING)

    def begin(self):
        for way in range(2):
            self.copy(self.source(self.by(2), way), self.relay(way), 4 + way, way).start()
        for way, d in ((0, 1), (1, 3)):
            self.copy(self.source(self.by(d), None), self.target(self.at, None), way, way).start()

    def begin_sent(self):
        for way in range(2):
            self.copy(self.source(self.by(2), way), self.relay(way), 4 + way, way).wait_send()
        for way, d in ((0, 1), (1, 3)):
            self.copy(self.source(self.by(d), None), self.target(self.at, None), way, way).wait_send()

    def forward(self):
        for way, d in ((0, 3), (1, 1)):
            held = self.relay(way)
            self.copy(held, held, 4 + way, way).wait_recv()
            self.copy(held, self.target(self.by(d), way), 2 + way, way).start()

    def forward_sent(self):
        for way, d in ((0, 3), (1, 1)):
            self.copy(self.relay(way), self.target(self.by(d), way), 2 + way, way).wait_send()

    def arrived(self):
        for way, d in ((0, 3), (1, 1)):
            part = self.target(self.by(d), None)
            self.copy(part, part, way, way).wait_recv()
        for way in range(2):
            part = self.target(self.by(2), way)
            self.copy(part, part, 2 + way, way).wait_recv()


def exchange_kernel(
    n_col, packed, table, got, got_table, a_one, a_two, t_one, t_two, a_relay_one,
    a_relay_two, a_relay_three, t_relay_one, t_relay_two, t_relay_three, l_one, l_two, l_relay_one,
    l_relay_two, l_relay_three, a_stage_one, a_stage_two, a_stage_three, t_stage, t_last, send_sems,
    recv_sems, hand_sems, own_sems,
):
    x, y, z, core = position()
    here = (x, y, z)
    sibling = place_of(x, y, z, 1 - core)
    barrier = pltpu.get_barrier_semaphore()

    def greet(at):
        pl.semaphore_signal(barrier, 1, device_id=at, device_id_type=MESH)

    greet(sibling)
    for axis in range(3):
        for d in (1, 3):
            for side in range(2):
                greet(place_of(*[here[i] + (d if i == axis else 0) for i in range(3)], side))
    pl.semaphore_wait(barrier, 13)

    def along(axis, to_core):
        def go(d):
            return place_of(*[here[i] + (d if i == axis else 0) for i in range(3)], to_core)

        return here[axis], go

    def along_mine(phase):
        axes = [lax.rem(phase + core, 3) == i for i in range(3)]
        picked = [axes[i].astype(jnp.int32) for i in range(3)]
        at = sum(p * h for p, h in zip(picked, here))
        return at, lambda d: place_of(*[h + d * p for p, h in zip(picked, here)], core)

    whole = slice(None)
    depth = packed.shape[4] // 2

    def half(ref_at, width):
        return lambda i, h: ref_at(i, pl.ds(0, 2 * width) if h is None else pl.ds(h * width, width))

    def arrays(which):
        if which < 0:
            return (
                (table, got_table, l_one, l_two, l_relay_one, l_relay_two, l_relay_three),
                whole, 18, 14,
            )
        return (
            (packed, got, a_one, a_two, a_relay_one, a_relay_two, a_relay_three),
            pl.ds(which * depth, depth), 9 * which, 7 * which,
        )

    def first_ring(kind, which):
        (src, end, one, two, relay, relay_two, relay_three), rows, sent, received = arrays(which)
        at, go = along(kind, kind)
        return Ring(
            at, go, half(lambda j, s: src.at[kind, j, s, whole, rows], 2),
            half(lambda i, s: one.at[i * 2 + core, s, whole, rows], 2),
            lambda way: relay.at[way, core, whole, whole, rows],
            send_sems.at[sent + kind], recv_sems.at[received + core],
        )

    def first_mine(origin, which):
        (src, end, one, two, relay, relay_two, relay_three), rows, sent, received = arrays(which)
        at, go = along_mine(0)
        return Ring(
            at, go, None, half(lambda i, s: one.at[i * 2 + origin, s, whole, rows], 2),
            lambda way: relay.at[way, origin, whole, whole, rows], send_sems.at[sent + 2 + origin],
            recv_sems.at[received + origin],
        )

    def second_ring(which):
        (src, end, one, two, relay, relay_two, relay_three), rows, sent, received = arrays(which)
        return Ring(
            *along_mine(1), half(lambda j, s: one.at[s, j, whole, rows], 4),
            half(lambda i, s: two.at[i, s, whole, rows], 4),
            lambda way: relay_two.at[way, whole, whole, rows],
            send_sems.at[sent + 4], recv_sems.at[received + 2],
        )

    def third_ring(which):
        (src, end, one, two, relay, relay_two, relay_three), rows, sent, received = arrays(which)
        return Ring(
            *along_mine(2), half(lambda j, s: two.at[s, whole, j, rows], 2),
            half(lambda i, s: end.at[i, s, whole, rows], 2),
            lambda way: relay_three.at[way, whole, whole, rows],
            send_sems.at[sent + 5], recv_sems.at[received + 3],
        )

    def shared_first(which):
        rows, sent, received = arrays(which)[1:]
        return Ring(
            *along(2, core), half(lambda j, s: packed.at[2, j, s, whole, rows], 2),
            half(lambda i, s: t_one.at[i, s, whole, rows], 2),
            lambda way: t_relay_one.at[way, whole, whole, rows],
            send_sems.at[sent + 6], recv_sems.at[received + 4],
        )

    def shared_second(which):
        rows, sent, received = arrays(which)[1:]

        def part(i, h):
            begin = lax.rem(i, 2) * 4
            taken = pl.ds(begin, 4) if h is None else pl.ds(begin + 2 * h, 2)
            return t_two.at[i // 2, taken, whole, rows]

        return Ring(
            *along(0, core), half(lambda j, s: t_one.at[s, j, whole, rows], 2), part,
            lambda way: t_relay_two.at[way, whole, whole, rows],
            send_sems.at[sent + 7], recv_sems.at[received + 5],
        )

    def shared_got(side, rows):
        def part(i, h):
            begin = lax.rem(i, 2) * 2
            taken = pl.ds(begin, 2) if h is None else pl.ds(begin + h, 1)
            return got.at[4 + side * 2 + i // 2, taken, whole, rows]

        return part

    def shared_third(which):
        rows, sent, received = arrays(which)[1:]
        return Ring(
            *along(1, core), half(lambda j, s: t_two.at[s, whole, j, rows], 1),
            shared_got(core, rows), lambda way: t_relay_three.at[way, whole, whole, rows],
            send_sems.at[sent + 8], recv_sems.at[received + 6],
        )

    class Keep:
        def __init__(self, ring, stage, i, which):
            sem = own_sems.at[which, i]
            kept = stage.at[whole, whole, arrays(which)[1]]
            self.load = pltpu.make_async_copy(ring.source(ring.at, None), kept, sem)
            self.store = pltpu.make_async_copy(kept, ring.target(ring.at, None), sem)

        def run(self):
            self.load.wait()
            self.store.start()

    def keep_line(ring):
        return pltpu.make_async_copy(
            ring.source(ring.at, None), ring.target(ring.at, None), own_sems.at[0, 6]
        )

    def to_sibling(kind, which):
        ring = first_ring(kind, which)
        return remote(
            ring.source(ring.at, None), ring.target(ring.at, None), hand_sems.at[0, 9 + which],
            hand_sems.at[1, 9 + which], sibling,
        )

    def hand(side, d, which):
        part = shared_got(side, arrays(which)[1])(lax.rem(y + d, RING), None)
        i = which * RING + d
        return remote(part, part, hand_sems.at[0, i], hand_sems.at[1, i], sibling)

    def by_core(kind, mine, other):
        pl.when(core == kind)(mine)
        pl.when(core != kind)(other)

    for kind in range(2):
        first_ring(kind, -1).begin()
        by_core(kind, keep_line(first_ring(kind, -1)).start, to_sibling(kind, -1).start)
    for which in range(2):
        first_ring(0, which).begin()
        first_ring(1, which).begin()
        shared_first(which).begin()
        for kind in range(2):
            by_core(
                kind, Keep(first_ring(kind, which), a_stage_one, 0, which).load.start,
                to_sibling(kind, which).start,
            )
        Keep(shared_first(which), t_stage.at[0], 1, which).load.start()
    for which in range(2):
        for kind in range(2):
            pl.when(core == kind)(Keep(first_ring(kind, which), a_stage_one, 0, which).run)
        Keep(shared_first(which), t_stage.at[0], 1, which).run()
    for origin in range(2):
        first_mine(origin, -1).forward()

    def first_done(which):
        for origin in range(2):
            first_mine(origin, which).arrived()
        for kind in range(2):

            def mine():
                if which < 0:
                    keep_line(first_ring(kind, which)).wait()
                else:
                    Keep(first_ring(kind, which), a_stage_one, 0, which).store.wait()
                to_sibling(kind, which).wait_recv()

            by_core(kind, mine, to_sibling(kind, which).wait_send)

    for which in range(2):
        for origin in range(2):
            first_mine(origin, which).forward()
        shared_first(which).forward()
    first_done(-1)
    second_ring(-1).begin()
    keep_line(second_ring(-1)).start()
    for which in range(2):
        first_done(which)
        second_ring(which).begin()
        Keep(second_ring(which), a_stage_two, 2, which).load.start()
        shared_first(which).arrived()
        Keep(shared_first(which), t_stage.at[0], 1, which).store.wait()
        shared_second(which).begin()
        Keep(shared_second(which), t_stage.at[1], 3, which).load.start()
        Keep(second_ring(which), a_stage_two, 2, which).run()
        Keep(shared_second(which), t_stage.at[1], 3, which).run()
    second_ring(-1).forward()
    for which in range(2):
        second_ring(which).forward()
        shared_second(which).forward()
    second_ring(-1).arrived()
    keep_line(second_ring(-1)).wait()
    third_ring(-1).begin()
    keep_line(third_ring(-1)).start()
    for which in range(2):
        shared_second(which).arrived()
        Keep(shared_second(which), t_stage.at[1], 3, which).store.wait()
        shared_third(which).begin()
        Keep(shared_third(which), t_last, 5, which).load.start()
        second_ring(which).arrived()
        Keep(second_ring(which), a_stage_two, 2, which).store.wait()
        third_ring(which).begin()
        Keep(third_ring(which), a_stage_three, 4, which).load.start()
        Keep(shared_third(which), t_last, 5, which).run()
        Keep(third_ring(which), a_stage_three, 4, which).run()
    third_ring(-1).forward()
    for which in range(2):
        shared_third(which).forward()
        third_ring(which).forward()
        Keep(shared_third(which), t_last, 5, which).store.wait()
        hand(core, 0, which).start()
    for which in range(2):
        shared_third(which).arrived()
        for d in range(1, RING):
            hand(core, d, which).start()
    for which in range(2):
        third_ring(which).arrived()
        Keep(third_ring(which), a_stage_three, 4, which).store.wait()
    third_ring(-1).arrived()
    keep_line(third_ring(-1)).wait()
    for which in range(2):
        for d in range(RING):
            hand(1 - core, d, which).wait_recv()
    for which in range(-1, 2):
        first_ring(0, which).begin_sent()
        first_ring(1, which).begin_sent()
        for origin in range(2):
            first_mine(origin, which).forward_sent()
        rings = [second_ring(which), third_ring(which)]
        if which >= 0:
            rings += [shared_first(which), shared_second(which), shared_third(which)]
            for d in range(RING):
                hand(core, d, which).wait_send()
        for ring in rings:
            ring.begin_sent()
            ring.forward_sent()


def exchange(packed, table, n_col):
    block, line = packed.shape[4:], table.shape[4:]

    def held(*shape):
        return jax.ShapeDtypeStruct(shape + block, packed.dtype)

    def lines(*shape):
        return jax.ShapeDtypeStruct(shape + line, table.dtype)

    def stage(*shape):
        return pltpu.VMEM(shape + block, packed.dtype)

    out_shape = (
        held(12, 4, 8), lines(4, 4, 8),
        held(8, 4, 4), held(4, 8, 4), held(4, 4, 4), held(2, 8, 4),
        held(2, 2, 2, 4), held(2, 4, 4), held(2, 2, 8), held(2, 2, 4), held(2, 2, 4), held(2, 1, 8),
        lines(8, 4, 4), lines(4, 8, 4), lines(2, 2, 2, 4), lines(2, 4, 4), lines(2, 2, 8),
    )
    return pl.pallas_call(
        functools.partial(exchange_kernel, n_col),
        out_shape=out_shape,
        in_specs=[HBM, HBM],
        out_specs=(HBM,) * len(out_shape),
        scratch_shapes=[
            stage(4, 4), stage(8, 4), stage(4, 8), stage(2, 4, 4), stage(2, 8),
            DMA((24, 6)), DMA((18, 6)), DMA((2, 11)), DMA((2, 7)),
        ],
        compiler_params=pltpu.CompilerParams(
            collective_id=2, has_side_effects=True, vmem_limit_bytes=LIMIT
        ),
        name="exchange",
    )(packed, table)[:2]


def last_place(got, side, at):
    x, y, z = at
    return got.at[8 + side * 2 + x // 2, lax.rem(x, 2) * 2 + y // 2, lax.rem(y, 2) * 4 + z]


def gather_kernel(
    spare, got_in, got, one, two, three, relay_one, relay_two, relay_three, send_sems, recv_sems,
    own_sems, out_sem, swap_sems,
):
    x, y, z, core = position()
    here = (x, y, z)
    sibling = place_of(x, y, z, 1 - core)
    whole = slice(None)
    lanes = spare.shape[1] // 2
    barrier = pltpu.get_barrier_semaphore()

    def along(axis):
        def go(d):
            return place_of(*[here[i] + (d if i == axis else 0) for i in range(3)], core)

        return here[axis], go

    def greet(at):
        pl.semaphore_signal(barrier, 1, device_id=at, device_id_type=MESH)

    for axis in range(3):
        for d in (1, 3):
            greet(along(axis)[1](d))
    pl.when(core == 1)(lambda: greet(sibling))
    pl.when(core == 1)(lambda: pl.semaphore_wait(barrier, 6))
    pl.when(core == 0)(lambda: pl.semaphore_wait(barrier, 7))

    def cols(h):
        return pl.ds(0, 2 * lanes) if h is None else pl.ds(h * lanes, lanes)

    def ring(p, phase):
        rows = pl.ds(48 * p, 48 if p < 2 else 32)
        at, go = along((p + phase) % 3)
        if phase == 0:
            source = lambda j, h: spare.at[rows, cols(h)]
            target = lambda i, h: one.at[i, rows, cols(h)]
            relay = lambda way: relay_one.at[way, rows]
        elif phase == 1:
            source = lambda j, h: one.at[whole, rows, cols(h)]
            target = lambda i, h: (
                two.at[i, whole, rows, cols(h)] if p == 2 else two.at[whole, i, rows, cols(h)]
            )
            relay = lambda way: relay_two.at[way, whole, rows]
        else:
            source = lambda j, h: two.at[whole, whole, rows, cols(h)]
            target = lambda i, h: (
                three.at[whole, whole, i, rows, cols(h)] if p == 0
                else three.at[i, whole, whole, rows, cols(h)] if p == 1
                else three.at[whole, i, whole, rows, cols(h)]
            )
            relay = lambda way: relay_three.at[way, whole, whole, rows]
        k = 3 * phase + p
        return Ring(at, go, source, target, relay, send_sems.at[k], recv_sems.at[k])

    def own(p, phase):
        r = ring(p, phase)
        return pltpu.make_async_copy(
            r.source(r.at, None), r.target(r.at, None), own_sems.at[3 * phase + p]
        )

    for phase in range(3):
        for p in range(3):
            if phase > 0:
                ring(p, phase - 1).arrived()
                own(p, phase - 1).wait()
            ring(p, phase).begin()
            own(p, phase).start()
        for p in range(3):
            ring(p, phase).forward()
    for p in range(3):
        ring(p, 2).arrived()
        own(p, 2).wait()

    def pieces(side):
        for i in range(RING):
            for j in range(RING):
                dst = got.at[8 + side * 2 + i // 2, i % 2 * 2 + j // 2, pl.ds(j % 2 * 4, 4)]
                yield three.at[i, j], dst

    half = got.at[pl.ds(8, 2)]

    @pl.when(core == 0)
    def _():
        for src, dst in pieces(0):
            remote(src, dst, swap_sems.at[0], swap_sems.at[1], sibling).start()
        pltpu.make_async_copy(half, half, swap_sems.at[0]).wait()

    @pl.when(core == 1)
    def _():
        for src, dst in pieces(1):
            pltpu.make_async_copy(src, dst, out_sem).start()
        pltpu.make_async_copy(half, half, out_sem).wait()
        pltpu.make_async_copy(half, half, swap_sems.at[1]).wait()

    for phase in range(3):
        for p in range(3):
            ring(p, phase).begin_sent()
            ring(p, phase).forward_sent()


def gather_last(spare, got):
    depth, size = spare.shape

    def held(*shape):
        return pltpu.VMEM(shape + (depth, size), spare.dtype)

    def relays(*shape):
        return pltpu.VMEM((2,) + shape + (depth, size // 2), spare.dtype)

    return pl.pallas_call(
        gather_kernel,
        out_shape=jax.ShapeDtypeStruct(got.shape, got.dtype),
        in_specs=[HBM, HBM],
        out_specs=HBM,
        input_output_aliases={1: 0},
        scratch_shapes=[
            held(4), held(4, 4), held(4, 4, 4), relays(), relays(4), relays(4, 4),
            DMA((9, 6)), DMA((9, 6)), DMA((9,)), DMA, DMA((2,)),
        ],
        compiler_params=pltpu.CompilerParams(
            collective_id=4, has_side_effects=True, vmem_limit_bytes=LIMIT
        ),
        name="gather_last",
    )(spare, got)


def last_kernel(n_row, n_col, packed, got_in, got, relay, sems, relay_sem, own_sem):
    devices = n_row * n_col
    x, y, z, core = position()
    mine = place_of(x, y, z, core)
    me = mine[0] * n_col + mine[1]
    barrier = pltpu.get_barrier_semaphore()

    def at_step(steps, core):
        return place_of(x + steps[0], y + steps[1], z + steps[2], core)

    def number(device):
        return device[0] * n_col + device[1]

    def greet(at):
        pl.semaphore_signal(barrier, 1, device_id=at, device_id_type=MESH)

    def near(k, carry):
        d, steps, far, both, up = step_of(k)

        @pl.when(jnp.logical_and(core == 1, jnp.logical_not(both)))
        def _():
            greet(at_step(steps, 0))
            greet(at_step(steps, 1))

        return carry

    def relayed(k, carry):
        bits = (k // 8, lax.rem(k // 4, 2), lax.rem(k // 2, 2))
        way = lax.rem(k, 2)

        @pl.when(jnp.logical_and(core == 0, k != 15))
        def _():
            greet(at_step([b * (3 - 2 * way) for b in bits], 0))

        return carry

    lax.fori_loop(1, CHIPS, near, 0)
    lax.fori_loop(2, 16, relayed, 0)

    @pl.when(core == 1)
    def _():
        greet(place_of(x, y, z, 0))
        pl.semaphore_wait(barrier, 26)

    @pl.when(core == 0)
    def _():
        pl.semaphore_wait(barrier, 26 + 13 + 1)

    def block_for(target):
        chip = number(target) // 2
        return packed.at[3, chip // 16, lax.rem(chip // 4, 4), lax.rem(chip, 4)]

    def landing(steps, side):
        return last_place(got, side, [lax.rem(h + s, RING) for h, s in zip((x, y, z), steps)])

    def first_leg(k, carry):
        d, steps, far, both, up = step_of(k)

        @pl.when(both)
        def _():
            first, second = legs(steps, far, up)
            remote(
                block_for(at_step(steps, 1)), relay.at[d], sems.at[0], relay_sem.at[d],
                at_step(first, core),
            ).start()

        return carry

    def direct(k, carry):
        d, steps, far, both, up = step_of(k)

        @pl.when(jnp.logical_not(both))
        def _():
            target = at_step(steps, 1)
            remote(block_for(target), landing((0, 0, 0), core), sems.at[0], sems.at[1], target).start()

        return carry

    def second_leg(k, carry):
        d, steps, far, both, up = step_of(k)

        @pl.when(both)
        def _():
            first, second = legs(steps, far, up)
            target = at_step(second, 1)
            held = relay.at[d]
            remote(held, held, sems.at[2], relay_sem.at[d], target).wait_recv()
            remote(held, landing([4 - f for f in first], core), sems.at[2], sems.at[1], target).start()

        return carry

    lax.fori_loop(1, CHIPS, first_leg, 0)
    lax.fori_loop(1, CHIPS, direct, 0)
    lax.fori_loop(1, CHIPS, second_leg, 0)

    def settle(ref, count, sem):
        part = ref.at[pl.ds(0, count)]
        pltpu.make_async_copy(part, part, sem).wait()

    settle(relay, far_count(), sems.at[2])

    @pl.when(core == 0)
    def _():
        to = place_of(x, y, z, 1)
        remote(block_for(to), landing((0, 0, 0), core), sems.at[0], sems.at[1], to).start()
        settle(relay, CHIPS, sems.at[0])

    @pl.when(core == 1)
    def _():
        own = pltpu.make_async_copy(block_for(mine), landing((0, 0, 0), core), own_sem)
        own.start()
        own.wait()
        settle(relay, CHIPS - 1, sems.at[0])
        settle(relay, devices - 1, sems.at[1])


def exchange_last(packed, got, n_row, n_col):
    return pl.pallas_call(
        functools.partial(last_kernel, n_row, n_col),
        out_shape=(
            jax.ShapeDtypeStruct(got.shape, got.dtype),
            jax.ShapeDtypeStruct((2 * CHIPS,) + packed.shape[4:], packed.dtype),
        ),
        in_specs=[HBM, HBM],
        out_specs=(HBM, HBM),
        input_output_aliases={1: 0},
        scratch_shapes=[DMA((3,)), DMA((CHIPS,)), DMA],
        compiler_params=pltpu.CompilerParams(collective_id=3, has_side_effects=True),
        name="exchange_last",
    )(packed, got)[0]


def fetch_target(t, at, total, counts, order, base, got, buffer, sem):
    base[t] = at

    def one(e, c):
        pltpu.make_async_copy(got.at[order[t, e]], buffer.at[at + e], sem).start()
        return c

    lax.fori_loop(0, counts[t, 0], one, 0)
    return at + counts[t, 0]


def await_target(t, counts, got, buffer, sem):
    def one(e, c):
        pltpu.make_async_copy(got.at[0], buffer.at[0], sem).wait()
        return c

    lax.fori_loop(0, counts[t, 0], one, 0)


def product(t, e, counts, base, buffer):
    rank = buffer.shape[1] // 2
    n, begin = counts[t, 0], base[t]
    picked = [
        jnp.where(e * STACK + k < n, begin + e * STACK + k, buffer.shape[0] - 1) for k in range(STACK)
    ]
    lefts = jnp.concatenate([buffer[s, 0:rank, :] for s in picked], axis=0)
    rights = jnp.concatenate([buffer[s, rank:, :] for s in picked], axis=0)
    return dot(lefts, rights, ((0,), (0,)))


def add_rest(t, counts, base, buffer, sum_ref, rows, cols):
    def chunk(e, c):
        sum_ref[rows, cols] += product(t, e, counts, base, buffer)
        return c

    lax.fori_loop(1, (counts[t, 0] + STACK - 1) // STACK, chunk, 0)


def split(x):
    high = x.astype(jnp.bfloat16)
    return high, (x - high.astype(jnp.float32)).astype(jnp.bfloat16)


def dot3(a, b):
    a_high, a_low = split(a)
    b_high, b_low = split(b)
    return dot(a_high, b_high) + (dot(a_high, b_low) + dot(a_low, b_high))


def permutation(pivots):
    size = pivots.shape[1]
    places = lax.broadcasted_iota(jnp.int32, (size, size), 0)
    return (places == pivots).astype(jnp.float32)


def panel_kernel(
    total, table, got, front, pivots, upper_inverse, lower_inverse, column_basis, row_basis,
    column_ranks, row_ranks, a_out, b_out, counts, order, left_sum, top_sum, buffer, top_weights,
    left_weights, coupling, order_rows, count_rows, base, sem, front_sem, sort_sem,
):
    size, rank = upper_inverse.shape[0], column_basis.shape[0]
    row_blocks, col_blocks = front.shape[0] // size, front.shape[1] // size
    targets = row_blocks * col_blocks
    devices = total // CAP
    is_top, is_left = lax.axis_index("row") == 0, lax.axis_index("col") == 0
    load_left = pltpu.make_async_copy(front.at[:, pl.ds(0, size)], left_sum, front_sem.at[0])
    load_top = pltpu.make_async_copy(front.at[pl.ds(0, size)], top_sum, front_sem.at[1])
    pl.when(is_left)(load_left.start)
    pl.when(is_top)(load_top.start)

    core = lax.rem(lax.axis_index("col"), 2)
    k = lax.broadcasted_iota(jnp.int32, (1, devices), 1)
    high, middle, low, side = k >> 5, (k >> 3) & 3, (k >> 1) & 3, k & 1
    x, y, z = (jnp.where(core == 0, a, b) for a, b in ((low, high), (middle, low), (high, middle)))
    shared = devices + side * CHIPS + y * 16 + x * 4 + z
    last = 2 * devices + side * CHIPS + x * 16 + y * 4 + z
    block = jnp.concatenate([k, shared, last], axis=1)
    target = jnp.concatenate([table[p : p + 1, :] for p in range(3)], axis=1)
    entries = block.shape[1]
    member = lax.broadcasted_iota(jnp.int32, (targets, entries), 0) == target
    member_one = member.astype(jnp.float32)
    before = (
        lax.broadcasted_iota(jnp.int32, (entries, entries), 0)
        < lax.broadcasted_iota(jnp.int32, (entries, entries), 1)
    ).astype(jnp.bfloat16)
    earlier = dot(member_one.astype(jnp.bfloat16), before)
    rank_of = jnp.sum(jnp.where(member, earlier, 0.0), axis=0, keepdims=True)
    chosen = lax.broadcasted_iota(jnp.int32, (total, entries), 0) == rank_of.astype(jnp.int32)
    upper_part = jnp.where(member, (block >> 7).astype(jnp.float32), 0.0).astype(jnp.bfloat16)
    lower_part = jnp.where(member, (block & 127).astype(jnp.float32), 0.0).astype(jnp.bfloat16)
    chosen = chosen.astype(jnp.float32).astype(jnp.bfloat16)
    listed = dot(upper_part, chosen, ((1,), (1,))) * 128.0 + dot(lower_part, chosen, ((1,), (1,)))
    order_rows[...] = listed.astype(jnp.int32)
    tally = jnp.sum(member_one, axis=1, keepdims=True).astype(jnp.int32)
    count_rows[...] = jnp.broadcast_to(tally, count_rows.shape)
    copies = (
        pltpu.make_async_copy(order_rows, order, sort_sem.at[0]),
        pltpu.make_async_copy(count_rows, counts, sort_sem.at[1]),
    )
    for copy in copies:
        copy.start()
    for copy in copies:
        copy.wait()

    @pl.when(jnp.logical_or(is_top, is_left))
    def _():
        buffer[buffer.shape[0] - 1] = jnp.zeros(buffer.shape[1:], buffer.dtype)

        def fetch(t, at):
            return fetch_target(t, at, total, counts, order, base, got, buffer, sem)

        def fetch_left(i, at):
            return fetch(i * col_blocks, at)

        at = lax.fori_loop(0, jnp.where(is_left, row_blocks, 0), fetch_left, 0)
        lax.fori_loop(jnp.where(is_left, 1, 0), jnp.where(is_top, col_blocks, 0), fetch, at)

    @pl.when(is_top)
    def _():
        weights = dot(row_basis[...], lower_inverse[...], precision=HIGHEST)
        weights = dot(weights, permutation(pivots[...]), ((1,), (1,)), precision=HIGHEST)
        top_weights[0:rank] = weights
        top_weights[rank:] = weights

    @pl.when(is_left)
    def _():
        left_weights[...] = dot(
            upper_inverse[...], column_basis[...], ((1,), (1,)), precision=HIGHEST
        )
        coupled = dot(column_basis[...], row_basis[...], ((1,), (1,)), precision=HIGHEST)
        coupling[...] = jnp.concatenate([coupled, coupled], axis=1)

    @pl.when(jnp.logical_or(is_top, is_left))
    def _():
        def ready(t):
            await_target(t, counts, got, buffer, sem)

        def ready_left(i, c):
            ready(i * col_blocks)
            return c

        def ready_top(t, c):
            ready(t)
            return c

        lax.fori_loop(0, jnp.where(is_left, row_blocks, 0), ready_left, 0)
        lax.fori_loop(jnp.where(is_left, 1, 0), jnp.where(is_top, col_blocks, 0), ready_top, 0)

    @pl.when(is_top)
    def _():
        row = lax.broadcasted_iota(jnp.int32, (2 * rank, size), 0)
        load_top.wait()
        for j in range(col_blocks):
            cols = slice(j * size, (j + 1) * size)
            top_sum[:, cols] += product(j, 0, counts, base, buffer)
        for j in range(col_blocks):
            add_rest(j, counts, base, buffer, top_sum, slice(0, size), slice(j * size, (j + 1) * size))
        for j in range(col_blocks):
            cols = slice(j * size, (j + 1) * size)
            factor = dot3(top_weights[...], top_sum[:, cols])
            factor = jnp.where(lax.rem(row, rank) < row_ranks[j], factor, 0.0)
            high, low = split(factor)
            value = jnp.where(row < rank, high.astype(jnp.float32), low.astype(jnp.float32))
            for h in range(size // 128):
                b_out[j * (size // 128) + h] = value[:, h * 128 : (h + 1) * 128].astype(jnp.bfloat16)

    @pl.when(is_left)
    def _():
        lane = lax.broadcasted_iota(jnp.int32, (size, 2 * rank), 1)
        load_left.wait()

        def add(i, c):
            rows = pl.ds(pl.multiple_of(i * size, size), size)
            left_sum[rows, :] += product(i * col_blocks, 0, counts, base, buffer)
            return c

        lax.fori_loop(0, row_blocks, add, 0, unroll=4)

        def add_more(i, c):
            rows = pl.ds(pl.multiple_of(i * size, size), size)
            add_rest(i * col_blocks, counts, base, buffer, left_sum, rows, slice(0, size))
            return c

        lax.fori_loop(0, row_blocks, add_more, 0)

        def block(i, c):
            rows = pl.ds(pl.multiple_of(i * size, size), size)
            factor = dot3(left_sum[rows, :], left_weights[...])
            factor = jnp.where(lane[:, 0:rank] < column_ranks[i], factor, 0.0)
            high, low = split(dot3(factor, coupling[...]))
            value = jnp.where(lane < rank, high.astype(jnp.float32), low.astype(jnp.float32))
            for h in range(size // 128):
                a_out[i * (size // 128) + h] = value[h * 128 : (h + 1) * 128].astype(jnp.bfloat16)
            return c

        lax.fori_loop(0, row_blocks, block, 0, unroll=4)


def panel(
    table, got, front, pivots, upper_inverse, lower_inverse, column_basis, row_basis, column_ranks,
    row_ranks,
):
    depth, size = got.shape[1:]
    total = table.shape[1] * CAP
    rows, cols = front.shape
    targets = (rows // size) * (cols // size)
    return pl.pallas_call(
        functools.partial(panel_kernel, total),
        out_shape=(
            jax.ShapeDtypeStruct((rows // 128, 128, 128), jnp.bfloat16),
            jax.ShapeDtypeStruct((cols // 128, 128, 128), jnp.bfloat16),
            jax.ShapeDtypeStruct((targets, 128), jnp.int32),
            jax.ShapeDtypeStruct((targets, total), jnp.int32),
        ),
        in_specs=[VMEM, HBM, HBM, VMEM, VMEM, VMEM, VMEM, VMEM, SMEM, SMEM],
        out_specs=(VMEM, VMEM, SMEM, SMEM),
        scratch_shapes=[
            pltpu.VMEM((rows, size), jnp.float32),
            pltpu.VMEM((size, cols), jnp.float32),
            pltpu.VMEM((total + 1, depth, size), jnp.bfloat16),
            pltpu.VMEM((depth, size), jnp.float32),
            pltpu.VMEM((size, depth // 2), jnp.float32),
            pltpu.VMEM((depth // 2, depth), jnp.float32),
            pltpu.VMEM((targets, total), jnp.int32),
            pltpu.VMEM((targets, 128), jnp.int32),
            pltpu.SMEM((targets,), jnp.int32),
            DMA,
            DMA((2,)),
            DMA((2,)),
        ],
        compiler_params=pltpu.CompilerParams(vmem_limit_bytes=LIMIT),
        name="panel",
    )(
        table, got, front, pivots, upper_inverse, lower_inverse, column_basis, row_basis,
        column_ranks, row_ranks,
    )


def spread_kernel(
    n_row, n_col, a_src, b_src, a_all, b_all, a_part_send, a_part_recv, b_part_send, b_part_recv,
    a_send, a_recv, b_send, b_recv, swap_sem, own_sem,
):
    r, c = lax.axis_index("row"), lax.axis_index("col")
    half = n_col // 2
    chip, core = c // 2, lax.rem(c, 2)
    sibling = (r, chip * 2 + 1 - core)
    barrier = pltpu.get_barrier_semaphore()

    def mates(n, me, body):
        def one(k, carry):
            body(lax.rem(me + k, n))
            return carry

        lax.fori_loop(1, n, one, 0)

    mates(n_col, c, lambda o: pl.semaphore_signal(barrier, 1, device_id=(r, o), device_id_type=MESH))
    mates(n_row, r, lambda o: pl.semaphore_signal(barrier, 1, device_id=(o, c), device_id_type=MESH))
    pl.semaphore_wait(barrier, n_col + n_row - 2)

    def piece(o):
        return lax.rem(o, 2) * half + o // 2

    def a_part(o):
        return remote(a_src.at[piece(o)], a_all.at[piece(o)], a_part_send.at[o], a_part_recv, (r, o))

    def b_part(o):
        return remote(b_src.at[o], b_all.at[o], b_part_send.at[o], b_part_recv, (o, c))

    def a_full(h):
        at = piece(c)
        return remote(a_all.at[at], a_all.at[at], a_send.at[h], a_recv.at[chip], (r, h * 2 + core))

    def a_from(h):
        at = core * half + h
        return remote(a_all.at[at], a_all.at[at], a_send.at[h], a_recv.at[h], (r, h * 2 + core))

    def b_full(o):
        return remote(b_all.at[r], b_all.at[r], b_send.at[o], b_recv.at[r], (o, c))

    def b_from(o):
        return remote(b_all.at[o], b_all.at[o], b_send.at[o], b_recv.at[o], (o, c))

    def swap(side):
        part = a_all.at[pl.ds(side * half, half)]
        return remote(part, part, swap_sem.at[0], swap_sem.at[1], sibling)

    own_a = pltpu.make_async_copy(a_src.at[0], a_all.at[0], own_sem.at[0])
    own_b = pltpu.make_async_copy(b_src.at[0], b_all.at[0], own_sem.at[1])

    @pl.when(c == 0)
    def _():
        own_a.start()
        mates(n_col, c, lambda o: a_part(o).start())

    @pl.when(r == 0)
    def _():
        own_b.start()
        mates(n_row, r, lambda o: b_part(o).start())

    pl.when(c == 0)(own_a.wait)
    pl.when(c != 0)(lambda: a_part(c).wait_recv())
    mates(half, chip, lambda h: a_full(h).start())
    pl.when(r == 0)(own_b.wait)
    pl.when(r != 0)(lambda: b_part(r).wait_recv())
    mates(n_row, r, lambda o: b_full(o).start())
    mates(half, chip, lambda h: a_from(h).wait_recv())
    swap(core).start()
    mates(n_row, r, lambda o: b_from(o).wait_recv())
    swap(1 - core).wait_recv()
    mates(half, chip, lambda h: a_full(h).wait_send())
    mates(n_row, r, lambda o: b_full(o).wait_send())
    swap(core).wait_send()

    @pl.when(c == 0)
    def _():
        mates(n_col, c, lambda o: a_part(o).wait_send())

    @pl.when(r == 0)
    def _():
        mates(n_row, r, lambda o: b_part(o).wait_send())


def spread(a_src, b_src, n_row, n_col):
    return pl.pallas_call(
        functools.partial(spread_kernel, n_row, n_col),
        out_shape=(
            jax.ShapeDtypeStruct(a_src.shape, a_src.dtype),
            jax.ShapeDtypeStruct(b_src.shape, b_src.dtype),
        ),
        in_specs=[VMEM, VMEM],
        out_specs=(VMEM, VMEM),
        scratch_shapes=[
            DMA((n_col,)), DMA, DMA((n_row,)), DMA,
            DMA((n_col // 2,)), DMA((n_col // 2,)), DMA((n_row,)), DMA((n_row,)), DMA((2,)), DMA((2,)),
        ],
        compiler_params=pltpu.CompilerParams(collective_id=1, has_side_effects=True),
        name="spread",
    )(a_src, b_src)


def finish_kernel(
    total, counts, order, got, front, a_all, b_all, pivots, upper_inverse, lower_inverse, out,
    extended, buffer, b_cat, inverse_parts, corner, base, sem, front_sem, out_sem,
):
    size = upper_inverse.shape[0]
    row_blocks, col_blocks = front.shape[0] // size, front.shape[1] // size
    lanes = a_all.shape[2]
    rank = lanes // 2
    pieces = size // lanes
    is_top, is_left = lax.axis_index("row") == 0, lax.axis_index("col") == 0

    def rows(i):
        return pl.ds(pl.multiple_of(i * size, size), size)

    def load(i):
        return pltpu.make_async_copy(front.at[rows(i)], extended.at[rows(i)], front_sem.at[i])

    def store(i):
        return pltpu.make_async_copy(extended.at[rows(i)], out.at[rows(i)], out_sem.at[i])

    load(0).start()

    def fetch(i, at):
        for j in range(col_blocks):
            at = fetch_target(
                i * col_blocks + j, at, total, counts, order, base, got, buffer, sem.at[i]
            )
        pl.when(i + 1 < row_blocks)(lambda: load(i + 1).start())
        return at

    lax.fori_loop(0, row_blocks, fetch, 0)
    buffer[buffer.shape[0] - 1] = jnp.zeros(buffer.shape[1:], buffer.dtype)

    @pl.when(is_left)
    def _():
        high, low = split(upper_inverse[...])
        inverse_parts[0:size] = high
        inverse_parts[size : 2 * size] = low
        inverse_parts[2 * size :] = high

    for k in range(b_all.shape[0]):
        cols = slice(k * lanes, (k + 1) * lanes)
        high, low = b_all[k, 0:rank, :], b_all[k, rank:, :]
        if k < pieces:
            high = jnp.where(is_left, jnp.zeros_like(high), high)
            low = jnp.where(is_left, jnp.zeros_like(low), low)
        for h in range(2):
            b_cat[h * rank : (h + 1) * rank, cols] = high
            b_cat[(2 + h) * rank : (3 + h) * rank, cols] = low

    def step(i, c):
        load(i).wait()
        for j in range(col_blocks):
            await_target(i * col_blocks + j, counts, got, buffer, sem.at[i])
        a = jnp.concatenate([a_all[i * pieces + k] for k in range(pieces)], axis=0)
        a = jnp.concatenate([a, a], axis=1)
        a = jnp.where(jnp.logical_and(is_top, i == 0), jnp.zeros_like(a), a)
        for j in range(col_blocks):
            cols = slice(j * size, (j + 1) * size)
            added = product(i * col_blocks + j, 0, counts, base, buffer)
            extended[rows(i), cols] += added - dot(a, b_cat[:, cols])
        for j in range(col_blocks):
            cols = slice(j * size, (j + 1) * size)
            add_rest(i * col_blocks + j, counts, base, buffer, extended, rows(i), cols)

        @pl.when(jnp.logical_and(is_left, jnp.logical_not(jnp.logical_and(is_top, i == 0))))
        def _():
            high, low = split(extended[rows(i), 0:size])
            extended[rows(i), 0:size] = dot(
                jnp.concatenate([high, high, low], axis=1), inverse_parts[...]
            )

        @pl.when(jnp.logical_and(is_top, i == 0))
        def _():
            permute = permutation(pivots[...])
            corner[...] = dot(permute, extended[0:size, 0:size], ((0,), (0,)), precision=HIGHEST)
            weights = dot(lower_inverse[...], permute, ((1,), (1,)), precision=HIGHEST)
            for j in range(col_blocks):
                cols = slice(j * size, (j + 1) * size)
                upper = dot(weights, extended[0:size, cols], precision=HIGHEST)
                if j == 0:
                    upper = jnp.where(is_left, corner[...], upper)
                extended[0:size, cols] = upper

        store(i).start()
        return c

    lax.fori_loop(0, row_blocks, step, 0)
    for i in range(row_blocks):
        store(i).wait()


def finish(counts, order, got, front, a_all, b_all, pivots, upper_inverse, lower_inverse, total):
    depth, size = got.shape[1:]
    rows, cols = front.shape
    row_blocks = rows // size
    targets = row_blocks * (cols // size)
    return pl.pallas_call(
        functools.partial(finish_kernel, total),
        out_shape=jax.ShapeDtypeStruct(front.shape, jnp.float32),
        in_specs=[SMEM, SMEM, HBM, HBM, VMEM, VMEM, VMEM, VMEM, VMEM],
        out_specs=HBM,
        scratch_shapes=[
            pltpu.VMEM(front.shape, jnp.float32),
            pltpu.VMEM((total + 1, depth, size), jnp.bfloat16),
            pltpu.VMEM((2 * depth, cols), jnp.bfloat16),
            pltpu.VMEM((3 * size, size), jnp.bfloat16),
            pltpu.VMEM((size, size), jnp.float32),
            pltpu.SMEM((targets,), jnp.int32),
            DMA((row_blocks,)), DMA((row_blocks,)), DMA((row_blocks,)),
        ],
        compiler_params=pltpu.CompilerParams(vmem_limit_bytes=LIMIT),
        name="finish",
    )(counts, order, got, front, a_all, b_all, pivots, upper_inverse, lower_inverse)


def shards(
    front, child_left, child_right, child_owner, child_slot, pivots, upper_inverse, lower_inverse,
    column_basis, row_basis, column_ranks, row_ranks,
):
    n_row, n_col = lax.axis_size("row"), lax.axis_size("col")
    devices = n_row * n_col
    packed, table, spare = pack(
        child_owner[:, 0], child_slot, jnp.swapaxes(child_left, 1, 2), child_right, devices
    )
    packed = packed.reshape((4, RING, RING, RING) + packed.shape[1:])
    table = table.reshape((2, RING, RING, RING) + table.shape[1:])
    got, got_table = exchange(packed, table, n_col)
    got_table = got_table.reshape((devices,) + got_table.shape[3:])
    lines = got_table[:, 0, 0:8].T
    most = jnp.max(lines, axis=1)
    once, often = (most[3] == 1).astype(jnp.int32), (most[3] > 1).astype(jnp.int32)
    got = lax.fori_loop(0, once, lambda i, g: gather_last(spare, g), got)
    got = lax.fori_loop(0, often, lambda i, g: exchange_last(packed, g, n_row, n_col), got)
    got = got.reshape((3 * devices,) + got.shape[3:])
    a_src, b_src, counts, order = panel(
        lines, got, front, pivots[None, :], upper_inverse, lower_inverse, column_basis.T,
        row_basis.T, column_ranks, row_ranks,
    )
    a_all, b_all = spread(a_src, b_src, n_row, n_col)
    return finish(
        counts, order, got, front, a_all, b_all, pivots[None, :], upper_inverse, lower_inverse,
        devices * CAP,
    )


def solution(mesh):
    in_specs = (
        P("row", "col"),
        P(("row", "col"), None, None),
        P(("row", "col"), None, None),
        P(("row", "col"), None),
        P(("row", "col")),
        P(),
        P(),
        P(),
        P(),
        P(),
        P("row"),
        P("col"),
    )
    out_specs = P("row", "col")
    return jax.shard_map(shards, mesh=mesh, in_specs=in_specs, out_specs=out_specs, check_vma=False)
```

```python
import functools

import jax
import jax.numpy as jnp
from jax import lax
from jax.experimental import pallas as pl
from jax.experimental.pallas import tpu as pltpu
from jax.sharding import PartitionSpec as P

MESH = pl.DeviceIdType.MESH
HBM = pl.BlockSpec(memory_space=pl.ANY)
SMEM = pl.BlockSpec(memory_space=pltpu.SMEM)
VMEM = pl.BlockSpec(memory_space=pltpu.VMEM)
DMA = pltpu.SemaphoreType.DMA
CAP = 2
STACK = 4
STRIDE = 37
RING = 4
CHIPS = RING**3
LEAD = 16
LIMIT = 56 * 1024 * 1024
HIGHEST = lax.Precision.HIGHEST


def dot(a, b, dims=((1,), (0,)), precision=None):
    return lax.dot_general(
        a, b, (dims, ((), ())), precision=precision, preferred_element_type=jnp.float32
    )


def pack_kernel(
    devices, owner, owner_row, slot_row, left, right, packed, table, spare, staged, named, placed,
    used, in_sem, out_sem, spare_sem,
):
    count, rank = left.shape[0], left.shape[1]
    chips = devices // 2
    chunks = in_sem.shape[0]
    each = count // chunks

    def load(k):
        part = pl.ds(k * each, each)
        return (
            pltpu.make_async_copy(left.at[part], staged.at[part, pl.ds(0, rank)], in_sem.at[k, 0]),
            pltpu.make_async_copy(right.at[part], staged.at[part, pl.ds(rank, rank)], in_sem.at[k, 1]),
        )

    for k in range(chunks):
        for copy in load(k):
            copy.start()

    def clear(o, c):
        named[o] = 0
        placed[o] = 0
        return c

    lax.fori_loop(0, devices, clear, 0, unroll=8)
    used[0] = 0

    def tally(i, c):
        named[owner[i]] += 1
        return c

    lax.fori_loop(0, count, tally, 0, unroll=4)

    for k in range(chunks):
        for copy in load(k):
            copy.wait()

        def send(i, c):
            o = owner[i]
            p = placed[o]
            placed[o] = 1
            core = o & 1
            x, y, z = o >> 5, (o >> 2) & 3, (o & 2) | ((o >> 4) & 1)
            late = jnp.logical_and(core == 1, named[o - core] == 2)
            first = jnp.where(core == 0, x * 16 + y * 4 + z, chips + y * 16 + z * 4 + x)
            second = 2 * chips + z * 16 + x * 4 + y
            extra = jnp.where(late, 3 * chips + (o >> 1), second)
            at = jnp.where(p == 0, first, extra)
            pltpu.make_async_copy(staged.at[i], packed.at[at], out_sem).start()

            @pl.when(jnp.logical_and(jnp.logical_and(late, p != 0), used[0] == 0))
            def _():
                pltpu.make_async_copy(staged.at[i], spare, spare_sem).start()
                used[0] = 1

            return c

        lax.fori_loop(k * each, (k + 1) * each, send, 0)

    shape = (devices, 1, count)
    place = lax.broadcasted_iota(jnp.int32, shape, 2)
    line = lax.broadcasted_iota(jnp.int32, shape, 0)
    core = line >> 6
    high, middle, low = (line >> 4) & 3, (line >> 2) & 3, line & 3
    x, y, z = (jnp.where(core == 0, a, b) for a, b in ((high, low), (middle, high), (low, middle)))
    device = x * 32 + (z & 1) * 16 + y * 4 + (z & 2) + core
    owners = owner_row[...][None]
    code = (place * 64 + slot_row[...][None]).astype(jnp.float32)

    def ends(which):
        least = jnp.min(jnp.where(which, code, 65536.0), axis=2, keepdims=True)
        most = jnp.max(jnp.where(which, code, -1.0), axis=2, keepdims=True)
        return least, most

    least, most = ends(owners == device)
    low_least, low_most = ends(owners == device - (device & 1))
    core = core[:, :, 0:1]
    first = jnp.where(most >= 0.0, least.astype(jnp.int32) & 63, -1)
    second = jnp.where(most > least, most.astype(jnp.int32) & 63, -1)
    late = jnp.logical_and(core == 1, low_most > low_least)
    last = jnp.where(late, second, -1)
    flag = jnp.sum(jnp.where(last >= 0, 1.0, 0.0), axis=0, keepdims=True).astype(jnp.int32)
    lane = lax.broadcasted_iota(jnp.int32, table.shape, 2)
    line = jnp.where(lane == 0, first, jnp.where(lane == 1, jnp.where(late, -1, second), -1))
    table[...] = jnp.where(lane == 2, last, jnp.where(lane == 3, flag, line))

    pltpu.make_async_copy(staged, packed.at[pl.ds(0, count)], out_sem).wait()
    pl.when(used[0] == 1)(pltpu.make_async_copy(staged.at[0], spare, spare_sem).wait)


def pack(owner, slots, left, right, devices):
    count, rank, size = left.shape
    return pl.pallas_call(
        functools.partial(pack_kernel, devices),
        out_shape=(
            jax.ShapeDtypeStruct((2 * devices, 2 * rank, size), left.dtype),
            jax.ShapeDtypeStruct((devices, 1, 128), jnp.int32),
            jax.ShapeDtypeStruct((2 * rank, size), left.dtype),
        ),
        in_specs=[SMEM, VMEM, VMEM, HBM, HBM],
        out_specs=(HBM, VMEM, HBM),
        scratch_shapes=[
            pltpu.VMEM((count, 2 * rank, size), left.dtype),
            pltpu.SMEM((devices,), jnp.int32),
            pltpu.SMEM((devices,), jnp.int32),
            pltpu.SMEM((1,), jnp.int32),
            DMA((4, 2)),
            DMA,
            DMA,
        ],
        compiler_params=pltpu.CompilerParams(vmem_limit_bytes=LIMIT),
        name="pack",
    )(owner, owner[None, :], slots[None, :], left, right)


def position():
    r, q = lax.axis_index("row"), lax.axis_index("col")
    return r // 2, q // 4, lax.rem(q // 2, 2) * 2 + lax.rem(r, 2), lax.rem(q, 2)


def place_of(x, y, z, core):
    x, y, z = lax.rem(x, RING), lax.rem(y, RING), lax.rem(z, RING)
    return x * 2 + lax.rem(z, 2), y * 4 + (z // 2) * 2 + core


def step_of(k):
    d = lax.rem(k * STRIDE, CHIPS)
    steps = (d // (RING * RING), lax.rem(d // RING, RING), lax.rem(d, RING))
    far = [s // 2 - s // 3 for s in steps]
    both = far[0] + far[1] + far[2] > 0
    up = 1 - lax.rem(steps[0] + steps[1] + steps[2], 2)
    return d, steps, far, both, up


def legs(steps, far, up):
    ahead = [f * (3 - 2 * up) for f in far]
    return ahead, [s + 4 - a for s, a in zip(steps, ahead)]


def far_count():
    return sum(2 in (d // 16, d // 4 % 4, d % 4) for d in range(1, CHIPS))


def remote(src, dst, send, recv, device):
    return pltpu.make_async_remote_copy(
        src_ref=src, dst_ref=dst, send_sem=send, recv_sem=recv, device_id=device,
        device_id_type=MESH,
    )


class Ring:
    def __init__(self, at, go, source, target, relay, send_sem, recv_sem, origin=0):
        self.at, self.go, self.source, self.target = at, go, source, target
        self.relay, self.send_sem, self.recv_sem, self.origin = relay, send_sem, recv_sem, origin

    def copy(self, src, dst, i, way):
        return remote(src, dst, self.send_sem.at[i], self.recv_sem.at[i], self.go(1 if way == 0 else 3))

    def by(self, d):
        return lax.rem(self.at + d, RING)

    def begin(self):
        for way in range(2):
            self.copy(self.source(self.by(2), way), self.relay(way), 4 + way, way).start()
        for way, d in ((0, 1), (1, 3)):
            self.copy(self.source(self.by(d), None), self.target(self.at, None), way, way).start()

    def begin_sent(self):
        for way in range(2):
            self.copy(self.source(self.by(2), way), self.relay(way), 4 + way, way).wait_send()
        for way, d in ((0, 1), (1, 3)):
            self.copy(self.source(self.by(d), None), self.target(self.at, None), way, way).wait_send()

    def forward(self):
        for way, d in ((0, 3), (1, 1)):
            held = self.relay(way)
            self.copy(held, held, 4 + way, way).wait_recv()
            self.copy(held, self.target(self.by(d), way), 2 + way, way).start()

    def forward_sent(self):
        for way, d in ((0, 3), (1, 1)):
            self.copy(self.relay(way), self.target(self.by(d), way), 2 + way, way).wait_send()

    def arrived(self):
        for way, d in ((0, 3), (1, 1)):
            part = self.target(self.by(d), None)
            self.copy(part, part, way, way).wait_recv()
        for way in range(2):
            part = self.target(self.by(2), way)
            self.copy(part, part, 2 + way, way).wait_recv()


def exchange_kernel(
    n_col, packed, table, got, got_table, a_one, a_two, t_one, t_two, a_relay_one,
    a_relay_two, a_relay_three, t_relay_one, t_relay_two, t_relay_three, l_one, l_two, l_relay_one,
    l_relay_two, l_relay_three, a_stage_one, a_stage_two, a_stage_three, t_stage, t_last, send_sems,
    recv_sems, hand_sems, own_sems,
):
    x, y, z, core = position()
    here = (x, y, z)
    sibling = place_of(x, y, z, 1 - core)
    barrier = pltpu.get_barrier_semaphore()

    def greet(at):
        pl.semaphore_signal(barrier, 1, device_id=at, device_id_type=MESH)

    greet(sibling)
    for axis in range(3):
        for d in (1, 3):
            for side in range(2):
                greet(place_of(*[here[i] + (d if i == axis else 0) for i in range(3)], side))
    pl.semaphore_wait(barrier, 13)

    def along(axis, to_core):
        def go(d):
            return place_of(*[here[i] + (d if i == axis else 0) for i in range(3)], to_core)

        return here[axis], go

    def along_mine(phase):
        axes = [lax.rem(phase + core, 3) == i for i in range(3)]
        picked = [axes[i].astype(jnp.int32) for i in range(3)]
        at = sum(p * h for p, h in zip(picked, here))
        return at, lambda d: place_of(*[h + d * p for p, h in zip(picked, here)], core)

    whole = slice(None)
    depth = packed.shape[4] // 2

    def half(ref_at, width):
        return lambda i, h: ref_at(i, pl.ds(0, 2 * width) if h is None else pl.ds(h * width, width))

    def arrays(which):
        if which < 0:
            return (
                (table, got_table, l_one, l_two, l_relay_one, l_relay_two, l_relay_three),
                whole, 18, 14,
            )
        return (
            (packed, got, a_one, a_two, a_relay_one, a_relay_two, a_relay_three),
            pl.ds(which * depth, depth), 9 * which, 7 * which,
        )

    def first_ring(kind, which):
        (src, end, one, two, relay, relay_two, relay_three), rows, sent, received = arrays(which)
        at, go = along(kind, kind)
        return Ring(
            at, go, half(lambda j, s: src.at[kind, j, s, whole, rows], 2),
            half(lambda i, s: one.at[i * 2 + core, s, whole, rows], 2),
            lambda way: relay.at[way, core, whole, whole, rows],
            send_sems.at[sent + kind], recv_sems.at[received + core],
        )

    def first_mine(origin, which):
        (src, end, one, two, relay, relay_two, relay_three), rows, sent, received = arrays(which)
        at, go = along_mine(0)
        return Ring(
            at, go, None, half(lambda i, s: one.at[i * 2 + origin, s, whole, rows], 2),
            lambda way: relay.at[way, origin, whole, whole, rows], send_sems.at[sent + 2 + origin],
            recv_sems.at[received + origin],
        )

    def second_ring(which):
        (src, end, one, two, relay, relay_two, relay_three), rows, sent, received = arrays(which)
        return Ring(
            *along_mine(1), half(lambda j, s: one.at[s, j, whole, rows], 4),
            half(lambda i, s: two.at[i, s, whole, rows], 4),
            lambda way: relay_two.at[way, whole, whole, rows],
            send_sems.at[sent + 4], recv_sems.at[received + 2],
        )

    def third_ring(which):
        (src, end, one, two, relay, relay_two, relay_three), rows, sent, received = arrays(which)
        return Ring(
            *along_mine(2), half(lambda j, s: two.at[s, whole, j, rows], 2),
            half(lambda i, s: end.at[i, s, whole, rows], 2),
            lambda way: relay_three.at[way, whole, whole, rows],
            send_sems.at[sent + 5], recv_sems.at[received + 3],
        )

    def shared_first(which):
        rows, sent, received = arrays(which)[1:]
        return Ring(
            *along(2, core), half(lambda j, s: packed.at[2, j, s, whole, rows], 2),
            half(lambda i, s: t_one.at[i, s, whole, rows], 2),
            lambda way: t_relay_one.at[way, whole, whole, rows],
            send_sems.at[sent + 6], recv_sems.at[received + 4],
        )

    def shared_second(which):
        rows, sent, received = arrays(which)[1:]

        def part(i, h):
            begin = lax.rem(i, 2) * 4
            taken = pl.ds(begin, 4) if h is None else pl.ds(begin + 2 * h, 2)
            return t_two.at[i // 2, taken, whole, rows]

        return Ring(
            *along(0, core), half(lambda j, s: t_one.at[s, j, whole, rows], 2), part,
            lambda way: t_relay_two.at[way, whole, whole, rows],
            send_sems.at[sent + 7], recv_sems.at[received + 5],
        )

    def shared_got(side, rows):
        def part(i, h):
            begin = lax.rem(i, 2) * 2
            taken = pl.ds(begin, 2) if h is None else pl.ds(begin + h, 1)
            return got.at[4 + side * 2 + i // 2, taken, whole, rows]

        return part

    def shared_third(which):
        rows, sent, received = arrays(which)[1:]
        return Ring(
            *along(1, core), half(lambda j, s: t_two.at[s, whole, j, rows], 1),
            shared_got(core, rows), lambda way: t_relay_three.at[way, whole, whole, rows],
            send_sems.at[sent + 8], recv_sems.at[received + 6],
        )

    class Keep:
        def __init__(self, ring, stage, i, which):
            sem = own_sems.at[which, i]
            kept = stage.at[whole, whole, arrays(which)[1]]
            self.load = pltpu.make_async_copy(ring.source(ring.at, None), kept, sem)
            self.store = pltpu.make_async_copy(kept, ring.target(ring.at, None), sem)

        def run(self):
            self.load.wait()
            self.store.start()

    def keep_line(ring):
        return pltpu.make_async_copy(
            ring.source(ring.at, None), ring.target(ring.at, None), own_sems.at[0, 6]
        )

    def to_sibling(kind, which):
        ring = first_ring(kind, which)
        return remote(
            ring.source(ring.at, None), ring.target(ring.at, None), hand_sems.at[0, 9 + which],
            hand_sems.at[1, 9 + which], sibling,
        )

    def hand(side, d, which):
        part = shared_got(side, arrays(which)[1])(lax.rem(y + d, RING), None)
        i = which * RING + d
        return remote(part, part, hand_sems.at[0, i], hand_sems.at[1, i], sibling)

    def by_core(kind, mine, other):
        pl.when(core == kind)(mine)
        pl.when(core != kind)(other)

    for kind in range(2):
        first_ring(kind, -1).begin()
        by_core(kind, keep_line(first_ring(kind, -1)).start, to_sibling(kind, -1).start)
    for which in range(2):
        first_ring(0, which).begin()
        first_ring(1, which).begin()
        shared_first(which).begin()
        for kind in range(2):
            by_core(
                kind, Keep(first_ring(kind, which), a_stage_one, 0, which).load.start,
                to_sibling(kind, which).start,
            )
        Keep(shared_first(which), t_stage.at[0], 1, which).load.start()
    for which in range(2):
        for kind in range(2):
            pl.when(core == kind)(Keep(first_ring(kind, which), a_stage_one, 0, which).run)
        Keep(shared_first(which), t_stage.at[0], 1, which).run()
    for origin in range(2):
        first_mine(origin, -1).forward()

    def first_done(which):
        for origin in range(2):
            first_mine(origin, which).arrived()
        for kind in range(2):

            def mine():
                if which < 0:
                    keep_line(first_ring(kind, which)).wait()
                else:
                    Keep(first_ring(kind, which), a_stage_one, 0, which).store.wait()
                to_sibling(kind, which).wait_recv()

            by_core(kind, mine, to_sibling(kind, which).wait_send)

    for which in range(2):
        for origin in range(2):
            first_mine(origin, which).forward()
        shared_first(which).forward()
    first_done(-1)
    second_ring(-1).begin()
    keep_line(second_ring(-1)).start()
    for which in range(2):
        first_done(which)
        second_ring(which).begin()
        Keep(second_ring(which), a_stage_two, 2, which).load.start()
        shared_first(which).arrived()
        Keep(shared_first(which), t_stage.at[0], 1, which).store.wait()
        shared_second(which).begin()
        Keep(shared_second(which), t_stage.at[1], 3, which).load.start()
        Keep(second_ring(which), a_stage_two, 2, which).run()
        Keep(shared_second(which), t_stage.at[1], 3, which).run()
    second_ring(-1).forward()
    for which in range(2):
        second_ring(which).forward()
        shared_second(which).forward()
    second_ring(-1).arrived()
    keep_line(second_ring(-1)).wait()
    third_ring(-1).begin()
    keep_line(third_ring(-1)).start()
    for which in range(2):
        shared_second(which).arrived()
        Keep(shared_second(which), t_stage.at[1], 3, which).store.wait()
        shared_third(which).begin()
        Keep(shared_third(which), t_last, 5, which).load.start()
        second_ring(which).arrived()
        Keep(second_ring(which), a_stage_two, 2, which).store.wait()
        third_ring(which).begin()
        Keep(third_ring(which), a_stage_three, 4, which).load.start()
        Keep(shared_third(which), t_last, 5, which).run()
        Keep(third_ring(which), a_stage_three, 4, which).run()
    third_ring(-1).forward()
    for which in range(2):
        shared_third(which).forward()
        third_ring(which).forward()
        Keep(shared_third(which), t_last, 5, which).store.wait()
        hand(core, 0, which).start()
    for which in range(2):
        shared_third(which).arrived()
        for d in range(1, RING):
            hand(core, d, which).start()
    for which in range(2):
        third_ring(which).arrived()
        Keep(third_ring(which), a_stage_three, 4, which).store.wait()
    third_ring(-1).arrived()
    keep_line(third_ring(-1)).wait()
    for which in range(2):
        for d in range(RING):
            hand(1 - core, d, which).wait_recv()
    for which in range(-1, 2):
        first_ring(0, which).begin_sent()
        first_ring(1, which).begin_sent()
        for origin in range(2):
            first_mine(origin, which).forward_sent()
        rings = [second_ring(which), third_ring(which)]
        if which >= 0:
            rings += [shared_first(which), shared_second(which), shared_third(which)]
            for d in range(RING):
                hand(core, d, which).wait_send()
        for ring in rings:
            ring.begin_sent()
            ring.forward_sent()


def exchange(packed, table, n_col):
    block, line = packed.shape[4:], table.shape[4:]

    def held(*shape):
        return jax.ShapeDtypeStruct(shape + block, packed.dtype)

    def lines(*shape):
        return jax.ShapeDtypeStruct(shape + line, table.dtype)

    def stage(*shape):
        return pltpu.VMEM(shape + block, packed.dtype)

    out_shape = (
        held(12, 4, 8), lines(4, 4, 8),
        held(8, 4, 4), held(4, 8, 4), held(4, 4, 4), held(2, 8, 4),
        held(2, 2, 2, 4), held(2, 4, 4), held(2, 2, 8), held(2, 2, 4), held(2, 2, 4), held(2, 1, 8),
        lines(8, 4, 4), lines(4, 8, 4), lines(2, 2, 2, 4), lines(2, 4, 4), lines(2, 2, 8),
    )
    return pl.pallas_call(
        functools.partial(exchange_kernel, n_col),
        out_shape=out_shape,
        in_specs=[HBM, HBM],
        out_specs=(HBM,) * len(out_shape),
        scratch_shapes=[
            stage(4, 4), stage(8, 4), stage(4, 8), stage(2, 4, 4), stage(2, 8),
            DMA((24, 6)), DMA((18, 6)), DMA((2, 11)), DMA((2, 7)),
        ],
        compiler_params=pltpu.CompilerParams(
            collective_id=2, has_side_effects=True, vmem_limit_bytes=LIMIT
        ),
        name="exchange",
    )(packed, table)[:2]


def last_place(got, side, at):
    x, y, z = at
    return got.at[8 + side * 2 + x // 2, lax.rem(x, 2) * 2 + y // 2, lax.rem(y, 2) * 4 + z]


def gather_kernel(
    spare, got_in, got, one, two, three, relay_one, relay_two, relay_three, send_sems, recv_sems,
    own_sems, out_sem, swap_sems,
):
    x, y, z, core = position()
    here = (x, y, z)
    sibling = place_of(x, y, z, 1 - core)
    whole = slice(None)
    lanes = spare.shape[1] // 2
    barrier = pltpu.get_barrier_semaphore()

    def along(axis):
        def go(d):
            return place_of(*[here[i] + (d if i == axis else 0) for i in range(3)], core)

        return here[axis], go

    def greet(at):
        pl.semaphore_signal(barrier, 1, device_id=at, device_id_type=MESH)

    for axis in range(3):
        for d in (1, 3):
            greet(along(axis)[1](d))
    pl.when(core == 1)(lambda: greet(sibling))
    pl.when(core == 1)(lambda: pl.semaphore_wait(barrier, 6))
    pl.when(core == 0)(lambda: pl.semaphore_wait(barrier, 7))

    def cols(h):
        return pl.ds(0, 2 * lanes) if h is None else pl.ds(h * lanes, lanes)

    def ring(p, phase):
        rows = pl.ds(48 * p, 48 if p < 2 else 32)
        at, go = along((p + phase) % 3)
        if phase == 0:
            source = lambda j, h: spare.at[rows, cols(h)]
            target = lambda i, h: one.at[i, rows, cols(h)]
            relay = lambda way: relay_one.at[way, rows]
        elif phase == 1:
            source = lambda j, h: one.at[whole, rows, cols(h)]
            target = lambda i, h: (
                two.at[i, whole, rows, cols(h)] if p == 2 else two.at[whole, i, rows, cols(h)]
            )
            relay = lambda way: relay_two.at[way, whole, rows]
        else:
            source = lambda j, h: two.at[whole, whole, rows, cols(h)]
            target = lambda i, h: (
                three.at[whole, whole, i, rows, cols(h)] if p == 0
                else three.at[i, whole, whole, rows, cols(h)] if p == 1
                else three.at[whole, i, whole, rows, cols(h)]
            )
            relay = lambda way: relay_three.at[way, whole, whole, rows]
        k = 3 * phase + p
        return Ring(at, go, source, target, relay, send_sems.at[k], recv_sems.at[k])

    def own(p, phase):
        r = ring(p, phase)
        return pltpu.make_async_copy(
            r.source(r.at, None), r.target(r.at, None), own_sems.at[3 * phase + p]
        )

    for phase in range(3):
        for p in range(3):
            if phase > 0:
                ring(p, phase - 1).arrived()
                own(p, phase - 1).wait()
            ring(p, phase).begin()
            own(p, phase).start()
        for p in range(3):
            ring(p, phase).forward()
    for p in range(3):
        ring(p, 2).arrived()
        own(p, 2).wait()

    def pieces(side):
        for i in range(RING):
            for j in range(RING):
                dst = got.at[8 + side * 2 + i // 2, i % 2 * 2 + j // 2, pl.ds(j % 2 * 4, 4)]
                yield three.at[i, j], dst

    half = got.at[pl.ds(8, 2)]

    @pl.when(core == 0)
    def _():
        for src, dst in pieces(0):
            remote(src, dst, swap_sems.at[0], swap_sems.at[1], sibling).start()
        pltpu.make_async_copy(half, half, swap_sems.at[0]).wait()

    @pl.when(core == 1)
    def _():
        for src, dst in pieces(1):
            pltpu.make_async_copy(src, dst, out_sem).start()
        pltpu.make_async_copy(half, half, out_sem).wait()
        pltpu.make_async_copy(half, half, swap_sems.at[1]).wait()

    for phase in range(3):
        for p in range(3):
            ring(p, phase).begin_sent()
            ring(p, phase).forward_sent()


def gather_last(spare, got):
    depth, size = spare.shape

    def held(*shape):
        return pltpu.VMEM(shape + (depth, size), spare.dtype)

    def relays(*shape):
        return pltpu.VMEM((2,) + shape + (depth, size // 2), spare.dtype)

    return pl.pallas_call(
        gather_kernel,
        out_shape=jax.ShapeDtypeStruct(got.shape, got.dtype),
        in_specs=[HBM, HBM],
        out_specs=HBM,
        input_output_aliases={1: 0},
        scratch_shapes=[
            held(4), held(4, 4), held(4, 4, 4), relays(), relays(4), relays(4, 4),
            DMA((9, 6)), DMA((9, 6)), DMA((9,)), DMA, DMA((2,)),
        ],
        compiler_params=pltpu.CompilerParams(
            collective_id=4, has_side_effects=True, vmem_limit_bytes=LIMIT
        ),
        name="gather_last",
    )(spare, got)


def last_kernel(n_row, n_col, packed, got_in, got, relay, sems, relay_sem, own_sem):
    devices = n_row * n_col
    x, y, z, core = position()
    mine = place_of(x, y, z, core)
    me = mine[0] * n_col + mine[1]
    barrier = pltpu.get_barrier_semaphore()

    def at_step(steps, core):
        return place_of(x + steps[0], y + steps[1], z + steps[2], core)

    def number(device):
        return device[0] * n_col + device[1]

    def greet(at):
        pl.semaphore_signal(barrier, 1, device_id=at, device_id_type=MESH)

    def near(k, carry):
        d, steps, far, both, up = step_of(k)

        @pl.when(jnp.logical_and(core == 1, jnp.logical_not(both)))
        def _():
            greet(at_step(steps, 0))
            greet(at_step(steps, 1))

        return carry

    def relayed(k, carry):
        bits = (k // 8, lax.rem(k // 4, 2), lax.rem(k // 2, 2))
        way = lax.rem(k, 2)

        @pl.when(jnp.logical_and(core == 0, k != 15))
        def _():
            greet(at_step([b * (3 - 2 * way) for b in bits], 0))

        return carry

    lax.fori_loop(1, CHIPS, near, 0)
    lax.fori_loop(2, 16, relayed, 0)

    @pl.when(core == 1)
    def _():
        greet(place_of(x, y, z, 0))
        pl.semaphore_wait(barrier, 26)

    @pl.when(core == 0)
    def _():
        pl.semaphore_wait(barrier, 26 + 13 + 1)

    def block_for(target):
        chip = number(target) // 2
        return packed.at[3, chip // 16, lax.rem(chip // 4, 4), lax.rem(chip, 4)]

    def landing(steps, side):
        return last_place(got, side, [lax.rem(h + s, RING) for h, s in zip((x, y, z), steps)])

    def first_leg(k, carry):
        d, steps, far, both, up = step_of(k)

        @pl.when(both)
        def _():
            first, second = legs(steps, far, up)
            remote(
                block_for(at_step(steps, 1)), relay.at[d], sems.at[0], relay_sem.at[d],
                at_step(first, core),
            ).start()

        return carry

    def direct(k, carry):
        d, steps, far, both, up = step_of(k)

        @pl.when(jnp.logical_not(both))
        def _():
            target = at_step(steps, 1)
            remote(block_for(target), landing((0, 0, 0), core), sems.at[0], sems.at[1], target).start()

        return carry

    def second_leg(k, carry):
        d, steps, far, both, up = step_of(k)

        @pl.when(both)
        def _():
            first, second = legs(steps, far, up)
            target = at_step(second, 1)
            held = relay.at[d]
            remote(held, held, sems.at[2], relay_sem.at[d], target).wait_recv()
            remote(held, landing([4 - f for f in first], core), sems.at[2], sems.at[1], target).start()

        return carry

    lax.fori_loop(1, CHIPS, first_leg, 0)
    lax.fori_loop(1, CHIPS, direct, 0)
    lax.fori_loop(1, CHIPS, second_leg, 0)

    def settle(ref, count, sem):
        part = ref.at[pl.ds(0, count)]
        pltpu.make_async_copy(part, part, sem).wait()

    settle(relay, far_count(), sems.at[2])

    @pl.when(core == 0)
    def _():
        to = place_of(x, y, z, 1)
        remote(block_for(to), landing((0, 0, 0), core), sems.at[0], sems.at[1], to).start()
        settle(relay, CHIPS, sems.at[0])

    @pl.when(core == 1)
    def _():
        own = pltpu.make_async_copy(block_for(mine), landing((0, 0, 0), core), own_sem)
        own.start()
        own.wait()
        settle(relay, CHIPS - 1, sems.at[0])
        settle(relay, devices - 1, sems.at[1])


def exchange_last(packed, got, n_row, n_col):
    return pl.pallas_call(
        functools.partial(last_kernel, n_row, n_col),
        out_shape=(
            jax.ShapeDtypeStruct(got.shape, got.dtype),
            jax.ShapeDtypeStruct((2 * CHIPS,) + packed.shape[4:], packed.dtype),
        ),
        in_specs=[HBM, HBM],
        out_specs=(HBM, HBM),
        input_output_aliases={1: 0},
        scratch_shapes=[DMA((3,)), DMA((CHIPS,)), DMA],
        compiler_params=pltpu.CompilerParams(collective_id=3, has_side_effects=True),
        name="exchange_last",
    )(packed, got)[0]


def fetch_target(t, at, total, counts, order, base, got, buffer, sem):
    base[t] = at

    def one(e, c):
        pltpu.make_async_copy(got.at[order[t, e]], buffer.at[at + e], sem).start()
        return c

    lax.fori_loop(0, counts[t, 0], one, 0)
    return at + counts[t, 0]


def await_target(t, counts, got, buffer, sem):
    def one(e, c):
        pltpu.make_async_copy(got.at[0], buffer.at[0], sem).wait()
        return c

    lax.fori_loop(0, counts[t, 0], one, 0)


def product(t, e, counts, base, buffer):
    rank = buffer.shape[1] // 2
    n, begin = counts[t, 0], base[t]
    picked = [
        jnp.where(e * STACK + k < n, begin + e * STACK + k, buffer.shape[0] - 1) for k in range(STACK)
    ]
    lefts = jnp.concatenate([buffer[s, 0:rank, :] for s in picked], axis=0)
    rights = jnp.concatenate([buffer[s, rank:, :] for s in picked], axis=0)
    return dot(lefts, rights, ((0,), (0,)))


def add_rest(t, counts, base, buffer, sum_ref, rows, cols):
    def chunk(e, c):
        sum_ref[rows, cols] += product(t, e, counts, base, buffer)
        return c

    lax.fori_loop(1, (counts[t, 0] + STACK - 1) // STACK, chunk, 0)


def split(x):
    high = x.astype(jnp.bfloat16)
    return high, (x - high.astype(jnp.float32)).astype(jnp.bfloat16)


def dot3(a, b):
    a_high, a_low = split(a)
    b_high, b_low = split(b)
    return dot(a_high, b_high) + (dot(a_high, b_low) + dot(a_low, b_high))


def permutation(pivots):
    size = pivots.shape[1]
    places = lax.broadcasted_iota(jnp.int32, (size, size), 0)
    return (places == pivots).astype(jnp.float32)


def panel_kernel(
    total, table, got, front, pivots, upper_inverse, lower_inverse, column_basis, row_basis,
    column_ranks, row_ranks, a_out, b_out, counts, order, left_sum, top_sum, buffer, top_weights,
    left_weights, coupling, order_rows, count_rows, base, sem, front_sem, sort_sem,
):
    size, rank = upper_inverse.shape[0], column_basis.shape[0]
    row_blocks, col_blocks = front.shape[0] // size, front.shape[1] // size
    targets = row_blocks * col_blocks
    devices = total // CAP
    is_top, is_left = lax.axis_index("row") == 0, lax.axis_index("col") == 0
    load_left = pltpu.make_async_copy(front.at[:, pl.ds(0, size)], left_sum, front_sem.at[0])
    load_top = pltpu.make_async_copy(front.at[pl.ds(0, size)], top_sum, front_sem.at[1])
    pl.when(is_left)(load_left.start)
    pl.when(is_top)(load_top.start)

    core = lax.rem(lax.axis_index("col"), 2)
    k = lax.broadcasted_iota(jnp.int32, (1, devices), 1)
    high, middle, low, side = k >> 5, (k >> 3) & 3, (k >> 1) & 3, k & 1
    x, y, z = (jnp.where(core == 0, a, b) for a, b in ((low, high), (middle, low), (high, middle)))
    shared = devices + side * CHIPS + y * 16 + x * 4 + z
    last = 2 * devices + side * CHIPS + x * 16 + y * 4 + z
    block = jnp.concatenate([k, shared, last], axis=1)
    target = jnp.concatenate([table[p : p + 1, :] for p in range(3)], axis=1)
    entries = block.shape[1]
    member = lax.broadcasted_iota(jnp.int32, (targets, entries), 0) == target
    member_one = member.astype(jnp.float32)
    before = (
        lax.broadcasted_iota(jnp.int32, (entries, entries), 0)
        < lax.broadcasted_iota(jnp.int32, (entries, entries), 1)
    ).astype(jnp.bfloat16)
    earlier = dot(member_one.astype(jnp.bfloat16), before)
    rank_of = jnp.sum(jnp.where(member, earlier, 0.0), axis=0, keepdims=True)
    chosen = lax.broadcasted_iota(jnp.int32, (total, entries), 0) == rank_of.astype(jnp.int32)
    upper_part = jnp.where(member, (block >> 7).astype(jnp.float32), 0.0).astype(jnp.bfloat16)
    lower_part = jnp.where(member, (block & 127).astype(jnp.float32), 0.0).astype(jnp.bfloat16)
    chosen = chosen.astype(jnp.float32).astype(jnp.bfloat16)
    listed = dot(upper_part, chosen, ((1,), (1,))) * 128.0 + dot(lower_part, chosen, ((1,), (1,)))
    order_rows[...] = listed.astype(jnp.int32)
    tally = jnp.sum(member_one, axis=1, keepdims=True).astype(jnp.int32)
    count_rows[...] = jnp.broadcast_to(tally, count_rows.shape)
    copies = (
        pltpu.make_async_copy(order_rows, order, sort_sem.at[0]),
        pltpu.make_async_copy(count_rows, counts, sort_sem.at[1]),
    )
    for copy in copies:
        copy.start()
    for copy in copies:
        copy.wait()

    @pl.when(jnp.logical_or(is_top, is_left))
    def _():
        buffer[buffer.shape[0] - 1] = jnp.zeros(buffer.shape[1:], buffer.dtype)

        def fetch(t, at):
            return fetch_target(t, at, total, counts, order, base, got, buffer, sem)

        def fetch_left(i, at):
            return fetch(i * col_blocks, at)

        at = lax.fori_loop(0, jnp.where(is_left, row_blocks, 0), fetch_left, 0)
        lax.fori_loop(jnp.where(is_left, 1, 0), jnp.where(is_top, col_blocks, 0), fetch, at)

    @pl.when(is_top)
    def _():
        weights = dot(row_basis[...], lower_inverse[...], precision=HIGHEST)
        weights = dot(weights, permutation(pivots[...]), ((1,), (1,)), precision=HIGHEST)
        top_weights[0:rank] = weights
        top_weights[rank:] = weights

    @pl.when(is_left)
    def _():
        left_weights[...] = dot(
            upper_inverse[...], column_basis[...], ((1,), (1,)), precision=HIGHEST
        )
        coupled = dot(column_basis[...], row_basis[...], ((1,), (1,)), precision=HIGHEST)
        coupling[...] = jnp.concatenate([coupled, coupled], axis=1)

    @pl.when(jnp.logical_or(is_top, is_left))
    def _():
        def ready(t):
            await_target(t, counts, got, buffer, sem)

        def ready_left(i, c):
            ready(i * col_blocks)
            return c

        def ready_top(t, c):
            ready(t)
            return c

        lax.fori_loop(0, jnp.where(is_left, row_blocks, 0), ready_left, 0)
        lax.fori_loop(jnp.where(is_left, 1, 0), jnp.where(is_top, col_blocks, 0), ready_top, 0)

    @pl.when(is_top)
    def _():
        row = lax.broadcasted_iota(jnp.int32, (2 * rank, size), 0)
        load_top.wait()
        for j in range(col_blocks):
            cols = slice(j * size, (j + 1) * size)
            top_sum[:, cols] += product(j, 0, counts, base, buffer)
        for j in range(col_blocks):
            add_rest(j, counts, base, buffer, top_sum, slice(0, size), slice(j * size, (j + 1) * size))
        for j in range(col_blocks):
            cols = slice(j * size, (j + 1) * size)
            factor = dot3(top_weights[...], top_sum[:, cols])
            factor = jnp.where(lax.rem(row, rank) < row_ranks[j], factor, 0.0)
            high, low = split(factor)
            value = jnp.where(row < rank, high.astype(jnp.float32), low.astype(jnp.float32))
            for h in range(size // 128):
                b_out[j * (size // 128) + h] = value[:, h * 128 : (h + 1) * 128].astype(jnp.bfloat16)

    @pl.when(is_left)
    def _():
        lane = lax.broadcasted_iota(jnp.int32, (size, 2 * rank), 1)
        load_left.wait()

        def add(i, c):
            rows = pl.ds(pl.multiple_of(i * size, size), size)
            left_sum[rows, :] += product(i * col_blocks, 0, counts, base, buffer)
            return c

        lax.fori_loop(0, row_blocks, add, 0, unroll=4)

        def add_more(i, c):
            rows = pl.ds(pl.multiple_of(i * size, size), size)
            add_rest(i * col_blocks, counts, base, buffer, left_sum, rows, slice(0, size))
            return c

        lax.fori_loop(0, row_blocks, add_more, 0)

        def block(i, c):
            rows = pl.ds(pl.multiple_of(i * size, size), size)
            factor = dot3(left_sum[rows, :], left_weights[...])
            factor = jnp.where(lane[:, 0:rank] < column_ranks[i], factor, 0.0)
            high, low = split(dot3(factor, coupling[...]))
            value = jnp.where(lane < rank, high.astype(jnp.float32), low.astype(jnp.float32))
            for h in range(size // 128):
                a_out[i * (size // 128) + h] = value[h * 128 : (h + 1) * 128].astype(jnp.bfloat16)
            return c

        lax.fori_loop(0, row_blocks, block, 0, unroll=4)


def panel(
    table, got, front, pivots, upper_inverse, lower_inverse, column_basis, row_basis, column_ranks,
    row_ranks,
):
    depth, size = got.shape[1:]
    total = table.shape[1] * CAP
    rows, cols = front.shape
    targets = (rows // size) * (cols // size)
    return pl.pallas_call(
        functools.partial(panel_kernel, total),
        out_shape=(
            jax.ShapeDtypeStruct((rows // 128, 128, 128), jnp.bfloat16),
            jax.ShapeDtypeStruct((cols // 128, 128, 128), jnp.bfloat16),
            jax.ShapeDtypeStruct((targets, 128), jnp.int32),
            jax.ShapeDtypeStruct((targets, total), jnp.int32),
        ),
        in_specs=[VMEM, HBM, HBM, VMEM, VMEM, VMEM, VMEM, VMEM, SMEM, SMEM],
        out_specs=(VMEM, VMEM, SMEM, SMEM),
        scratch_shapes=[
            pltpu.VMEM((rows, size), jnp.float32),
            pltpu.VMEM((size, cols), jnp.float32),
            pltpu.VMEM((total + 1, depth, size), jnp.bfloat16),
            pltpu.VMEM((depth, size), jnp.float32),
            pltpu.VMEM((size, depth // 2), jnp.float32),
            pltpu.VMEM((depth // 2, depth), jnp.float32),
            pltpu.VMEM((targets, total), jnp.int32),
            pltpu.VMEM((targets, 128), jnp.int32),
            pltpu.SMEM((targets,), jnp.int32),
            DMA,
            DMA((2,)),
            DMA((2,)),
        ],
        compiler_params=pltpu.CompilerParams(vmem_limit_bytes=LIMIT),
        name="panel",
    )(
        table, got, front, pivots, upper_inverse, lower_inverse, column_basis, row_basis,
        column_ranks, row_ranks,
    )


def spread_kernel(
    n_row, n_col, a_src, b_src, a_all, b_all, a_part_send, a_part_recv, b_part_send, b_part_recv,
    a_send, a_recv, b_send, b_recv, swap_sem, own_sem,
):
    r, c = lax.axis_index("row"), lax.axis_index("col")
    half = n_col // 2
    chip, core = c // 2, lax.rem(c, 2)
    sibling = (r, chip * 2 + 1 - core)
    barrier = pltpu.get_barrier_semaphore()

    def mates(n, me, body):
        for k in range(1, n):
            body(lax.rem(me + k, n))

    mates(n_col, c, lambda o: pl.semaphore_signal(barrier, 1, device_id=(r, o), device_id_type=MESH))
    mates(n_row, r, lambda o: pl.semaphore_signal(barrier, 1, device_id=(o, c), device_id_type=MESH))
    pl.semaphore_wait(barrier, n_col + n_row - 2)

    def piece(o):
        return lax.rem(o, 2) * half + o // 2

    def a_part(o):
        return remote(a_src.at[piece(o)], a_all.at[piece(o)], a_part_send.at[o], a_part_recv, (r, o))

    def b_part(o):
        return remote(b_src.at[o], b_all.at[o], b_part_send.at[o], b_part_recv, (o, c))

    def a_full(h):
        at = piece(c)
        return remote(a_all.at[at], a_all.at[at], a_send.at[h], a_recv.at[chip], (r, h * 2 + core))

    def a_from(h):
        at = core * half + h
        return remote(a_all.at[at], a_all.at[at], a_send.at[h], a_recv.at[h], (r, h * 2 + core))

    def b_full(o):
        return remote(b_all.at[r], b_all.at[r], b_send.at[o], b_recv.at[r], (o, c))

    def b_from(o):
        return remote(b_all.at[o], b_all.at[o], b_send.at[o], b_recv.at[o], (o, c))

    def swap(side):
        part = a_all.at[pl.ds(side * half, half)]
        return remote(part, part, swap_sem.at[0], swap_sem.at[1], sibling)

    own_a = pltpu.make_async_copy(a_src.at[0], a_all.at[0], own_sem.at[0])
    own_b = pltpu.make_async_copy(b_src.at[0], b_all.at[0], own_sem.at[1])

    @pl.when(c == 0)
    def _():
        own_a.start()
        mates(n_col, c, lambda o: a_part(o).start())

    @pl.when(r == 0)
    def _():
        own_b.start()
        mates(n_row, r, lambda o: b_part(o).start())

    pl.when(c == 0)(own_a.wait)
    pl.when(c != 0)(lambda: a_part(c).wait_recv())
    mates(half, chip, lambda h: a_full(h).start())
    pl.when(r == 0)(own_b.wait)
    pl.when(r != 0)(lambda: b_part(r).wait_recv())
    mates(n_row, r, lambda o: b_full(o).start())
    mates(half, chip, lambda h: a_from(h).wait_recv())
    swap(core).start()
    mates(n_row, r, lambda o: b_from(o).wait_recv())
    swap(1 - core).wait_recv()
    mates(half, chip, lambda h: a_full(h).wait_send())
    mates(n_row, r, lambda o: b_full(o).wait_send())
    swap(core).wait_send()

    @pl.when(c == 0)
    def _():
        mates(n_col, c, lambda o: a_part(o).wait_send())

    @pl.when(r == 0)
    def _():
        mates(n_row, r, lambda o: b_part(o).wait_send())


def spread(a_src, b_src, n_row, n_col):
    return pl.pallas_call(
        functools.partial(spread_kernel, n_row, n_col),
        out_shape=(
            jax.ShapeDtypeStruct(a_src.shape, a_src.dtype),
            jax.ShapeDtypeStruct(b_src.shape, b_src.dtype),
        ),
        in_specs=[VMEM, VMEM],
        out_specs=(VMEM, VMEM),
        scratch_shapes=[
            DMA((n_col,)), DMA, DMA((n_row,)), DMA,
            DMA((n_col // 2,)), DMA((n_col // 2,)), DMA((n_row,)), DMA((n_row,)), DMA((2,)), DMA((2,)),
        ],
        compiler_params=pltpu.CompilerParams(collective_id=1, has_side_effects=True),
        name="spread",
    )(a_src, b_src)


def finish_kernel(
    total, counts, order, got, front, a_all, b_all, pivots, upper_inverse, lower_inverse, out,
    extended, buffer, b_cat, inverse_parts, corner, base, sem, front_sem, out_sem,
):
    size = upper_inverse.shape[0]
    row_blocks, col_blocks = front.shape[0] // size, front.shape[1] // size
    lanes = a_all.shape[2]
    rank = lanes // 2
    pieces = size // lanes
    is_top, is_left = lax.axis_index("row") == 0, lax.axis_index("col") == 0

    def rows(i):
        return pl.ds(pl.multiple_of(i * size, size), size)

    def load(i):
        return pltpu.make_async_copy(front.at[rows(i)], extended.at[rows(i)], front_sem.at[i])

    def store(i):
        return pltpu.make_async_copy(extended.at[rows(i)], out.at[rows(i)], out_sem.at[i])

    load(0).start()

    def fetch(i, at):
        for j in range(col_blocks):
            at = fetch_target(
                i * col_blocks + j, at, total, counts, order, base, got, buffer, sem.at[i]
            )
        pl.when(i + 1 < row_blocks)(lambda: load(i + 1).start())
        return at

    lax.fori_loop(0, row_blocks, fetch, 0)
    buffer[buffer.shape[0] - 1] = jnp.zeros(buffer.shape[1:], buffer.dtype)

    @pl.when(is_left)
    def _():
        high, low = split(upper_inverse[...])
        inverse_parts[0:size] = high
        inverse_parts[size : 2 * size] = low
        inverse_parts[2 * size :] = high

    for k in range(b_all.shape[0]):
        cols = slice(k * lanes, (k + 1) * lanes)
        high, low = b_all[k, 0:rank, :], b_all[k, rank:, :]
        if k < pieces:
            high = jnp.where(is_left, jnp.zeros_like(high), high)
            low = jnp.where(is_left, jnp.zeros_like(low), low)
        for h in range(2):
            b_cat[h * rank : (h + 1) * rank, cols] = high
            b_cat[(2 + h) * rank : (3 + h) * rank, cols] = low

    def step(i, c):
        load(i).wait()
        for j in range(col_blocks):
            await_target(i * col_blocks + j, counts, got, buffer, sem.at[i])
        a = jnp.concatenate([a_all[i * pieces + k] for k in range(pieces)], axis=0)
        a = jnp.concatenate([a, a], axis=1)
        a = jnp.where(jnp.logical_and(is_top, i == 0), jnp.zeros_like(a), a)
        for j in range(col_blocks):
            cols = slice(j * size, (j + 1) * size)
            added = product(i * col_blocks + j, 0, counts, base, buffer)
            extended[rows(i), cols] += added - dot(a, b_cat[:, cols])
        for j in range(col_blocks):
            cols = slice(j * size, (j + 1) * size)
            add_rest(i * col_blocks + j, counts, base, buffer, extended, rows(i), cols)

        @pl.when(jnp.logical_and(is_left, jnp.logical_not(jnp.logical_and(is_top, i == 0))))
        def _():
            high, low = split(extended[rows(i), 0:size])
            extended[rows(i), 0:size] = dot(
                jnp.concatenate([high, high, low], axis=1), inverse_parts[...]
            )

        @pl.when(jnp.logical_and(is_top, i == 0))
        def _():
            permute = permutation(pivots[...])
            corner[...] = dot(permute, extended[0:size, 0:size], ((0,), (0,)), precision=HIGHEST)
            weights = dot(lower_inverse[...], permute, ((1,), (1,)), precision=HIGHEST)
            for j in range(col_blocks):
                cols = slice(j * size, (j + 1) * size)
                upper = dot(weights, extended[0:size, cols], precision=HIGHEST)
                if j == 0:
                    upper = jnp.where(is_left, corner[...], upper)
                extended[0:size, cols] = upper

        store(i).start()
        return c

    lax.fori_loop(0, row_blocks, step, 0)
    for i in range(row_blocks):
        store(i).wait()


def finish(counts, order, got, front, a_all, b_all, pivots, upper_inverse, lower_inverse, total):
    depth, size = got.shape[1:]
    rows, cols = front.shape
    row_blocks = rows // size
    targets = row_blocks * (cols // size)
    return pl.pallas_call(
        functools.partial(finish_kernel, total),
        out_shape=jax.ShapeDtypeStruct(front.shape, jnp.float32),
        in_specs=[SMEM, SMEM, HBM, HBM, VMEM, VMEM, VMEM, VMEM, VMEM],
        out_specs=HBM,
        scratch_shapes=[
            pltpu.VMEM(front.shape, jnp.float32),
            pltpu.VMEM((total + 1, depth, size), jnp.bfloat16),
            pltpu.VMEM((2 * depth, cols), jnp.bfloat16),
            pltpu.VMEM((3 * size, size), jnp.bfloat16),
            pltpu.VMEM((size, size), jnp.float32),
            pltpu.SMEM((targets,), jnp.int32),
            DMA((row_blocks,)), DMA((row_blocks,)), DMA((row_blocks,)),
        ],
        compiler_params=pltpu.CompilerParams(vmem_limit_bytes=LIMIT),
        name="finish",
    )(counts, order, got, front, a_all, b_all, pivots, upper_inverse, lower_inverse)


def shards(
    front, child_left, child_right, child_owner, child_slot, pivots, upper_inverse, lower_inverse,
    column_basis, row_basis, column_ranks, row_ranks,
):
    n_row, n_col = lax.axis_size("row"), lax.axis_size("col")
    devices = n_row * n_col
    packed, table, spare = pack(
        child_owner[:, 0], child_slot, jnp.swapaxes(child_left, 1, 2), child_right, devices
    )
    packed = packed.reshape((4, RING, RING, RING) + packed.shape[1:])
    table = table.reshape((2, RING, RING, RING) + table.shape[1:])
    got, got_table = exchange(packed, table, n_col)
    got_table = got_table.reshape((devices,) + got_table.shape[3:])
    lines = got_table[:, 0, 0:8].T
    most = jnp.max(lines, axis=1)
    once, often = (most[3] == 1).astype(jnp.int32), (most[3] > 1).astype(jnp.int32)
    got = lax.fori_loop(0, once, lambda i, g: gather_last(spare, g), got)
    got = lax.fori_loop(0, often, lambda i, g: exchange_last(packed, g, n_row, n_col), got)
    got = got.reshape((3 * devices,) + got.shape[3:])
    a_src, b_src, counts, order = panel(
        lines, got, front, pivots[None, :], upper_inverse, lower_inverse, column_basis.T,
        row_basis.T, column_ranks, row_ranks,
    )
    a_all, b_all = spread(a_src, b_src, n_row, n_col)
    return finish(
        counts, order, got, front, a_all, b_all, pivots[None, :], upper_inverse, lower_inverse,
        devices * CAP,
    )


def solution(mesh):
    in_specs = (
        P("row", "col"),
        P(("row", "col"), None, None),
        P(("row", "col"), None, None),
        P(("row", "col"), None),
        P(("row", "col")),
        P(),
        P(),
        P(),
        P(),
        P(),
        P("row"),
        P("col"),
    )
    out_specs = P("row", "col")
    return jax.shard_map(shards, mesh=mesh, in_specs=in_specs, out_specs=out_specs, check_vma=False)
```
